32 devices in a mesh: batch: 8 (over z, y), seq: 2 (over x), tensor: 2 (over core).
Axes of the slice: x: 2, y: 2, z: 4, core: 2. Of those that a mesh axis runs over, the one named last changes fastest.
Arguments:
- hidden_in: bfloat16 [8, 2, 128, 2048], P('batch', None, 'seq', 'tensor'), may hold values from -6 to 6
- summary_counts: int32 [8], P('batch'), may hold values from 20 to 50, as said below
- summary_embed: bfloat16 [50, 2048], P(None, 'tensor'), may hold values from -6 to 6
- ln1_gain: bfloat16 [2048], P('tensor'), may hold values from 0.5 to 1.5
- ln1_bias: bfloat16 [2048], P('tensor'), may hold values from -1.75 to 1.75
- w_query: bfloat16 [2048, 2048], P(None, 'tensor'), may hold values from -0.125 to 0.125
- b_query: bfloat16 [2048], P('tensor'), may hold values from -3 to 3
- w_key: bfloat16 [2048, 2048], P(None, 'tensor'), may hold values from -0.125 to 0.125
- w_value: bfloat16 [2048, 2048], P(None, 'tensor'), may hold values from -0.125 to 0.125
- b_value: bfloat16 [2048], P('tensor'), may hold values from -3 to 3
- w_out: bfloat16 [2048, 2048], P('tensor'), may hold values from -1 to 1
- b_out: bfloat16 [2048], P('tensor'), may hold values from -1.75 to 1.75
- ln2_gain: bfloat16 [2048], P('tensor'), may hold values from 0.5 to 1.5
- ln2_bias: bfloat16 [2048], P('tensor'), may hold values from -1.75 to 1.75
- w_up: bfloat16 [2048, 8192], P(None, 'tensor'), may hold values from -0.125 to 0.125
- b_up: bfloat16 [8192], P('tensor'), may hold values from -3 to 3
- w_down: bfloat16 [8192, 2048], P('tensor'), may hold values from -0.0625 to 0.0625
- b_down: bfloat16 [2048], P('tensor'), may hold values from -1.75 to 1.75
- d_hidden: bfloat16 [8, 2, 128, 2048], P('batch', None, 'seq', 'tensor'), may hold values from -6 to 6
- d_summary: bfloat16 [8, 2, 50, 2048], P('batch', None, None, 'tensor'), may hold values from -6 to 6
Outputs:
- hidden_out: bfloat16 [8, 2, 128, 2048], P('batch', None, 'seq', 'tensor')
- summary_out: bfloat16 [8, 2, 50, 2048], P('batch', None, None, 'tensor')
- grad_input: float32 [8, 2, 128, 2048], P('batch', None, 'seq', 'tensor')
- grad_embed: float32 [50, 2048], P(None, 'tensor')
- grad_ln1_gain: float32 [2048], P('tensor')
- grad_ln1_bias: float32 [2048], P('tensor')
- grad_query: float32 [2048, 2048], P(('batch', 'seq'), 'tensor')
- grad_query_bias: float32 [2048], P('tensor')
- grad_key: float32 [2048, 2048], P(('batch', 'seq'), 'tensor')
- grad_value: float32 [2048, 2048], P(('batch', 'seq'), 'tensor')
- grad_value_bias: float32 [2048], P('tensor')
- grad_out: float32 [2048, 2048], P('tensor', ('batch', 'seq'))
- grad_out_bias: float32 [2048], P('tensor')
- grad_ln2_gain: float32 [2048], P('tensor')
- grad_ln2_bias: float32 [2048], P('tensor')
- grad_up: float32 [2048, 8192], P(('batch', 'seq'), 'tensor')
- grad_up_bias: float32 [8192], P('tensor')
- grad_down: float32 [8192, 2048], P('tensor', ('batch', 'seq'))
- grad_down_bias: float32 [2048], P('tensor')
The draws below stay inside these ranges and needn't reach their ends.
Inputs may be any that keep to these rules, and one draw needn't show every extreme that they name: Each item uses its first summary_counts[b] of the 50 slots; some item uses all 50 and some item uses 2 * 10.
All inputs are finite; a program needn't handle non-finite values.
Results may differ from the reference program's by a relative error of at most 0.015.
Values may be sent and summed in bfloat16 or wider, within the bound.
A program may use at most 320 MiB of HBM per device.

```python
import jax
import jax.numpy as jnp
from jax import lax

D = 2048
HD = 64
FF = 8192
SUMM = 50
SEGS = 2
ITEMS = 8
SEG_LEN = 128


def draw_summary_counts(key, part):
    key = jax.random.fold_in(key, 11)
    lowest = SUMM * 2 // 5
    values = jax.random.randint(jax.random.fold_in(key, 1), (ITEMS,), lowest, SUMM + 1)
    order = jax.random.permutation(jax.random.fold_in(key, 2), ITEMS)
    values = jnp.where(order == 0, SUMM, values)
    values = jnp.where(order == 1, lowest, values)
    return values.astype(jnp.int32)


def levels(stream_key, shape, split, low, high):
    factor_of = 1.0
    for axis_at, shards_of in split:
        steps = jax.random.uniform(jax.random.fold_in(jax.random.fold_in(stream_key, 6), axis_at), (shards_of,), jnp.float32, low / len(split), high / len(split))
        factor_of = factor_of * jnp.repeat(jnp.exp(steps), shape[axis_at] // shards_of).reshape((-1,) + (1,) * (len(shape) - 1 - axis_at))
    return factor_of


def bell_draw(key, dims, scale, most, shards=(), kind=jnp.bfloat16):
    values = jax.random.normal(key, dims, jnp.float32) * scale
    if len(shards) > 0:
        values = levels(key, dims, shards, -0.22, 0.18) * values
    return jnp.clip(values, min=-most, max=most).astype(kind)


def setup_inputs(seed: int = 0) -> dict:
    splits = jax.random.split(jax.random.key(seed), 21)
    return {
        "hidden_in": bell_draw(splits[0], (ITEMS, SEGS, SEG_LEN, D), 1.0, 6.0, ((0, 8), (2, 2), (3, 2))),
        "summary_counts": draw_summary_counts(jax.random.fold_in(splits[20], 71), 0),
        "summary_embed": bell_draw(splits[2], (SUMM, D), 1.0, 6.0, ((1, 2),)),
        "ln1_gain": jnp.clip(1.0 + 0.1 * jax.random.normal(splits[3], (D,), jnp.float32), 0.5, 1.5).astype(jnp.bfloat16),
        "ln1_bias": bell_draw(splits[4], (D,), 0.3, 1.75, ((0, 2),)),
        "w_query": bell_draw(splits[5], (D, D), D ** -0.5, 0.125, ((1, 2),)),
        "b_query": bell_draw(splits[6], (D,), 0.5, 3.0, ((0, 2),)),
        "w_key": bell_draw(splits[7], (D, D), D ** -0.5, 0.125, ((1, 2),)),
        "w_value": bell_draw(splits[8], (D, D), D ** -0.5, 0.125, ((1, 2),)),
        "b_value": bell_draw(splits[9], (D,), 0.5, 3.0, ((0, 2),)),
        "w_out": bell_draw(splits[10], (D, D), (max(D // 64, 1)) ** -0.5, 1.0, ((0, 2),)),
        "b_out": bell_draw(splits[11], (D,), 0.3, 1.75, ((0, 2),)),
        "ln2_gain": jnp.clip(1.0 + 0.1 * jax.random.normal(splits[12], (D,), jnp.float32), 0.5, 1.5).astype(jnp.bfloat16),
        "ln2_bias": bell_draw(splits[13], (D,), 0.3, 1.75, ((0, 2),)),
        "w_up": bell_draw(splits[14], (D, FF), D ** -0.5, 0.125, ((1, 2),)),
        "b_up": bell_draw(splits[15], (FF,), 0.5, 3.0, ((0, 2),)),
        "w_down": bell_draw(splits[16], (FF, D), FF ** -0.5, 0.0625, ((0, 2),)),
        "b_down": bell_draw(splits[17], (D,), 0.3, 1.75, ((0, 2),)),
        "d_hidden": bell_draw(splits[18], (ITEMS, SEGS, SEG_LEN, D), 1.0, 6.0, ((0, 8), (2, 2), (3, 2))),
        "d_summary": bell_draw(splits[19], (ITEMS, SEGS, SUMM, D), 1.0, 6.0, ((0, 8), (3, 2))),
    }


EPSILON = 1e-05
NEGATIVE = -1e+30

@jax.custom_vjp
def low(v):
    return lax.optimization_barrier(v.astype(jnp.bfloat16)).astype(jnp.float32)

@jax.custom_vjp
def low_back(v):
    return v

def low_keep(v):
    return (low(v), None)

def low_pass(kept, grad):
    return (grad,)

def back_keep(v):
    return (v, None)

def back_low(kept, grad):
    return (low(grad),)
low.defvjp(low_keep, low_pass)
low_back.defvjp(back_keep, back_low)

def matmul(first, second):
    return jnp.dot(first, second, precision=lax.Precision.HIGHEST, preferred_element_type=jnp.float32)

def layer_norm(resid, gain_vec, shift_vec):
    row_mean = lax.optimization_barrier(jnp.mean(resid, axis=-1, keepdims=True))
    variance = lax.optimization_barrier(jnp.mean(resid * resid, axis=-1, keepdims=True)) - row_mean * row_mean
    return (resid - row_mean) * lax.rsqrt(variance + EPSILON) * gain_vec + shift_vec

def by_heads(block):
    return block.reshape(block.shape[0], -1, HD).transpose(1, 0, 2)

def attention(queries, key_block, value_block, allowed):
    row_count = queries.shape[0]
    score_scale = HD ** (-0.5)

    def one_head(pieces):
        query_head, key_head, value_head = pieces
        scores = low_back(matmul(query_head, key_head.T) * score_scale)
        scores = jnp.where(allowed, scores, NEGATIVE)
        weights = jax.nn.softmax(scores, axis=-1)
        return matmul(low(weights), value_head)
    mixture = lax.map(jax.checkpoint(one_head), (by_heads(queries), by_heads(key_block), by_heads(value_block)))
    return mixture.transpose(1, 0, 2).reshape(row_count, -1)

def item_forward(params, inputs, counted):
    embedding, first_gain, first_shift, query_weight, query_shift, key_weight, value_weight, value_shift, out_weight, out_shift, second_gain, second_shift, up_weight, up_shift, down_weight, down_shift = params
    seg_rows = inputs.shape[1]
    slot_ids = jnp.arange(SUMM)
    live_slots = slot_ids < counted
    live = live_slots.astype(jnp.float32)
    positions = jnp.concatenate([jnp.arange(seg_rows), seg_rows + slot_ids])
    own_live = jnp.concatenate([jnp.ones(seg_rows, dtype=bool), live_slots])
    prefix = None
    outputs = []
    summaries = []
    for segment in range(SEGS):
        rows = jnp.concatenate([inputs[segment], embedding], 0)
        act1 = low(layer_norm(rows, first_gain, first_shift))
        queries = low(low_back(matmul(act1, query_weight) + query_shift))
        key_block = low(low_back(matmul(act1, key_weight)))
        value_block = low(low_back(matmul(act1, value_weight) + value_shift))
        allowed = (positions[None, :] <= positions[:, None]) & own_live[None, :]
        if prefix is not None:
            prefix_act = low(layer_norm(prefix, first_gain, first_shift))
            key_block = jnp.concatenate([key_block, low(low_back(matmul(prefix_act, key_weight)))], 0)
            value_block = jnp.concatenate([value_block, low(low_back(matmul(prefix_act, value_weight) + value_shift))], 0)
            allowed = jnp.concatenate([allowed, jnp.broadcast_to(live_slots[None, :], (allowed.shape[0], SUMM))], 1)
        mixture = low(low_back(attention(queries, key_block, value_block, allowed)))
        middle = rows + low_back(matmul(mixture, out_weight) + out_shift)
        act2 = low(layer_norm(middle, second_gain, second_shift))
        before = low_back(matmul(act2, up_weight) + up_shift)
        activated = low(jax.nn.gelu(before, approximate=True))
        output_rows = middle + low_back(matmul(activated, down_weight) + down_shift)
        outputs.append(output_rows[:seg_rows])
        summary = output_rows[seg_rows:] * live[:, None]
        summaries.append(summary)
        prefix = low(summary)
    return (jnp.stack(outputs), jnp.stack(summaries))

def reference(hidden_in, summary_counts, summary_embed, ln1_gain, ln1_bias, w_query, b_query, w_key, w_value, b_value, w_out, b_out, ln2_gain, ln2_bias, w_up, b_up, w_down, b_down, d_hidden, d_summary):
    params = tuple((item.astype(jnp.float32) for item in (summary_embed, ln1_gain, ln1_bias, w_query, b_query, w_key, w_value, b_value, w_out, b_out, ln2_gain, ln2_bias, w_up, b_up, w_down, b_down)))

    def one_item(totals, item):
        inputs, counted, out_grad, summary_grad = item

        def forward(weights, values):
            return item_forward(weights, values, counted)
        (outputs, summaries), pull = jax.vjp(forward, params, inputs)
        grad_params, grad_inputs = pull((out_grad, summary_grad))
        totals = jax.tree.map(lambda first, second: first + second, totals, grad_params)
        return (totals, (outputs.astype(jnp.bfloat16), summaries.astype(jnp.bfloat16), grad_inputs))
    start = jax.tree.map(jnp.zeros_like, params)
    totals, (hidden_out, summary_out, grad_input) = lax.scan(one_item, start, (hidden_in.astype(jnp.float32), summary_counts, d_hidden.astype(jnp.float32), d_summary.astype(jnp.float32)))
    return (hidden_out, summary_out, grad_input, totals[0], totals[1], totals[2], totals[3], totals[4], totals[5], totals[6], totals[7], totals[8], totals[9], totals[10], totals[11], totals[12], totals[13], totals[14], totals[15])
```

```python
import functools

import jax
import jax.numpy as jnp
from jax import lax
from jax.experimental import pallas as pl
from jax.experimental.pallas import tpu as pltpu
from jax.sharding import PartitionSpec as P

HD = 64
EPSILON = 1e-05
NEGATIVE = -1e30
MESH = pl.DeviceIdType.MESH
BF = jnp.bfloat16
F32 = jnp.float32
PAIR_BIT = 1


def flip(index, bit):
    weight = 1 << bit
    return index + weight - 2 * weight * lax.rem(index // weight, 2)


def bit_of(index, bit):
    return lax.rem(index // (1 << bit), 2)


def grads_kernel(
    bits,
    tiles,
    lhs_ref,
    rhs_ref,
    small_ref,
    out_ref,
    small_out_ref,
    send0,
    recv0,
    keep0,
    sends,
    recvs,
    keeps,
    send_p,
    recv_p,
    keep_p,
    send_x,
    recv_x,
    small_cur,
    small_recv,
    sem0,
    sems,
    sem_p,
    sem_x,
    sem_s,
):
    b, s, t = lax.axis_index("batch"), lax.axis_index("seq"), lax.axis_index("tensor")
    halving = list(range(bits - 1, PAIR_BIT, -1))
    at_y = (flip(b, 0), s, t)
    at_p = (flip(b, PAIR_BIT), s, t)
    at_x = (b, 1 - s, t)
    at_h = [(flip(b, bit), s, t) for bit in halving]
    partners = [at_y, at_p, at_x] + at_h
    barrier = pltpu.get_barrier_semaphore()
    for partner in partners:
        pl.semaphore_signal(barrier, inc=1, device_id=partner, device_id_type=MESH)
    pl.semaphore_wait(barrier, len(partners))

    features = lhs_ref.shape[1]
    chunk = features // (1 << bits)
    half_count = 1 << (bits - 1)
    mine = bit_of(b, 0)

    def operand(i):
        return i // 4 + ((i + 1) // 4 + 2) // 3

    def remote(src, dst, sem, partner):
        return pltpu.make_async_remote_copy(
            src_ref=src,
            dst_ref=dst,
            send_sem=sem.at[0],
            recv_sem=sem.at[1],
            device_id=partner,
            device_id_type=MESH,
        )

    def copy_y(i):
        return remote(send0.at[i], recv0.at[i], sem0.at[i], at_y)

    def copy_h(k, i):
        return remote(sends[k].at[i], recvs[k].at[i], sems[k].at[i], at_h[k])

    def copy_p(i):
        return remote(send_p.at[i], recv_p.at[i], sem_p.at[i], at_p)

    def copy_x(i):
        return remote(send_x.at[i], recv_x.at[i], sem_x.at[i], at_x)

    def product(i, j, side):
        start = pl.multiple_of((2 * j + side) * chunk, chunk)
        return jnp.dot(
            lhs_ref[operand(i), pl.ds(start, chunk), :],
            rhs_ref[i],
            preferred_element_type=F32,
        )

    small_cur[...] = small_ref[...]
    small_partners = [at_y] + at_h + [at_p]
    for k, partner in enumerate(small_partners):
        copy = remote(small_cur, small_recv.at[k], sem_s.at[k], partner)
        copy.start()

        if k == 0:

            @pl.loop(0, tiles)
            def _(i):
                @pl.loop(0, half_count)
                def _(j):
                    at = pl.ds(pl.multiple_of(j * chunk, chunk), chunk)
                    send0[i, at, :] = product(i, j, 1 - mine).astype(BF)

                copy_y(i).start()

        copy.wait()
        small_cur[...] = small_cur[...] + small_recv[k]
    last = len(small_partners)
    copy = remote(small_cur, small_recv.at[last], sem_s.at[last], at_x)
    copy.start()
    copy.wait()
    small_out_ref[s] = small_cur[...]
    small_out_ref[1 - s] = small_recv[last]

    stages = len(halving)

    def split(i, k, total, rows):
        bit = bit_of(b, halving[k])
        half = rows // 2
        keeps[k][i] = total(pl.multiple_of(bit * half, half), half)
        sends[k][i] = total(pl.multiple_of((1 - bit) * half, half), half).astype(BF)
        copy_h(k, i).start()

    def stage_first(i):
        copy_y(i).wait()

        @pl.loop(0, half_count)
        def _(j):
            at = pl.ds(pl.multiple_of(j * chunk, chunk), chunk)
            keep0[at, :] = product(i, j, mine) + recv0[i, at, :].astype(F32)

        split(i, 0, lambda at, n: keep0[pl.ds(at, n), :], half_count * chunk)

    def stage_next(k, i):
        copy_h(k, i).wait()

        def total(at, n):
            return keeps[k][i, pl.ds(at, n), :] + recvs[k][i, pl.ds(at, n), :].astype(F32)

        rows = (half_count * chunk) >> (k + 1)
        if k + 1 < stages:
            split(i, k + 1, total, rows)
        else:
            bit = bit_of(b, PAIR_BIT)
            keep_p[i] = total(pl.multiple_of(bit * chunk, chunk), chunk)
            send_p[i] = total(pl.multiple_of((1 - bit) * chunk, chunk), chunk).astype(BF)
            copy_p(i).start()

    def stage_pair(i):
        copy_p(i).wait()
        bit = bit_of(b, PAIR_BIT)
        half = chunk // 2
        mine_at = pl.multiple_of(s * half, half)
        other_at = pl.multiple_of((1 - s) * half, half)
        out_ref[i, s, bit] = keep_p[i, pl.ds(mine_at, half), :]
        out_ref[i, s, 1 - bit] = recv_p[i, pl.ds(mine_at, half), :].astype(F32)
        send_x[i, bit] = keep_p[i, pl.ds(other_at, half), :].astype(BF)
        send_x[i, 1 - bit] = recv_p[i, pl.ds(other_at, half), :]
        copy_x(i).start()

    def stage_last(i):
        copy_x(i).wait()
        out_ref[i, 1 - s] = recv_x[i].astype(F32)

    @pl.loop(0, tiles + stages + 2)
    def _(i):
        @pl.when(i < tiles)
        def _():
            stage_first(i)

        for k in range(stages):

            @pl.when((i >= k + 1) & (i < tiles + k + 1))
            def _():
                stage_next(k, i - (k + 1))

        @pl.when((i >= stages + 1) & (i < tiles + stages + 1))
        def _():
            stage_pair(i - (stages + 1))

        @pl.when(i >= stages + 2)
        def _():
            stage_last(i - (stages + 2))


def reduce_grads(lhs, rhs, small):
    count = lax.axis_size("batch")
    bits = count.bit_length() - 1
    tiles, _, width = rhs.shape
    features = lhs.shape[1]
    chunk = features // count
    rows = features // 2
    halving = bits - 1 - PAIR_BIT
    dma = pltpu.SemaphoreType.DMA
    pieces = [rows >> (k + 1) for k in range(halving)]
    scratch = [
        pltpu.VMEM((tiles, rows, width), BF),
        pltpu.VMEM((tiles, rows, width), BF),
        pltpu.VMEM((rows, width), F32),
        [pltpu.VMEM((tiles, n, width), BF) for n in pieces],
        [pltpu.VMEM((tiles, n, width), BF) for n in pieces],
        [pltpu.VMEM((tiles, n, width), F32) for n in pieces],
        pltpu.VMEM((tiles, chunk, width), BF),
        pltpu.VMEM((tiles, chunk, width), BF),
        pltpu.VMEM((tiles, chunk, width), F32),
        pltpu.VMEM((tiles, 2, chunk // 2, width), BF),
        pltpu.VMEM((tiles, 2, chunk // 2, width), BF),
        pltpu.VMEM(small.shape, F32),
        pltpu.VMEM((bits + 1,) + small.shape, F32),
        dma((tiles, 2)),
        [dma((tiles, 2)) for _ in pieces],
        dma((tiles, 2)),
        dma((tiles, 2)),
        dma((bits + 1, 2)),
    ]
    vmem = pl.BlockSpec(memory_space=pltpu.VMEM)
    return pl.pallas_call(
        functools.partial(grads_kernel, bits, tiles),
        name="weight_grads",
        out_shape=(
            jax.ShapeDtypeStruct((tiles, 2, 2, chunk // 2, width), F32),
            jax.ShapeDtypeStruct((2,) + small.shape, F32),
        ),
        in_specs=[vmem] * 3,
        out_specs=(vmem, vmem),
        scratch_shapes=scratch,
        compiler_params=pltpu.CompilerParams(
            collective_id=1, has_side_effects=True, vmem_limit_bytes=62 * 2**20
        ),
    )(lhs, rhs, small)


def dot_nn(a, b):
    return jnp.dot(a, b, preferred_element_type=F32)


def dot_nt(a, b):
    return lax.dot_general(a, b, (((1,), (1,)), ((), ())), preferred_element_type=F32)


def dot_tn(a, b):
    return lax.dot_general(a, b, (((0,), (0,)), ((), ())), preferred_element_type=F32)


def total4(x):
    return lax.psum(x, ("seq", "tensor"))


def stats(x):
    m = jnp.mean(x, axis=1, keepdims=True)
    e = jnp.mean(x * x, axis=1, keepdims=True)
    return m, lax.rsqrt(e - m * m + EPSILON)


def norm_back(d, xhat, r, g):
    q = d * g
    return r * (
        q - jnp.mean(q, axis=1, keepdims=True) - xhat * jnp.mean(q * xhat, axis=1, keepdims=True)
    )


def heads(x):
    return x.reshape(x.shape[0], -1, HD).transpose(1, 0, 2)


def unheads(x):
    return x.transpose(1, 0, 2).reshape(x.shape[1], -1)


def gelu_parts(v):
    c = 0.7978845608028654
    th = jnp.tanh(c * (v + 0.044715 * v * v * v))
    act = 0.5 * v * (1.0 + th)
    slope = 0.5 * (1.0 + th) + 0.5 * v * (1.0 - th * th) * c * (1.0 + 3 * 0.044715 * v * v)
    return act, slope


def local(
    hidden_in, summary_counts, summary_embed, ln1_gain, ln1_bias, w_query, b_query, w_key, w_value,
    b_value, w_out, b_out, ln2_gain, ln2_bias, w_up, b_up, w_down, b_down, d_hidden, d_summary,
):
    b, s, t = lax.axis_index("batch"), lax.axis_index("seq"), lax.axis_index("tensor")
    slots = summary_embed.shape[0]
    pad = 64
    seg_count = hidden_in.shape[1]
    toks = hidden_in.shape[2] * 2
    counted = summary_counts[0]
    full = lambda x: lax.all_gather(x, "tensor", axis=x.ndim - 1, tiled=True)
    tokens = lambda x: full(lax.all_gather(x[0], "seq", axis=1, tiled=True))
    padded = lambda x: jnp.pad(x, ((0, pad - x.shape[0]), (0, 0)))
    hid = tokens(hidden_in).astype(F32)
    dhid = tokens(d_hidden).astype(F32)
    dsum = full(d_summary[0]).astype(F32)
    emb = padded(full(summary_embed).astype(F32))
    g1, c1, g2, c2, bo, bd = (full(v).astype(F32)[None] for v in (ln1_gain, ln1_bias, ln2_gain, ln2_bias, b_out, b_down))
    nq = w_query.shape[1] // 2
    nu = w_up.shape[1] // 2
    cut = lambda x, n, axis: lax.dynamic_slice_in_dim(x, s * n, n, axis)
    wq, wk, wv = (cut(w, nq, 1) for w in (w_query, w_key, w_value))
    bq, bv = (cut(v, nq, 0).astype(F32)[None] for v in (b_query, b_value))
    wo = cut(w_out, nq, 0)
    wu, bu, wd = cut(w_up, nu, 1), cut(b_up, nu, 0).astype(F32)[None], cut(w_down, nu, 0)
    live = (jnp.arange(pad) < counted)
    livef = live.astype(F32)[:, None]
    n_own = toks + pad
    pos = jnp.arange(n_own)
    own_live = jnp.concatenate([jnp.ones(toks, bool), live])
    seen = (pos[None, :] <= pos[:, None]) & own_live[None, :]
    seen_p = jnp.concatenate([seen, jnp.broadcast_to(live[None], (n_own, pad))], 1)
    low = lambda x: x.astype(BF)
    kept, outs, sums = [], [], []
    prefix = None
    for seg in range(seg_count):
        rows = jnp.concatenate([hid[seg], emb], 0)
        stacked = rows if prefix is None else jnp.concatenate([rows, prefix.astype(F32)], 0)
        m1, r1 = stats(stacked)
        xh1 = (stacked - m1) * r1
        act1 = low(xh1 * g1 + c1)
        q = low(dot_nn(act1[:n_own], wq) + bq)
        k = low(dot_nn(act1, wk))
        v = low(dot_nn(act1, wv) + bv)
        sc = jnp.einsum("hqd,hkd->hqk", heads(q), heads(k), preferred_element_type=F32) * HD**-0.5
        sc = jnp.where((seen if prefix is None else seen_p)[None], sc, NEGATIVE)
        p = jax.nn.softmax(sc, axis=-1)
        mix = low(unheads(jnp.einsum("hqk,hkd->hqd", low(p), heads(v), preferred_element_type=F32)))
        mid = rows + total4(low(dot_nn(mix, wo))).astype(F32) + bo
        m2, r2 = stats(mid)
        xh2 = (mid - m2) * r2
        act2 = low(xh2 * g2 + c2)
        activated, slope = gelu_parts(dot_nn(act2, wu) + bu)
        activated = low(activated)
        out = mid + total4(low(dot_nn(activated, wd))).astype(F32) + bd
        outs.append(low(out[:toks]))
        prefix = low(out[toks:] * livef)
        sums.append(prefix[:slots])
        kept.append((xh1, r1, act1, q, k, v, p, mix, xh2, r2, act2, slope, activated))
    carried = jnp.zeros((pad, hid.shape[2]), F32)
    gin = [None] * seg_count
    got = [None] * seg_count
    small = 0.0
    f = hid.shape[2]
    quarter = f // 4
    fcut = lambda x: lax.dynamic_slice_in_dim(x, t * (f // 2) + s * quarter, quarter, 1)
    csum = lambda x: jnp.sum(x.astype(F32), axis=0, keepdims=True)
    for seg in reversed(range(seg_count)):
        xh1, r1, act1, q, k, v, p, mix, xh2, r2, act2, slope, activated = kept[seg]
        dout = jnp.concatenate([dhid[seg], (padded(dsum[seg]) + carried) * livef], 0)
        gd = low(dout)
        db = low(slope * dot_nt(gd, wd))
        da2 = total4(low(dot_nt(db, wu))).astype(F32)
        dmid = dout + norm_back(da2, xh2, r2, g2)
        gm = low(dmid)
        dmix = low(dot_nt(gm, wo))
        hq, hk, hv, hg = heads(q), heads(k), heads(v), heads(dmix)
        dp = jnp.einsum("hqd,hkd->hqk", hg, hv, preferred_element_type=F32)
        ds = low(p * (dp - jnp.sum(p * dp, axis=-1, keepdims=True)))
        ein = functools.partial(jnp.einsum, preferred_element_type=F32)
        dq = low(unheads(ein("hqk,hkd->hqd", ds, hk)) * HD**-0.5)
        dk = low(unheads(ein("hqk,hqd->hkd", ds, hq)) * HD**-0.5)
        dv = low(unheads(ein("hqk,hqd->hkd", low(p), hg)))
        da1 = dot_nt(dk, wk) + dot_nt(dv, wv)
        da1 = da1.at[:n_own].add(dot_nt(dq, wq))
        da1 = total4(low(da1)).astype(F32)
        dst = norm_back(da1, xh1, r1, g1)
        drows = dmid + dst[:n_own]
        gin[seg] = drows[:toks]
        if seg > 0:
            carried = dst[n_own:]
        fs = [drows[toks : toks + slots]] + [
            jnp.sum(a, axis=0, keepdims=True)
            for a in (da1 * xh1, da1, gm.astype(F32), da2 * xh2, da2, gd.astype(F32))
        ]
        fs = fcut(jnp.concatenate(fs, 0))
        us = [csum(dq), csum(dv), csum(db).reshape(4, -1)]
        rest = -(fs.shape[0] + 6) % 8
        small = small + jnp.concatenate([fs] + us + [jnp.zeros((rest, quarter), F32)], 0)
        got[seg] = (act1, gm, act2, gd, dq, dk, dv, mix, db, activated)

    def stack(n, prefix_rows):
        first, second = got[0][n], got[1][n]
        if prefix_rows:
            body = [first, second] if second.shape[0] > n_own else [first, second, jnp.zeros((pad, second.shape[1]), BF)]
        else:
            body = [first, second, jnp.zeros((pad, first.shape[1]), BF)]
        return jnp.concatenate(body, 0)

    lhs = jnp.stack([stack(0, True)] + [stack(n, False) for n in (1, 2, 3)])
    right = [stack(4, True), stack(5, True), stack(6, True), stack(7, False), stack(8, False), stack(9, False)]
    count = lax.axis_size("batch")
    pair = [(i, i ^ (1 << PAIR_BIT)) for i in range(count)]
    zl = bit_of(b, PAIR_BIT)
    half = lambda x, side: lax.dynamic_slice_in_dim(x, side * (x.shape[1] // 2), x.shape[1] // 2, 1)
    width = nq // 2
    tile = lambda x: x.reshape(x.shape[0], -1, width).transpose(1, 0, 2)
    keep = jnp.concatenate([tile(half(x, zl)) for x in right], 0)
    give = jnp.concatenate([tile(half(x, 1 - zl)) for x in right], 0)
    take = lax.ppermute(give, "batch", pair)
    lhs_take = lax.ppermute(lhs, "batch", pair)
    rhs = jnp.concatenate([keep, take], 1)
    lhs = jnp.concatenate([lhs, lhs_take], 1).transpose(0, 2, 1)
    w, sm = reduce_grads(lhs, rhs, small)
    def place(lo, hi):
        x = w[lo:hi]
        return x.transpose(3, 1, 2, 0, 4).reshape(x.shape[3], -1)
    per = nu // 2 // width
    gq, gk, gv, go = (place(i, i + 1) for i in range(4))
    gu, gdn = place(4, 4 + per), place(4 + per, 4 + 2 * per)
    sm = sm.transpose(1, 0, 2)
    fl = lambda r: sm[r].reshape(-1)
    n = slots
    bup = sm[n + 8 : n + 12].transpose(1, 0, 2).reshape(-1)
    cutf = lambda x: lax.dynamic_slice_in_dim(x, t * (f // 2), f // 2, x.ndim - 1)
    own = lambda x: lax.dynamic_slice_in_dim(cutf(x), s * (toks // 2), toks // 2, 1)
    return (
        own(jnp.stack(outs))[None], cutf(jnp.stack(sums))[None], own(jnp.stack(gin))[None],
        sm[:n].reshape(n, -1), fl(n), fl(n + 1), gq, fl(n + 6), gk, gv, fl(n + 7), go.T, fl(n + 2),
        fl(n + 3), fl(n + 4), gu, bup, gdn.T, fl(n + 5),
    )


def solution(mesh):
    return jax.shard_map(
        local,
        mesh=mesh,
        in_specs=(
            P("batch", None, "seq", "tensor"),
            P("batch"),
            P(None, "tensor"),
            P("tensor"),
            P("tensor"),
            P(None, "tensor"),
            P("tensor"),
            P(None, "tensor"),
            P(None, "tensor"),
            P("tensor"),
            P("tensor", None),
            P("tensor"),
            P("tensor"),
            P("tensor"),
            P(None, "tensor"),
            P("tensor"),
            P("tensor", None),
            P("tensor"),
            P("batch", None, "seq", "tensor"),
            P("batch", None, None, "tensor"),
        ),
        out_specs=(
            P("batch", None, "seq", "tensor"),
            P("batch", None, None, "tensor"),
            P("batch", None, "seq", "tensor"),
            P(None, "tensor"),
            P("tensor"),
            P("tensor"),
            P(("batch", "seq"), "tensor"),
            P("tensor"),
            P(("batch", "seq"), "tensor"),
            P(("batch", "seq"), "tensor"),
            P("tensor"),
            P("tensor", ("batch", "seq")),
            P("tensor"),
            P("tensor"),
            P("tensor"),
            P(("batch", "seq"), "tensor"),
            P("tensor"),
            P("tensor", ("batch", "seq")),
            P("tensor"),
        ),
        check_vma=False,
    )
```

```python
import functools

import jax
import jax.numpy as jnp
from jax import lax
from jax.experimental import pallas as pl
from jax.experimental.pallas import tpu as pltpu
from jax.sharding import PartitionSpec as P

HD = 64
EPSILON = 1e-05
NEGATIVE = -1e30
MESH = pl.DeviceIdType.MESH
BF = jnp.bfloat16
F32 = jnp.float32
PAIR_BIT = 1


def flip(index, bit):
    weight = 1 << bit
    return index + weight - 2 * weight * lax.rem(index // weight, 2)


def bit_of(index, bit):
    return lax.rem(index // (1 << bit), 2)


def dot_nt(a, b):
    return lax.dot_general(a, b, (((1,), (1,)), ((), ())), preferred_element_type=F32)


def dot_tn(a, b):
    return lax.dot_general(a, b, (((0,), (0,)), ((), ())), preferred_element_type=F32)


def grads_kernel(
    bits,
    tiles,
    width,
    la_ref,
    lx_ref,
    ra_ref,
    rb_ref,
    small_ref,
    out_ref,
    small_out_ref,
    send0,
    recv0,
    keep0,
    both,
    sends,
    recvs,
    keeps,
    send_p,
    recv_p,
    keep_p,
    send_x,
    recv_x,
    small_cur,
    small_recv,
    sem0,
    sems,
    sem_p,
    sem_x,
    sem_s,
):
    b, s, t = lax.axis_index("batch"), lax.axis_index("seq"), lax.axis_index("tensor")
    halving = list(range(bits - 1, PAIR_BIT, -1))
    at_y = (flip(b, 0), s, t)
    at_p = (flip(b, PAIR_BIT), s, t)
    at_x = (b, 1 - s, t)
    at_h = [(flip(b, bit), s, t) for bit in halving]
    partners = [at_y, at_p, at_x] + at_h
    barrier = pltpu.get_barrier_semaphore()
    for partner in partners:
        pl.semaphore_signal(barrier, inc=1, device_id=partner, device_id_type=MESH)
    pl.semaphore_wait(barrier, len(partners))

    features = la_ref.shape[1]
    inner = ra_ref.shape[1] // width
    chunk = features // (1 << bits)
    half_count = 1 << (bits - 1)
    mine = bit_of(b, 0)

    def remote(src, dst, sem, partner):
        return pltpu.make_async_remote_copy(
            src_ref=src,
            dst_ref=dst,
            send_sem=sem.at[0],
            recv_sem=sem.at[1],
            device_id=partner,
            device_id_type=MESH,
        )

    def copy_y(i):
        return remote(send0.at[i], recv0.at[i], sem0.at[i], at_y)

    def copy_h(k, i):
        return remote(sends[k].at[i], recvs[k].at[i], sems[k].at[i], at_h[k])

    def copy_p(i):
        return remote(send_p.at[i], recv_p.at[i], sem_p.at[i], at_p)

    def copy_x(i):
        return remote(send_x.at[i], recv_x.at[i], sem_x.at[i], at_x)

    per = (tiles - inner - 1) // 2

    def product(i, side, put):
        def blocks(left, right):
            @pl.loop(0, half_count)
            def _(j):
                at = pl.ds(pl.multiple_of(j * chunk, chunk), chunk)
                if chunk % 128 == 0:
                    start = pl.multiple_of((2 * j + side) * chunk, chunk)
                    put(at, dot_tn(left(pl.ds(start, chunk)), right))
                else:
                    start = pl.multiple_of(2 * j * chunk, 2 * chunk)
                    both[...] = dot_tn(left(pl.ds(start, 2 * chunk)), right)
                    put(at, both[pl.ds(pl.multiple_of(side * chunk, chunk), chunk), :])

        @pl.when(i < inner)
        def _():
            cols = pl.ds(pl.multiple_of(i * width, width), width)
            blocks(lambda at: la_ref[:, at], ra_ref[:, cols])

        @pl.when(i >= inner)
        def _():
            k = i - inner
            cols = pl.ds(pl.multiple_of(k * width, width), width)
            op = (k + per - 1) // per
            blocks(lambda at: lx_ref[op, :, at], rb_ref[:, cols])

    small_cur[...] = small_ref[...]
    small_partners = [at_y] + at_h + [at_p]
    for k, partner in enumerate(small_partners):
        copy = remote(small_cur, small_recv.at[k], sem_s.at[k], partner)
        copy.start()

        if k == 0:

            @pl.loop(0, tiles)
            def _(i):
                def put(at, value):
                    send0[i, at, :] = value.astype(BF)

                product(i, 1 - mine, put)
                copy_y(i).start()

        copy.wait()
        small_cur[...] = small_cur[...] + small_recv[k]
    last = len(small_partners)
    copy = remote(small_cur, small_recv.at[last], sem_s.at[last], at_x)
    copy.start()
    copy.wait()
    small_out_ref[s] = small_cur[...]
    small_out_ref[1 - s] = small_recv[last]

    stages = len(halving)

    def split(i, k, total, rows):
        bit = bit_of(b, halving[k])
        half = rows // 2
        keeps[k][i] = total(pl.multiple_of(bit * half, half), half)
        sends[k][i] = total(pl.multiple_of((1 - bit) * half, half), half).astype(BF)
        copy_h(k, i).start()

    def stage_first(i):
        copy_y(i).wait()

        def put(at, value):
            keep0[at, :] = value + recv0[i, at, :].astype(F32)

        product(i, mine, put)
        split(i, 0, lambda at, n: keep0[pl.ds(at, n), :], half_count * chunk)

    def stage_next(k, i):
        copy_h(k, i).wait()

        def total(at, n):
            return keeps[k][i, pl.ds(at, n), :] + recvs[k][i, pl.ds(at, n), :].astype(F32)

        rows = (half_count * chunk) >> (k + 1)
        if k + 1 < stages:
            split(i, k + 1, total, rows)
        else:
            bit = bit_of(b, PAIR_BIT)
            keep_p[i] = total(pl.multiple_of(bit * chunk, chunk), chunk)
            send_p[i] = total(pl.multiple_of((1 - bit) * chunk, chunk), chunk).astype(BF)
            copy_p(i).start()

    def stage_pair(i):
        copy_p(i).wait()
        bit = bit_of(b, PAIR_BIT)
        half = chunk // 2
        mine_at = pl.multiple_of(s * half, half)
        other_at = pl.multiple_of((1 - s) * half, half)
        out_ref[i, s, bit] = keep_p[i, pl.ds(mine_at, half), :]
        out_ref[i, s, 1 - bit] = recv_p[i, pl.ds(mine_at, half), :].astype(F32)
        send_x[i, bit] = keep_p[i, pl.ds(other_at, half), :].astype(BF)
        send_x[i, 1 - bit] = recv_p[i, pl.ds(other_at, half), :]
        copy_x(i).start()

    def stage_last(i):
        copy_x(i).wait()
        out_ref[i, 1 - s] = recv_x[i].astype(F32)

    @pl.loop(0, tiles + stages + 2)
    def _(i):
        @pl.when(i < tiles)
        def _():
            stage_first(i)

        for k in range(stages):

            @pl.when((i >= k + 1) & (i < tiles + k + 1))
            def _():
                stage_next(k, i - (k + 1))

        @pl.when((i >= stages + 1) & (i < tiles + stages + 1))
        def _():
            stage_pair(i - (stages + 1))

        @pl.when(i >= stages + 2)
        def _():
            stage_last(i - (stages + 2))


def reduce_grads(la, lx, ra, rb, small, width):
    count = lax.axis_size("batch")
    bits = count.bit_length() - 1
    tiles = (ra.shape[1] + rb.shape[1]) // width
    features = la.shape[1]
    chunk = features // count
    rows = features // 2
    halving = bits - 1 - PAIR_BIT
    dma = pltpu.SemaphoreType.DMA
    pieces = [rows >> (k + 1) for k in range(halving)]
    scratch = [
        pltpu.VMEM((tiles, rows, width), BF),
        pltpu.VMEM((tiles, rows, width), BF),
        pltpu.VMEM((rows, width), F32),
        pltpu.VMEM((2 * chunk if chunk % 128 else 8, width), F32),
        [pltpu.VMEM((tiles, n, width), BF) for n in pieces],
        [pltpu.VMEM((tiles, n, width), BF) for n in pieces],
        [pltpu.VMEM((tiles, n, width), F32) for n in pieces],
        pltpu.VMEM((tiles, chunk, width), BF),
        pltpu.VMEM((tiles, chunk, width), BF),
        pltpu.VMEM((tiles, chunk, width), F32),
        pltpu.VMEM((tiles, 2, chunk // 2, width), BF),
        pltpu.VMEM((tiles, 2, chunk // 2, width), BF),
        pltpu.VMEM(small.shape, F32),
        pltpu.VMEM((bits + 1,) + small.shape, F32),
        dma((tiles, 2)),
        [dma((tiles, 2)) for _ in pieces],
        dma((tiles, 2)),
        dma((tiles, 2)),
        dma((bits + 1, 2)),
    ]
    vmem = pl.BlockSpec(memory_space=pltpu.VMEM)
    return pl.pallas_call(
        functools.partial(grads_kernel, bits, tiles, width),
        name="weight_grads",
        out_shape=(
            jax.ShapeDtypeStruct((tiles, 2, 2, chunk // 2, width), F32),
            jax.ShapeDtypeStruct((2,) + small.shape, F32),
        ),
        in_specs=[vmem] * 5,
        out_specs=(vmem, vmem),
        scratch_shapes=scratch,
        compiler_params=pltpu.CompilerParams(
            collective_id=1, has_side_effects=True, vmem_limit_bytes=62 * 2**20
        ),
    )(la, lx, ra, rb, small)


def chain_kernel(
    count_ref,
    vecu_ref,
    hid_hbm,
    dhid_hbm,
    emb_hbm,
    dsum_hbm,
    vec_hbm,
    wq_hbm,
    wk_hbm,
    wv_hbm,
    wo_hbm,
    wu_hbm,
    wd_hbm,
    hid_out,
    sum_out,
    gin_out,
    small_out,
    la_hbm,
    lx_hbm,
    ra_hbm,
    rb_hbm,
    wqkv,
    wo,
    wu,
    wd,
    rows,
    act1,
    qkv,
    probs,
    mix,
    mid,
    act2,
    actv,
    db,
    slope0,
    gd,
    gm,
    dmix,
    dqkv,
    dsum,
    vec,
    bias,
    stat,
    outacc,
    fsum,
    gsum,
    gx_send,
    gx_recv,
    ar_send,
    ar_core,
    ar_x,
    ar_full,
    ar_own,
    wsem,
    lsem,
    rsem,
):
    b, s, t = lax.axis_index("batch"), lax.axis_index("seq"), lax.axis_index("tensor")
    at_core = (b, s, 1 - t)
    at_x = (b, 1 - s, t)
    at_p = (flip(b, PAIR_BIT), s, t)
    zl = bit_of(b, PAIR_BIT)
    barrier = pltpu.get_barrier_semaphore()
    for partner in (at_core, at_x, at_p):
        pl.semaphore_signal(barrier, inc=1, device_id=partner, device_id_type=MESH)

    toks = hid_hbm.shape[1]
    slots = emb_hbm.shape[0]
    feats = rows.shape[1]
    half = feats // 2
    quarter = feats // 4
    span = 2 * toks
    s0, t0, t1, s1, p0 = 0, slots, slots + span, slots + 2 * span, 2 * slots + 2 * span
    own = slots + span
    end = p0 + slots
    nq = wo.shape[0]
    nu = wu.shape[1]
    my_cols = pl.ds(pl.multiple_of(t * half, half), half)
    its_cols = pl.ds(pl.multiple_of((1 - t) * half, half), half)
    my_toks = pl.multiple_of(s * toks, toks)
    its_toks = pl.multiple_of((1 - s) * toks, toks)
    my_quarter = pl.ds(pl.multiple_of(t * half + s * quarter, quarter), quarter)

    counter = {"l": 0, "r": 0}

    def local(src, dst):
        counter["l"] += 1
        copy = pltpu.make_async_copy(src, dst, lsem.at[counter["l"] - 1])
        copy.start()
        return copy

    def remote(src, dst, partner):
        counter["r"] += 1
        at = counter["r"] - 1
        copy = pltpu.make_async_remote_copy(
            src_ref=src,
            dst_ref=dst,
            send_sem=rsem.at[at, 0],
            recv_sem=rsem.at[at, 1],
            device_id=partner,
            device_id_type=MESH,
        )
        copy.start()
        return copy

    part = lambda ref, n, axis: (
        ref.at[:, pl.ds(pl.multiple_of(s * n, n), n)]
        if axis
        else ref.at[pl.ds(pl.multiple_of(s * n, n), n), :]
    )
    weights = []
    for at, (src, dst) in enumerate(
        (
            (part(wq_hbm, nq, 1), wqkv.at[:, pl.ds(0, nq)]),
            (part(wk_hbm, nq, 1), wqkv.at[:, pl.ds(nq, nq)]),
            (part(wv_hbm, nq, 1), wqkv.at[:, pl.ds(2 * nq, nq)]),
            (part(wo_hbm, nq, 0), wo),
            (part(wu_hbm, nu, 1), wu),
            (part(wd_hbm, nu, 0), wd),
        )
    ):
        copy = pltpu.make_async_copy(src, dst, wsem.at[at])
        weights.append(copy)

    firsts = [
        local(emb_hbm, rows.at[pl.ds(s0, slots), my_cols]),
        local(emb_hbm, rows.at[pl.ds(s1, slots), my_cols]),
        local(vec_hbm, vec.at[:, my_cols]),
    ]
    for seg, at in enumerate((t0, t1)):
        firsts.append(local(hid_hbm.at[seg], rows.at[pl.ds(at + my_toks, toks), my_cols]))
    laters = [local(dsum_hbm, dsum.at[:, my_cols])]
    for seg, at in enumerate((t0, t1)):
        laters.append(local(dhid_hbm.at[seg], gd.at[pl.ds(at + my_toks, toks), my_cols]))
    for copy in weights[:3]:
        copy.start()
    pl.semaphore_wait(barrier, 3)

    from_x, from_core, forwards = [], [], []
    for src, dst, at in (
        (hid_hbm.at[0], rows, t0),
        (hid_hbm.at[1], rows, t1),
        (dhid_hbm.at[0], gd, t0),
        (dhid_hbm.at[1], gd, t1),
    ):
        block = dst.at[pl.ds(at + my_toks, toks), my_cols]
        from_x.append((remote(src, block, at_x), dst, at))
    from_core.append(remote(emb_hbm, rows.at[pl.ds(s0, slots), my_cols], at_core))
    from_core.append(remote(emb_hbm, rows.at[pl.ds(s1, slots), my_cols], at_core))
    from_core.append(remote(vec_hbm, vec.at[:, my_cols], at_core))
    for src, dst, at in ((hid_hbm.at[0], rows, t0), (hid_hbm.at[1], rows, t1)):
        from_core.append(remote(src, dst.at[pl.ds(at + my_toks, toks), my_cols], at_core))
    late_core = [remote(dsum_hbm, dsum.at[:, my_cols], at_core)]
    for src, dst, at in ((dhid_hbm.at[0], gd, t0), (dhid_hbm.at[1], gd, t1)):
        late_core.append(remote(src, dst.at[pl.ds(at + my_toks, toks), my_cols], at_core))
    for copy in weights[3:]:
        copy.start()

    live_count = count_ref[0]
    row_live = (lax.broadcasted_iota(jnp.int32, (slots, 1), 0) < live_count).astype(F32)
    dqkv[pl.ds(p0, slots), pl.ds(0, nq)] = jnp.zeros((slots, nq), BF)
    bias[:, pl.ds(0, nq)] = vecu_ref[:, pl.ds(pl.multiple_of(s * nq, nq), nq)]
    bias[:, pl.ds(nq, nq)] = jnp.zeros((1, nq), F32)
    bias[:, pl.ds(2 * nq, nq)] = vecu_ref[:, pl.ds(pl.multiple_of((2 + s) * nq, nq), nq)]
    bias[:, pl.ds(3 * nq, nu)] = vecu_ref[:, pl.ds(pl.multiple_of(4 * nq + s * nu, nq), nu)]
    fsum[...] = jnp.zeros_like(fsum)
    gsum[...] = jnp.zeros_like(gsum)

    step = 16
    inverse = 1.0 / feats

    def row_loop(start, n, body):
        @pl.loop(0, n // step)
        def _(i):
            body(pl.ds(pl.multiple_of(start + i * step, step), step))

    def mean(x):
        return jnp.sum(x, axis=1, keepdims=True) * inverse

    def stats(x):
        m = mean(x)
        return m, lax.rsqrt(mean(x * x) - m * m + EPSILON)

    def norm1(start, n):
        def body(at):
            x = rows[at, :].astype(F32)
            m, r = stats(x)
            act1[at, :] = ((x - m) * r * vec[0:1, :] + vec[1:2, :]).astype(BF)
            stat[at, 0:1] = m
            stat[at, 1:2] = r

        row_loop(start, n, body)

    def norm_back(d, xhat, r, gain):
        q = d * gain
        return r * (q - mean(q) - xhat * mean(q * xhat))

    def fold(x):
        return jnp.sum(x.reshape(step // 8, 8, x.shape[1]), axis=0)

    wide = 512

    def col_loop(n, body):
        @pl.loop(0, n // wide)
        def _(j):
            body(pl.multiple_of(j * wide, wide))

    def project(at, n, lo, hi):
        def body(c):
            cols = pl.ds(pl.multiple_of(lo + c, wide), wide)
            x = jnp.dot(act1[pl.ds(at, n), :], wqkv[:, cols], preferred_element_type=F32)
            qkv[pl.ds(at, n), cols] = (x + bias[:, cols]).astype(BF)

        col_loop(hi - lo, body)

    class Total:
        def __init__(self, n, at, full, pieces, own_at=0):
            self.n, self.at, self.full, self.own_at = n, at, full, own_at
            self.pieces = pieces

        def mine(self, r, n):
            if self.full is None:
                return ar_own.at[pl.ds(self.own_at + r, n), :]
            return ar_full.at[pl.ds(self.full + r, n), my_cols]

        def start(self, product):
            at = pl.ds(self.at, self.n)

            def other(c):
                x = product(pl.multiple_of((1 - t) * half + c, wide), wide)
                ar_send[at, pl.ds(c, wide)] = x.astype(BF)

            col_loop(half, other)
            self.core = remote(ar_send.at[at, :], ar_core.at[at, :], at_core)

            def this(c):
                x = product(pl.multiple_of(t * half + c, wide), wide)
                if self.full is None:
                    ar_own[pl.ds(self.own_at, self.n), pl.ds(c, wide)] = x.astype(BF)
                else:
                    cols = pl.ds(pl.multiple_of(t * half + c, wide), wide)
                    ar_full[pl.ds(self.full, self.n), cols] = x.astype(BF)

            col_loop(half, this)

        def middle(self):
            self.core.wait()
            self.xs = []
            for base, n, scatter in self.pieces:
                at = pl.ds(self.at + base, n)
                ar_core[at, :] = (
                    self.mine(base, n)[...].astype(F32) + ar_core[at, :].astype(F32)
                ).astype(BF)
                if scatter:
                    src = ar_core.at[pl.ds(self.at + base + its_toks, toks), :]
                    dst = ar_x.at[pl.ds(self.at + base, toks), :]
                else:
                    src, dst = ar_core.at[at, :], ar_x.at[at, :]
                self.xs.append(remote(src, dst, at_x))

        def sums(self, base, n, scatter):
            if scatter:
                near = ar_core[pl.ds(self.at + base + my_toks, toks), :]
                far = ar_x[pl.ds(self.at + base, toks), :]
            else:
                near = ar_core[pl.ds(self.at + base, n), :]
                far = ar_x[pl.ds(self.at + base, n), :]
            return near.astype(F32) + far.astype(F32)

        def finish(self):
            self.backs = []
            for (base, n, scatter), copy in zip(self.pieces, self.xs):
                copy.wait()
                n = toks if scatter else n
                block = ar_full.at[pl.ds(self.full + base, n), my_cols]
                block[...] = self.sums(base, n, scatter).astype(BF)
                self.backs.append(remote(block, block, at_core))

        def done(self):
            for copy in self.backs:
                copy.wait()

    whole = lambda n: [(i, 64, False) for i in range(0, n, 64)]

    def out_product(at, n):
        return lambda c, w: jnp.dot(
            mix[pl.ds(at, n), :], wo[:, pl.ds(c, w)], preferred_element_type=F32
        )

    def down_product(at, n):
        return lambda c, w: jnp.dot(
            actv[pl.ds(at, n), :], wd[:, pl.ds(c, w)], preferred_element_type=F32
        )

    def up_back(at, n):
        return lambda c, w: dot_nt(db[pl.ds(at, n), :], wu[pl.ds(c, w), :])

    def in_back(at, n, lo):
        return lambda c, w: dot_nt(
            dqkv[pl.ds(at, n), pl.ds(lo, 3 * nq - lo)], wqkv[pl.ds(c, w), pl.ds(lo, 3 * nq - lo)]
        )

    def enter_ffn(total, at, n):
        def body(i):
            r = pl.ds(pl.multiple_of(at + i * step, step), step)
            f = pl.ds(pl.multiple_of(total.full + i * step, step), step)
            x = rows[r, :].astype(F32) + ar_full[f, :].astype(F32) + vec[4:5, :]
            m, rs = stats(x)
            mid[r, :] = x
            act2[r, :] = ((x - m) * rs * vec[2:3, :] + vec[3:4, :]).astype(BF)
            stat[r, 2:3] = m
            stat[r, 3:4] = rs

        pl.loop(0, n // step)(body)

    def gelu(v):
        c = 0.7978845608028654
        th = jnp.tanh(c * (v + 0.044715 * (v * v * v)))
        act = 0.5 * v * (1.0 + th)
        sl = 0.5 * (1.0 + th) + (0.5 * c) * v * (1.0 - th * th) * (1.0 + (3 * 0.044715) * v * v)
        return act, sl

    def ffn(at, n, back):
        r = pl.ds(at, n)

        def body(c):
            cols = pl.ds(c, wide)
            v = jnp.dot(act2[r, :], wu[:, cols], preferred_element_type=F32)
            act, sl = gelu(v + bias[:, pl.ds(pl.multiple_of(3 * nq + c, wide), wide)])
            actv[r, cols] = act.astype(BF)
            if back:
                db[r, cols] = (sl * dot_nt(gd[r, :], wd[cols, :])).astype(BF)
            else:
                slope0[:, cols] = sl

        col_loop(nu, body)

    def leave_ffn(total, at, n):
        def body(i):
            r = pl.ds(pl.multiple_of(at + i * step, step), step)
            f = pl.ds(pl.multiple_of(total.full + i * step, step), step)
            d = ar_full[f, :].astype(F32)
            xhat = (mid[r, :] - stat[r, 2:3]) * stat[r, 3:4]
            fsum[pl.ds(0, 8), :] = fsum[pl.ds(0, 8), :] + fold(d * xhat)
            fsum[pl.ds(8, 8), :] = fsum[pl.ds(8, 8), :] + fold(d)
            dm = gd[r, :].astype(F32) + norm_back(d, xhat, stat[r, 3:4], vec[2:3, :])
            mid[r, :] = dm
            gm[r, :] = dm.astype(BF)

        pl.loop(0, n // step)(body)

    def mix_back(at, n):
        dmix[pl.ds(at, n), :] = dot_nt(gm[pl.ds(at, n), :], wo[...]).astype(BF)

    pairs = nq // (2 * HD)
    scale = HD**-0.5

    def seen(seg, keys):
        q = lax.broadcasted_iota(jnp.int32, (own, keys), 0)
        k = lax.broadcasted_iota(jnp.int32, (own, keys), 1)
        if seg == 0:
            q = jnp.where(q < slots, q + span, q - slots)
            slot = k
            token = k >= slots
            k = jnp.where(token, k - slots, k + span)
            return (k <= q) & (token | (slot < live_count))
        token = k < span
        ahead = k >= own
        slot = jnp.where(ahead, k - own, k - span)
        return (ahead | (k <= q)) & (token | (slot < live_count))

    def lanes(n):
        first = (lax.broadcasted_iota(jnp.int32, (n, 2 * HD), 1) < HD).astype(F32)
        return first.astype(BF), (1.0 - first).astype(BF)

    def attend(seg):
        at, keys = (s0, own) if seg == 0 else (t1, own + slots)
        q_rows, k_rows = pl.ds(at, own), pl.ds(at, keys)

        @pl.loop(0, pairs)
        def _(j):
            col = lambda g: pl.ds(pl.multiple_of(g * nq + j * 2 * HD, 2 * HD), 2 * HD)
            q, k, v = qkv[q_rows, col(0)], qkv[k_rows, col(1)], qkv[k_rows, col(2)]
            first = lanes(keys)
            allowed = seen(seg, keys)
            got = jnp.zeros((own, 2 * HD), F32)
            for h in range(2):
                pick = first[h]
                sc = dot_nt(q, k * pick) * scale
                sc = jnp.where(allowed, sc, NEGATIVE)
                e = jnp.exp(sc - jnp.max(sc, axis=1, keepdims=True))
                p = (e / jnp.sum(e, axis=1, keepdims=True)).astype(BF)
                probs[seg, 2 * j + h, :, pl.ds(0, keys)] = p
                got += jnp.dot(p, v * pick, preferred_element_type=F32)
            mix[q_rows, pl.ds(pl.multiple_of(j * 2 * HD, 2 * HD), 2 * HD)] = got.astype(BF)

    def attend_back(seg):
        at, keys = (s0, own) if seg == 0 else (t1, own + slots)
        q_rows, k_rows = pl.ds(at, own), pl.ds(at, keys)

        @pl.loop(0, pairs)
        def _(j):
            col = lambda g: pl.ds(pl.multiple_of(g * nq + j * 2 * HD, 2 * HD), 2 * HD)
            q, k, v = qkv[q_rows, col(0)], qkv[k_rows, col(1)], qkv[k_rows, col(2)]
            d = dmix[q_rows, pl.ds(pl.multiple_of(j * 2 * HD, 2 * HD), 2 * HD)]
            first_k, first_q = lanes(keys), lanes(own)
            dq = jnp.zeros((own, 2 * HD), F32)
            dk = jnp.zeros((keys, 2 * HD), F32)
            dv = jnp.zeros((keys, 2 * HD), F32)
            for h in range(2):
                pick_k, pick_q = first_k[h], first_q[h]
                p = probs[seg, 2 * j + h, :, pl.ds(0, keys)]
                pf = p.astype(F32)
                dp = dot_nt(d, v * pick_k)
                ds = (pf * (dp - jnp.sum(pf * dp, axis=1, keepdims=True))).astype(BF)
                dq += jnp.dot(ds, k * pick_k, preferred_element_type=F32)
                dk += dot_tn(ds, q * pick_q)
                dv += dot_tn(p, d * pick_q)
            dqkv[q_rows, col(0)] = (dq * scale).astype(BF)
            dqkv[k_rows, col(1)] = (dk * scale).astype(BF)
            dqkv[k_rows, col(2)] = dv.astype(BF)

    stays, gifts, passed = [], [], []

    def share_feats(src, dst, at, n):
        stays.append(local(src.at[pl.ds(at, n), :], dst.at[0, pl.ds(at, n), :]))
        landing = dst.at[1, pl.ds(at, n), my_cols]
        gifts.append((remote(src.at[pl.ds(at, n), my_cols], landing, at_p), landing))

    def pass_on():
        while gifts:
            copy, landing = gifts.pop(0)
            copy.wait()
            if landing is not None:
                passed.append(remote(landing, landing, at_core))

    def share_units(src, col, n, dst, dst_col, at, rn):
        mine = pl.ds(pl.multiple_of(col + zl * n, n), n)
        its = pl.ds(pl.multiple_of(col + (1 - zl) * n, n), n)
        to = pl.ds(dst_col, n)
        stays.append(local(src.at[pl.ds(at, rn), mine], dst.at[0, pl.ds(at, rn), to]))
        gifts.append((remote(src.at[pl.ds(at, rn), its], dst.at[1, pl.ds(at, rn), to], at_p), None))

    hq, hu = nq // 2, nu // 2

    def share_qkv(at, n):
        for g in range(3):
            share_units(dqkv, g * nq, hq, ra_hbm, g * hq, at, n)

    share_mix = lambda at, n: share_units(mix, 0, hq, rb_hbm, 0, at, n)
    share_db = lambda at, n: share_units(db, 0, hu, rb_hbm, hq, at, n)
    share_actv = lambda at, n: share_units(actv, 0, hu, rb_hbm, hq + hu, at, n)

    for copy in firsts:
        copy.wait()
    for copy in from_core:
        copy.wait()
    for copy, dst, at in from_x[:2]:
        copy.wait()
        block = dst.at[pl.ds(at + its_toks, toks), my_cols]
        forwards.append(remote(block, block, at_core))
    for copy in forwards:
        copy.wait()
    norm1(0, p0)
    share_feats(act1, la_hbm, 0, p0)
    for copy in weights[:3]:
        copy.wait()
    project(0, p0, 0, 3 * nq)
    forwards = []
    for copy, dst, at in from_x[2:]:
        copy.wait()
        block = dst.at[pl.ds(at + its_toks, toks), my_cols]
        forwards.append(remote(block, block, at_core))
    attend(0)
    share_mix(0, own)
    for copy in weights[3:4]:
        copy.wait()
    T = span
    a1 = Total(slots, 0, 0, whole(slots))
    a2 = Total(T, 2 * slots, 2 * slots, whole(T))
    a1.start(out_product(s0, slots))
    a2.start(out_product(t0, T))
    a1.middle()
    a2.middle()
    for copy in forwards + laters + late_core:
        copy.wait()
    gd[pl.ds(s1, slots), :] = (dsum[pl.ds(slots, slots), :].astype(F32) * row_live).astype(BF)
    share_feats(gd, lx_hbm.at[2], t0, p0 - t0)
    a1.finish()
    a1.done()
    enter_ffn(a1, s0, slots)
    weights[4].wait()
    ffn(s0, slots, False)
    weights[5].wait()
    a3 = Total(slots, slots, slots, whole(slots))
    a3.start(down_product(s0, slots))
    a2.finish()
    a3.middle()
    a2.done()
    enter_ffn(a2, t0, T)
    outacc[0] = mid[pl.ds(t0 + my_toks, toks), my_cols]
    a3.finish()
    share_feats(act2, lx_hbm.at[1], s0, own)
    a3.done()

    def summary(i):
        r = pl.ds(pl.multiple_of(s0 + i * step, step), step)
        f = pl.ds(pl.multiple_of(a3.full + i * step, step), step)
        p = pl.ds(pl.multiple_of(p0 + i * step, step), step)
        x = mid[r, :] + ar_full[f, :].astype(F32) + vec[5:6, :]
        on = (lax.broadcasted_iota(jnp.int32, (step, 1), 0) + i * step < live_count).astype(F32)
        rows[p, :] = (x * on).astype(BF)

    pl.loop(0, slots // step)(summary)
    sum_out[0] = rows[pl.ds(p0, slots), my_cols]
    norm1(p0, slots)
    share_feats(act1, la_hbm, p0, slots)
    project(p0, slots, nq, 3 * nq)
    attend(1)
    share_mix(t1, own)
    a5 = Total(own, 2 * slots + T, 2 * slots + T, whole(own))
    a5.start(out_product(t1, own))
    ffn(t0, T, True)
    share_actv(s0, own)
    share_db(t0, T)
    a5.middle()
    a6 = Total(T, 2 * slots, 2 * slots, whole(T))
    a6.start(up_back(t0, T))
    a6.middle()
    a5.finish()
    a4 = Total(T, 2 * slots + T + 2 * own, None, [(0, T, True)], 0)
    a4.start(down_product(t0, T))
    a5.done()
    enter_ffn(a5, t1, own)
    outacc[1] = mid[pl.ds(t1 + my_toks, toks), my_cols]
    outacc[2] = mid[pl.ds(s1, slots), my_cols]
    share_feats(act2, lx_hbm.at[1], t1, own)
    ffn(t1, own, True)
    share_actv(t1, own)
    share_db(t1, own)
    a8 = Total(own, 2 * slots + T + own, 2 * slots + T + own, whole(own))
    a8.start(up_back(t1, own))
    a6.finish()
    a4.middle()
    a8.middle()
    a7 = Total(own, 2 * slots + 2 * T + 2 * own, None, [(0, T, True), (T, slots, False)], T)
    a7.start(down_product(t1, own))
    a7.middle()
    a6.done()
    leave_ffn(a6, t0, T)
    mix_back(t0, T)
    share_feats(gm, lx_hbm.at[0], t0, T)
    a8.finish()
    for copy in a4.xs:
        copy.wait()
    hid_out[0] = (outacc[0] + a4.sums(0, T, True) + vec[5:6, my_cols]).astype(BF)
    a8.done()
    leave_ffn(a8, t1, own)
    mix_back(t1, own)
    share_feats(gm, lx_hbm.at[0], t1, own)
    attend_back(1)
    share_qkv(t1, own + slots)
    a9 = Total(slots, 0, 0, whole(slots))
    a9.start(in_back(p0, slots, nq))
    a10 = Total(own, 2 * slots + T, 2 * slots + T, [(0, T, True), (T, slots, False)])
    a9.middle()
    a10.start(in_back(t1, own, 0))
    a9.finish()
    a10.middle()
    for copy in a7.xs:
        copy.wait()
    hid_out[1] = (outacc[1] + a7.sums(0, T, True) + vec[5:6, my_cols]).astype(BF)
    sum_out[1] = (
        (outacc[2] + a7.sums(T, slots, False) + vec[5:6, my_cols]) * row_live
    ).astype(BF)
    a9.done()
    first_only = (s == 0).astype(F32)

    def norm1_back(r, f, weight):
        d = ar_full[f, :].astype(F32)
        xhat = (rows[r, :].astype(F32) - stat[r, 0:1]) * stat[r, 1:2]
        gsum[pl.ds(0, 8), :] = gsum[pl.ds(0, 8), :] + fold(d * xhat) * weight
        gsum[pl.ds(8, 8), :] = gsum[pl.ds(8, 8), :] + fold(d) * weight
        return norm_back(d, xhat, stat[r, 1:2], vec[0:1, :])

    def prefix_back(i):
        r = pl.ds(pl.multiple_of(p0 + i * step, step), step)
        f = pl.ds(pl.multiple_of(a9.full + i * step, step), step)
        g = pl.ds(pl.multiple_of(s0 + i * step, step), step)
        on = (lax.broadcasted_iota(jnp.int32, (step, 1), 0) + i * step < live_count).astype(F32)
        d = norm1_back(r, f, first_only)
        gd[g, :] = ((dsum[pl.ds(pl.multiple_of(i * step, step), step), :].astype(F32) + d) * on).astype(BF)

    pl.loop(0, slots // step)(prefix_back)
    share_feats(gd, lx_hbm.at[2], s0, slots)

    def last_before(c):
        cols = pl.ds(c, wide)
        r = pl.ds(s0, slots)
        db[r, cols] = (slope0[:, cols] * dot_nt(gd[r, :], wd[cols, :])).astype(BF)

    col_loop(nu, last_before)
    share_db(s0, slots)
    a11 = Total(slots, slots, slots, whole(slots))
    a11.start(up_back(s0, slots))
    a10.finish()
    a11.middle()
    a10.done()

    def rows_back(total, seg):
        t_at, s_at = (t0, s0) if seg == 0 else (t1, s1)
        t_in, s_in = (slots, 0) if seg == 0 else (0, span)

        def tokens(i):
            r = pl.ds(pl.multiple_of(t_at + my_toks + i * step, step), step)
            f = pl.ds(pl.multiple_of(total.full + t_in + i * step, step), step)
            x = norm1_back(r, f, 1.0)
            mid[r, :] = mid[r, :] + x

        pl.loop(0, toks // step)(tokens)
        gin_out[seg] = mid[pl.ds(t_at + my_toks, toks), my_cols]

        def summaries(i):
            r = pl.ds(pl.multiple_of(s_at + i * step, step), step)
            f = pl.ds(pl.multiple_of(total.full + s_in + i * step, step), step)
            x = norm1_back(r, f, first_only) + mid[r, :]
            e = pl.ds(pl.multiple_of(i * step, step), step)
            emb_wide[e, :] = x if seg == 1 else emb_wide[e, :] + x

        pl.loop(0, slots // step)(summaries)

    emb_wide = slope0
    rows_back(a10, 1)
    a11.finish()
    a11.done()
    leave_ffn(a11, s0, slots)
    mix_back(s0, slots)
    share_feats(gm, lx_hbm.at[0], s0, slots)
    attend_back(0)
    share_qkv(0, own)
    a12 = Total(own, 2 * slots + T + own, 2 * slots + T + own, [(0, slots, False), (slots, T, True)])
    a12.start(in_back(s0, own, 0))
    a12.middle()
    ones = jnp.ones((8, p0), BF)
    column = lambda ref, cols: jnp.dot(ones, ref[pl.ds(0, p0), cols], preferred_element_type=F32)[0:1, :]
    base = slots
    small_out[base + 2 : base + 3, :] = column(gm, my_quarter)
    small_out[base + 5 : base + 6, :] = column(gd, my_quarter)
    small_out[base + 3 : base + 4, :] = jnp.sum(fsum[pl.ds(0, 8), my_quarter], axis=0, keepdims=True)
    small_out[base + 4 : base + 5, :] = jnp.sum(fsum[pl.ds(8, 8), my_quarter], axis=0, keepdims=True)
    small_out[base + 6 : base + 7, :] = column(dqkv, pl.ds(0, nq))
    small_out[base + 7 : base + 8, :] = column(dqkv, pl.ds(2 * nq, nq)) + jnp.sum(
        dqkv[pl.ds(p0, slots), pl.ds(2 * nq, nq)].astype(F32), axis=0, keepdims=True
    )
    for k in range(nu // quarter):
        small_out[base + 8 + k : base + 9 + k, :] = column(db, pl.ds(k * quarter, quarter))
    small_out[base + 12 : base + 16, :] = jnp.zeros((4, quarter), F32)
    pass_on()
    a12.finish()
    a12.done()
    rows_back(a12, 0)
    small_out[pl.ds(0, slots), :] = emb_wide[:, my_quarter]
    its_quarter = pl.ds(pl.multiple_of(t * half + (1 - s) * quarter, quarter), quarter)
    gx_send[0:1, :] = jnp.sum(gsum[pl.ds(0, 8), its_quarter], axis=0, keepdims=True)
    gx_send[1:2, :] = jnp.sum(gsum[pl.ds(8, 8), its_quarter], axis=0, keepdims=True)
    gx_send[2:8, :] = jnp.zeros((6, quarter), F32)
    copy = remote(gx_send, gx_recv, at_x)
    copy.wait()
    small_out[base : base + 1, :] = gx_recv[0:1, :] + jnp.sum(gsum[pl.ds(0, 8), my_quarter], axis=0, keepdims=True)
    small_out[base + 1 : base + 2, :] = gx_recv[1:2, :] + jnp.sum(gsum[pl.ds(8, 8), my_quarter], axis=0, keepdims=True)
    for copy in stays + passed:
        copy.wait()

def chain(count, vecu, hid, dhid, emb, dsum, vec, wq, wk, wv, wo, wu, wd):
    toks, slots = hid.shape[1], emb.shape[0]
    half = hid.shape[2]
    feats, quarter = 2 * half, half // 2
    nq, nu = wo.shape[0] // 2, wd.shape[0] // 2
    own = 2 * toks + slots
    main, end = 2 * own, 2 * own + slots
    sums = 2 * slots + 2 * toks + 2 * own
    vm = pltpu.VMEM
    sds = jax.ShapeDtypeStruct
    dma = pltpu.SemaphoreType.DMA
    scratch = [
        vm((feats, 3 * nq), BF),
        vm((nq, feats), BF),
        vm((feats, nu), BF),
        vm((nu, feats), BF),
        vm((end, feats), BF),
        vm((end, feats), BF),
        vm((end, 3 * nq), BF),
        vm((2, nq // HD, own, own + slots), BF),
        vm((main, nq), BF),
        vm((main, feats), F32),
        vm((main, feats), BF),
        vm((main, nu), BF),
        vm((main, nu), BF),
        vm((slots, nu), F32),
        vm((main, feats), BF),
        vm((main, feats), BF),
        vm((main, nq), BF),
        vm((end, 3 * nq), BF),
        vm((2 * slots, feats), BF),
        vm((8, feats), F32),
        vm((1, 3 * nq + nu), F32),
        vm((end, 128), F32),
        vm((3, toks, half), F32),
        vm((16, feats), F32),
        vm((16, feats), F32),
        vm((8, quarter), F32),
        vm((8, quarter), F32),
        vm((sums + 2 * toks + own, half), BF),
        vm((sums + 2 * toks + own, half), BF),
        vm((sums + 2 * toks + own, half), BF),
        vm((sums, feats), BF),
        vm((2 * toks + own, half), BF),
        dma((6,)),
        dma((48,)),
        dma((128, 2)),
    ]
    vmem = pl.BlockSpec(memory_space=pltpu.VMEM)
    hbm = pl.BlockSpec(memory_space=pl.ANY)
    smem = pl.BlockSpec(memory_space=pltpu.SMEM)
    return pl.pallas_call(
        chain_kernel,
        name="chain",
        out_shape=(
            sds((2, toks, half), BF),
            sds((2, slots, half), BF),
            sds((2, toks, half), F32),
            sds((slots + 16, quarter), F32),
            sds((2, end, feats), BF),
            sds((3, 2, main, feats), BF),
            sds((2, end, 3 * nq // 2), BF),
            sds((2, main, nq // 2 + nu), BF),
        ),
        in_specs=[smem, vmem] + [hbm] * 11,
        out_specs=(vmem,) * 4 + (hbm,) * 4,
        scratch_shapes=scratch,
        compiler_params=pltpu.CompilerParams(
            collective_id=2, has_side_effects=True, vmem_limit_bytes=62 * 2**20
        ),
    )(count, vecu, hid, dhid, emb, dsum, vec, wq, wk, wv, wo, wu, wd)


def local(
    hidden_in, summary_counts, summary_embed, ln1_gain, ln1_bias, w_query, b_query, w_key, w_value,
    b_value, w_out, b_out, ln2_gain, ln2_bias, w_up, b_up, w_down, b_down, d_hidden, d_summary,
):
    n = summary_embed.shape[0]
    pad = -n % 64
    emb = jnp.pad(summary_embed, ((0, pad), (0, 0)))
    dsum = jnp.pad(d_summary[0], ((0, 0), (0, pad), (0, 0))).reshape(-1, d_summary.shape[3])
    zero = jnp.zeros_like(ln1_gain)
    vec = jnp.stack([ln1_gain, ln1_bias, ln2_gain, ln2_bias, b_out, b_down, zero, zero]).astype(F32)
    vecu = jnp.concatenate([b_query, b_value, b_up]).astype(F32)[None]
    nq, nu = w_query.shape[1] // 2, w_up.shape[1] // 2
    hid, summaries, gin, small, la, lx, ra, rb = chain(
        summary_counts, vecu, hidden_in[0], d_hidden[0], emb, dsum, vec,
        w_query, w_key, w_value, w_out, w_up, w_down,
    )
    flat = lambda x: x.reshape(x.shape[:-3] + (-1, x.shape[-1]))
    width = nq // 2
    w, sm = reduce_grads(flat(la), flat(lx), flat(ra), flat(rb), small, width)

    def place(lo, hi):
        x = w[lo:hi]
        return x.transpose(3, 1, 2, 0, 4).reshape(x.shape[3], -1)

    per = nu // 2 // width
    gq, gk, gv, go = (place(i, i + 1) for i in range(4))
    gu, gdn = place(4, 4 + per), place(4 + per, 4 + 2 * per)
    sm = sm.transpose(1, 0, 2)
    at = n + pad
    fl = lambda r: sm[at + r].reshape(-1)
    bup = sm[at + 8 : at + 8 + nu // sm.shape[2]].transpose(1, 0, 2).reshape(-1)
    return (
        hid[None], summaries[None, :, :n], gin[None],
        sm[:n].reshape(n, -1), fl(0), fl(1), gq, fl(6), gk, gv, fl(7), go.T, fl(2),
        fl(3), fl(4), gu, bup, gdn.T, fl(5),
    )


def solution(mesh):
    return jax.shard_map(
        local,
        mesh=mesh,
        in_specs=(
            P("batch", None, "seq", "tensor"),
            P("batch"),
            P(None, "tensor"),
            P("tensor"),
            P("tensor"),
            P(None, "tensor"),
            P("tensor"),
            P(None, "tensor"),
            P(None, "tensor"),
            P("tensor"),
            P("tensor", None),
            P("tensor"),
            P("tensor"),
            P("tensor"),
            P(None, "tensor"),
            P("tensor"),
            P("tensor", None),
            P("tensor"),
            P("batch", None, "seq", "tensor"),
            P("batch", None, None, "tensor"),
        ),
        out_specs=(
            P("batch", None, "seq", "tensor"),
            P("batch", None, None, "tensor"),
            P("batch", None, "seq", "tensor"),
            P(None, "tensor"),
            P("tensor"),
            P("tensor"),
            P(("batch", "seq"), "tensor"),
            P("tensor"),
            P(("batch", "seq"), "tensor"),
            P(("batch", "seq"), "tensor"),
            P("tensor"),
            P("tensor", ("batch", "seq")),
            P("tensor"),
            P("tensor"),
            P("tensor"),
            P(("batch", "seq"), "tensor"),
            P("tensor"),
            P("tensor", ("batch", "seq")),
            P("tensor"),
        ),
        check_vma=False,
    )
```

```python
import functools

import jax
import jax.numpy as jnp
from jax import lax
from jax.experimental import pallas as pl
from jax.experimental.pallas import tpu as pltpu
from jax.sharding import PartitionSpec as P

HD = 64
EPSILON = 1e-05
NEGATIVE = -1e30
MESH = pl.DeviceIdType.MESH
BF = jnp.bfloat16
F32 = jnp.float32
PAIR_BIT = 1


def flip(index, bit):
    weight = 1 << bit
    return index + weight - 2 * weight * lax.rem(index // weight, 2)


def bit_of(index, bit):
    return lax.rem(index // (1 << bit), 2)


def dot_nt(a, b):
    return lax.dot_general(a, b, (((1,), (1,)), ((), ())), preferred_element_type=F32)


def dot_tn(a, b):
    return lax.dot_general(a, b, (((0,), (0,)), ((), ())), preferred_element_type=F32)


def dot_nt(a, b):
    return lax.dot_general(a, b, (((1,), (1,)), ((), ())), preferred_element_type=F32)


def dot_tn(a, b):
    return lax.dot_general(a, b, (((0,), (0,)), ((), ())), preferred_element_type=F32)


def grads_kernel(
    bits,
    tiles,
    width,
    la_ref,
    lx_ref,
    ra_ref,
    rb_ref,
    small_ref,
    gq_ref,
    gk_ref,
    gv_ref,
    go_ref,
    gu_ref,
    gd_ref,
    emb_ref,
    vec_refs,
    bup_ref,
    send0,
    recv0,
    keep0,
    both,
    sends,
    recvs,
    keeps,
    send_p,
    recv_p,
    keep_p,
    send_x,
    recv_x,
    small_cur,
    small_recv,
    sem0,
    sems,
    sem_p,
    sem_x,
    sem_s,
):
    b, s, t = lax.axis_index("batch"), lax.axis_index("seq"), lax.axis_index("tensor")
    halving = list(range(bits - 1, PAIR_BIT, -1))
    at_y = (flip(b, 0), s, t)
    at_p = (flip(b, PAIR_BIT), s, t)
    at_x = (b, 1 - s, t)
    at_h = [(flip(b, bit), s, t) for bit in halving]
    partners = [at_y, at_p, at_x] + at_h
    barrier = pltpu.get_barrier_semaphore()
    for partner in partners:
        pl.semaphore_signal(barrier, inc=1, device_id=partner, device_id_type=MESH)
    pl.semaphore_wait(barrier, len(partners))

    features = la_ref.shape[1]
    inner = ra_ref.shape[1] // width
    chunk = features // (1 << bits)
    half_count = 1 << (bits - 1)
    mine = bit_of(b, 0)

    def remote(src, dst, sem, partner):
        return pltpu.make_async_remote_copy(
            src_ref=src,
            dst_ref=dst,
            send_sem=sem.at[0],
            recv_sem=sem.at[1],
            device_id=partner,
            device_id_type=MESH,
        )

    def copy_y(i):
        return remote(send0.at[i], recv0.at[i], sem0.at[i], at_y)

    def copy_h(k, i):
        return remote(sends[k].at[i], recvs[k].at[i], sems[k].at[i], at_h[k])

    def copy_p(i):
        return remote(send_p.at[i], recv_p.at[i], sem_p.at[i], at_p)

    def copy_x(i):
        return remote(send_x.at[i], recv_x.at[i], sem_x.at[i], at_x)

    per = (tiles - inner - 1) // 2

    def product(i, side, put):
        def blocks(left, right):
            @pl.loop(0, half_count)
            def _(j):
                at = pl.ds(pl.multiple_of(j * chunk, chunk), chunk)
                if chunk % 128 == 0:
                    start = pl.multiple_of((2 * j + side) * chunk, chunk)
                    put(at, dot_tn(left(pl.ds(start, chunk)), right))
                else:
                    start = pl.multiple_of(2 * j * chunk, 2 * chunk)
                    both[...] = dot_tn(left(pl.ds(start, 2 * chunk)), right)
                    put(at, both[pl.ds(pl.multiple_of(side * chunk, chunk), chunk), :])

        @pl.when(i < inner)
        def _():
            cols = pl.ds(pl.multiple_of(i * width, width), width)
            blocks(lambda at: la_ref[:, at], ra_ref[:, cols])

        @pl.when(i >= inner)
        def _():
            k = i - inner
            cols = pl.ds(pl.multiple_of(k * width, width), width)
            op = (k + per - 1) // per
            blocks(lambda at: lx_ref[op, :, at], rb_ref[:, cols])

    small_cur[...] = small_ref[...]
    small_partners = [at_y] + at_h + [at_p]
    for k, partner in enumerate(small_partners):
        copy = remote(small_cur, small_recv.at[k], sem_s.at[k], partner)
        copy.start()

        if k == 0:

            @pl.loop(0, tiles)
            def _(i):
                def put(at, value):
                    send0[i, at, :] = value.astype(BF)

                product(i, 1 - mine, put)
                copy_y(i).start()

        copy.wait()
        small_cur[...] = small_cur[...] + small_recv[k]
    last = len(small_partners)
    copy = remote(small_cur, small_recv.at[last], sem_s.at[last], at_x)
    copy.start()
    copy.wait()
    used = emb_ref.shape[0]
    quarter = small_ref.shape[1]
    base = small_ref.shape[0] - 16
    for side, ref in ((s, small_cur), (1 - s, small_recv.at[last])):
        at = pl.ds(pl.multiple_of(side * quarter, quarter), quarter)
        emb_ref[:, at] = ref[pl.ds(0, used), :]
        for k, out in enumerate(vec_refs):
            out[:, at] = ref[base + k : base + k + 1, :]
        pieces = bup_ref.shape[1] // (2 * quarter)
        for k in range(pieces):
            at = pl.ds(pl.multiple_of((side * pieces + k) * quarter, quarter), quarter)
            bup_ref[:, at] = ref[base + 8 + k : base + 9 + k, :]

    stages = len(halving)

    def split(i, k, total, rows):
        bit = bit_of(b, halving[k])
        half = rows // 2
        keeps[k][i] = total(pl.multiple_of(bit * half, half), half)
        sends[k][i] = total(pl.multiple_of((1 - bit) * half, half), half).astype(BF)
        copy_h(k, i).start()

    def stage_first(i):
        copy_y(i).wait()

        def put(at, value):
            keep0[at, :] = value + recv0[i, at, :].astype(F32)

        product(i, mine, put)
        split(i, 0, lambda at, n: keep0[pl.ds(at, n), :], half_count * chunk)

    def stage_next(k, i):
        copy_h(k, i).wait()

        def total(at, n):
            return keeps[k][i, pl.ds(at, n), :] + recvs[k][i, pl.ds(at, n), :].astype(F32)

        rows = (half_count * chunk) >> (k + 1)
        if k + 1 < stages:
            split(i, k + 1, total, rows)
        else:
            bit = bit_of(b, PAIR_BIT)
            keep_p[i] = total(pl.multiple_of(bit * chunk, chunk), chunk)
            send_p[i] = total(pl.multiple_of((1 - bit) * chunk, chunk), chunk).astype(BF)
            copy_p(i).start()

    def write(i, side, pair, value):
        spot = pl.ds(pl.multiple_of((2 * side + pair) * width, width), width)
        for k, ref in enumerate((gq_ref, gk_ref, gv_ref)):

            @pl.when(i == k)
            def _():
                ref[:, spot] = value

        @pl.when(i == inner)
        def _():
            go_ref[spot, :] = value.T

        def unit(k):
            return pl.ds(pl.multiple_of(((2 * side + pair) * per + k) * width, width), width)

        @pl.when((i > inner) & (i <= inner + per))
        def _():
            gu_ref[:, unit(i - inner - 1)] = value

        @pl.when(i > inner + per)
        def _():
            gd_ref[unit(i - inner - 1 - per), :] = value.T

    def stage_pair(i):
        copy_p(i).wait()
        bit = bit_of(b, PAIR_BIT)
        half = chunk // 2
        mine_at = pl.multiple_of(s * half, half)
        other_at = pl.multiple_of((1 - s) * half, half)
        write(i, s, bit, keep_p[i, pl.ds(mine_at, half), :])
        write(i, s, 1 - bit, recv_p[i, pl.ds(mine_at, half), :].astype(F32))
        send_x[i, bit] = keep_p[i, pl.ds(other_at, half), :].astype(BF)
        send_x[i, 1 - bit] = recv_p[i, pl.ds(other_at, half), :]
        copy_x(i).start()

    def stage_last(i):
        copy_x(i).wait()
        for pair in range(2):
            write(i, 1 - s, pair, recv_x[i, pair].astype(F32))

    @pl.loop(0, tiles + stages + 2)
    def _(i):
        @pl.when(i < tiles)
        def _():
            stage_first(i)

        for k in range(stages):

            @pl.when((i >= k + 1) & (i < tiles + k + 1))
            def _():
                stage_next(k, i - (k + 1))

        @pl.when((i >= stages + 1) & (i < tiles + stages + 1))
        def _():
            stage_pair(i - (stages + 1))

        @pl.when(i >= stages + 2)
        def _():
            stage_last(i - (stages + 2))


class Strips:
    def __init__(self, refs, width):
        self.width = width
        self.free = [[ref, ref.shape[0], at, 0] for ref in refs for at in range(ref.shape[1] // width)]

    def take(self, tiles, n, unit):
        for k, (ref, height, at, used) in enumerate(self.free):
            if height < n:
                continue
            if used + tiles * n <= height:
                self.free[k][3] += tiles * n
                return Slab(ref, at, used, tiles, n, unit, self.width)
            per = height // n
            need = -(-tiles // per)
            run = self.free[k : k + need]
            if len(run) == need and all(r[0] is ref and r[3] == 0 for r in run):
                for r in run:
                    r[3] = height
                return Slab(ref, at, 0, per, n, unit, self.width)
        raise ValueError("no room")


class Slab:
    def __init__(self, ref, strip, start, per, n, unit, width):
        self.ref, self.strip, self.start, self.per = ref, strip, start, per
        self.n, self.unit, self.width = n, unit, width

    def at(self, i, lo, n):
        first = pl.multiple_of(self.start + (i % self.per) * self.n + lo, self.unit)
        col = pl.multiple_of((self.strip + i // self.per) * self.width, self.width)
        return self.ref.at[pl.ds(first, n), pl.ds(col, self.width)]

    def __call__(self, i):
        return self.at(i, 0, self.n)


def chain_kernel(
    bits,
    count_ref,
    emb_ref,
    dsum_ref,
    feat_refs,
    bq_ref,
    bv_ref,
    bu_ref,
    hid_hbm,
    dhid_hbm,
    wq_hbm,
    wk_hbm,
    wv_hbm,
    wo_hbm,
    wu_hbm,
    wd_hbm,
    hid_out,
    sum_out,
    gin_out,
    small_final,
    w_hbm,
    la_hbm,
    lm_hbm,
    ra_hbm,
    mx_hbm,
    wqkv,
    wo,
    wu,
    wd,
    rows,
    act1,
    qkv,
    probs,
    mix,
    mid,
    act2,
    actv,
    db,
    slope0,
    gd,
    gm,
    dmix,
    dqkv,
    dsum,
    vec,
    bias,
    stat,
    outacc,
    fsum,
    gsum,
    gx_send,
    gx_recv,
    ar_send,
    ar_core,
    ar_x,
    ar_full,
    ar_own,
    lxx,
    rbx,
    both,
    small_out,
    small_recv,
    wsem,
    lsem,
    rsem,
    free,
    sem_y,
    sem_za,
    sem_pa,
    sem_xa,
    sem_pb,
    sem_zb,
    sem_xb,
    sem_oa,
    sem_ob,
    sem_s,
):
    b, s, t = lax.axis_index("batch"), lax.axis_index("seq"), lax.axis_index("tensor")
    at_core = (b, s, 1 - t)
    at_x = (b, 1 - s, t)
    at_p = (flip(b, PAIR_BIT), s, t)
    at_y = (flip(b, 0), s, t)
    halving = list(range(bits - 1, PAIR_BIT, -1))
    at_h = [(flip(b, bit), s, t) for bit in halving]
    zl, y = bit_of(b, PAIR_BIT), bit_of(b, 0)
    barrier = pltpu.get_barrier_semaphore()
    partners = [at_core, at_x, at_p, at_y] + at_h
    for partner in partners:
        pl.semaphore_signal(barrier, inc=1, device_id=partner, device_id_type=MESH)

    toks = hid_hbm.shape[1]
    slots = slope0.shape[0]
    used = emb_ref.shape[0]
    feats = rows.shape[1]
    half = feats // 2
    quarter = feats // 4
    span = 2 * toks
    s0, t0, t1, s1, p0 = 0, slots, slots + span, slots + 2 * span, 2 * slots + 2 * span
    own = slots + span
    end = p0 + slots
    nq = wo.shape[0]
    nu = wu.shape[1]
    my_cols = pl.ds(pl.multiple_of(t * half, half), half)
    its_cols = pl.ds(pl.multiple_of((1 - t) * half, half), half)
    my_toks = pl.multiple_of(s * toks, toks)
    its_toks = pl.multiple_of((1 - s) * toks, toks)
    my_quarter = pl.ds(pl.multiple_of(t * half + s * quarter, quarter), quarter)

    counter = {"l": 0, "r": 0}

    def local(src, dst):
        counter["l"] += 1
        copy = pltpu.make_async_copy(src, dst, lsem.at[counter["l"] - 1])
        copy.start()
        return copy

    def remote(src, dst, partner):
        counter["r"] += 1
        at = counter["r"] - 1
        copy = pltpu.make_async_remote_copy(
            src_ref=src,
            dst_ref=dst,
            send_sem=rsem.at[at, 0],
            recv_sem=rsem.at[at, 1],
            device_id=partner,
            device_id_type=MESH,
        )
        copy.start()
        return copy

    part = lambda ref, n, axis: (
        ref.at[:, pl.ds(pl.multiple_of(s * n, n), n)]
        if axis
        else ref.at[pl.ds(pl.multiple_of(s * n, n), n), :]
    )
    weights = []
    for at, (src, dst) in enumerate(
        (
            (part(wq_hbm, nq, 1), wqkv.at[:, pl.ds(0, nq)]),
            (part(wk_hbm, nq, 1), wqkv.at[:, pl.ds(nq, nq)]),
            (part(wv_hbm, nq, 1), wqkv.at[:, pl.ds(2 * nq, nq)]),
            (part(wo_hbm, nq, 0), wo),
            (part(wu_hbm, nu, 1), wu),
            (part(wd_hbm, nu, 0), wd),
        )
    ):
        copy = pltpu.make_async_copy(src, dst, wsem.at[at])
        weights.append(copy)

    firsts = []
    for seg, at in enumerate((t0, t1)):
        firsts.append(local(hid_hbm.at[seg], rows.at[pl.ds(at + my_toks, toks), my_cols]))
    laters = []
    for seg, at in enumerate((t0, t1)):
        laters.append(local(dhid_hbm.at[seg], gd.at[pl.ds(at + my_toks, toks), my_cols]))
    for copy in weights[:3]:
        copy.start()
    for at in (s0, s1):
        rows[pl.ds(at, slots), my_cols] = jnp.zeros((slots, half), BF)
        rows[pl.ds(at, used), my_cols] = emb_ref[...]
    for seg in range(2):
        dsum[pl.ds(seg * slots, slots), my_cols] = jnp.zeros((slots, half), BF)
        dsum[pl.ds(seg * slots, used), my_cols] = dsum_ref[0, seg]
    for k, ref in enumerate(feat_refs):
        vec[k : k + 1, my_cols] = ref[...].astype(F32)[None]
    pl.semaphore_wait(barrier, len(partners))

    from_x, from_core, forwards = [], [], []
    for src, dst, at in (
        (hid_hbm.at[0], rows, t0),
        (hid_hbm.at[1], rows, t1),
        (dhid_hbm.at[0], gd, t0),
        (dhid_hbm.at[1], gd, t1),
    ):
        block = dst.at[pl.ds(at + my_toks, toks), my_cols]
        from_x.append((remote(src, block, at_x), dst, at))
    for block in (
        rows.at[pl.ds(s0, slots), my_cols],
        rows.at[pl.ds(s1, slots), my_cols],
        vec.at[:, my_cols],
    ):
        from_core.append(remote(block, block, at_core))
    for src, dst, at in ((hid_hbm.at[0], rows, t0), (hid_hbm.at[1], rows, t1)):
        from_core.append(remote(src, dst.at[pl.ds(at + my_toks, toks), my_cols], at_core))
    late_core = [remote(dsum.at[:, my_cols], dsum.at[:, my_cols], at_core)]
    for src, dst, at in ((dhid_hbm.at[0], gd, t0), (dhid_hbm.at[1], gd, t1)):
        late_core.append(remote(src, dst.at[pl.ds(at + my_toks, toks), my_cols], at_core))
    for copy in weights[3:]:
        copy.start()

    live_count = count_ref[0]
    row_live = (lax.broadcasted_iota(jnp.int32, (slots, 1), 0) < live_count).astype(F32)
    dqkv[pl.ds(p0, slots), pl.ds(0, nq)] = jnp.zeros((slots, nq), BF)
    bias[:, pl.ds(nq, nq)] = jnp.zeros((1, nq), F32)
    for ref, at, n in ((bq_ref, 0, nq), (bv_ref, 2 * nq, nq), (bu_ref, 3 * nq, nu)):
        x = ref[...].astype(F32)[None]
        bias[:, pl.ds(at, n)] = jnp.where(s == 0, x[:, :n], x[:, n:])
    fsum[...] = jnp.zeros_like(fsum)
    gsum[...] = jnp.zeros_like(gsum)

    step = 16
    inverse = 1.0 / feats

    def row_loop(start, n, body):
        @pl.loop(0, n // step)
        def _(i):
            body(pl.ds(pl.multiple_of(start + i * step, step), step))

    def mean(x):
        return jnp.sum(x, axis=1, keepdims=True) * inverse

    def stats(x):
        m = mean(x)
        return m, lax.rsqrt(mean(x * x) - m * m + EPSILON)

    def norm1(start, n):
        def body(at):
            x = rows[at, :].astype(F32)
            m, r = stats(x)
            act1[at, :] = ((x - m) * r * vec[0:1, :] + vec[1:2, :]).astype(BF)
            stat[at, 0:1] = m
            stat[at, 1:2] = r

        row_loop(start, n, body)

    def norm_back(d, xhat, r, gain):
        q = d * gain
        return r * (q - mean(q) - xhat * mean(q * xhat))

    def fold(x):
        return jnp.sum(x.reshape(step // 8, 8, x.shape[1]), axis=0)

    wide = 512

    def col_loop(n, body):
        @pl.loop(0, n // wide)
        def _(j):
            body(pl.multiple_of(j * wide, wide))

    def project(at, n, lo, hi):
        def body(c):
            cols = pl.ds(pl.multiple_of(lo + c, wide), wide)
            x = jnp.dot(act1[pl.ds(at, n), :], wqkv[:, cols], preferred_element_type=F32)
            qkv[pl.ds(at, n), cols] = (x + bias[:, cols]).astype(BF)

        col_loop(hi - lo, body)

    class Total:
        def __init__(self, n, at, full, pieces, own_at=0):
            self.n, self.at, self.full, self.own_at = n, at, full, own_at
            self.pieces = pieces

        def mine(self, r, n):
            if self.full is None:
                return ar_own.at[pl.ds(self.own_at + r, n), :]
            return ar_full.at[pl.ds(self.full + r, n), my_cols]

        def start(self, product):
            at = pl.ds(self.at, self.n)

            def other(c):
                x = product(pl.multiple_of((1 - t) * half + c, wide), wide)
                ar_send[at, pl.ds(c, wide)] = x.astype(BF)

            col_loop(half, other)
            self.core = remote(ar_send.at[at, :], ar_core.at[at, :], at_core)

            def this(c):
                x = product(pl.multiple_of(t * half + c, wide), wide)
                if self.full is None:
                    ar_own[pl.ds(self.own_at, self.n), pl.ds(c, wide)] = x.astype(BF)
                else:
                    cols = pl.ds(pl.multiple_of(t * half + c, wide), wide)
                    ar_full[pl.ds(self.full, self.n), cols] = x.astype(BF)

            col_loop(half, this)

        def middle(self):
            self.core.wait()
            self.xs = []
            for base, n, scatter in self.pieces:
                at = pl.ds(self.at + base, n)
                ar_core[at, :] = (
                    self.mine(base, n)[...].astype(F32) + ar_core[at, :].astype(F32)
                ).astype(BF)
                if scatter:
                    src = ar_core.at[pl.ds(self.at + base + its_toks, toks), :]
                    dst = ar_x.at[pl.ds(self.at + base, toks), :]
                else:
                    src, dst = ar_core.at[at, :], ar_x.at[at, :]
                self.xs.append(remote(src, dst, at_x))

        def sums(self, base, n, scatter):
            if scatter:
                near = ar_core[pl.ds(self.at + base + my_toks, toks), :]
                far = ar_x[pl.ds(self.at + base, toks), :]
            else:
                near = ar_core[pl.ds(self.at + base, n), :]
                far = ar_x[pl.ds(self.at + base, n), :]
            return near.astype(F32) + far.astype(F32)

        def finish(self):
            self.backs = []
            for (base, n, scatter), copy in zip(self.pieces, self.xs):
                copy.wait()
                n = toks if scatter else n
                block = ar_full.at[pl.ds(self.full + base, n), my_cols]
                block[...] = self.sums(base, n, scatter).astype(BF)
                self.backs.append(remote(block, block, at_core))

        def done(self):
            for copy in self.backs:
                copy.wait()

    whole = lambda n: [(i, 64, False) for i in range(0, n, 64)]

    def out_product(at, n):
        return lambda c, w: jnp.dot(
            mix[pl.ds(at, n), :], wo[:, pl.ds(c, w)], preferred_element_type=F32
        )

    def down_product(at, n):
        return lambda c, w: jnp.dot(
            actv[pl.ds(at, n), :], wd[:, pl.ds(c, w)], preferred_element_type=F32
        )

    def up_back(at, n):
        return lambda c, w: dot_nt(db[pl.ds(at, n), :], wu[pl.ds(c, w), :])

    def in_back(at, n, lo):
        return lambda c, w: dot_nt(
            dqkv[pl.ds(at, n), pl.ds(lo, 3 * nq - lo)], wqkv[pl.ds(c, w), pl.ds(lo, 3 * nq - lo)]
        )

    def enter_ffn(total, at, n):
        def body(i):
            r = pl.ds(pl.multiple_of(at + i * step, step), step)
            f = pl.ds(pl.multiple_of(total.full + i * step, step), step)
            x = rows[r, :].astype(F32) + ar_full[f, :].astype(F32) + vec[4:5, :]
            m, rs = stats(x)
            mid[r, :] = x
            act2[r, :] = ((x - m) * rs * vec[2:3, :] + vec[3:4, :]).astype(BF)
            stat[r, 2:3] = m
            stat[r, 3:4] = rs

        pl.loop(0, n // step)(body)

    def gelu(v):
        c = 0.7978845608028654
        th = jnp.tanh(c * (v + 0.044715 * (v * v * v)))
        act = 0.5 * v * (1.0 + th)
        sl = 0.5 * (1.0 + th) + (0.5 * c) * v * (1.0 - th * th) * (1.0 + (3 * 0.044715) * v * v)
        return act, sl

    def ffn(at, n, back):
        r = pl.ds(at, n)

        def body(c):
            cols = pl.ds(c, wide)
            v = jnp.dot(act2[r, :], wu[:, cols], preferred_element_type=F32)
            act, sl = gelu(v + bias[:, pl.ds(pl.multiple_of(3 * nq + c, wide), wide)])
            actv[r, cols] = act.astype(BF)
            if back:
                db[r, cols] = (sl * dot_nt(gd[r, :], wd[cols, :])).astype(BF)
            else:
                slope0[:, cols] = sl

        col_loop(nu, body)

    def leave_ffn(total, at, n):
        def body(i):
            r = pl.ds(pl.multiple_of(at + i * step, step), step)
            f = pl.ds(pl.multiple_of(total.full + i * step, step), step)
            d = ar_full[f, :].astype(F32)
            xhat = (mid[r, :] - stat[r, 2:3]) * stat[r, 3:4]
            fsum[pl.ds(0, 8), :] = fsum[pl.ds(0, 8), :] + fold(d * xhat)
            fsum[pl.ds(8, 8), :] = fsum[pl.ds(8, 8), :] + fold(d)
            dm = gd[r, :].astype(F32) + norm_back(d, xhat, stat[r, 3:4], vec[2:3, :])
            mid[r, :] = dm
            gm[r, :] = dm.astype(BF)

        pl.loop(0, n // step)(body)

    def mix_back(at, n):
        dmix[pl.ds(at, n), :] = dot_nt(gm[pl.ds(at, n), :], wo[...]).astype(BF)

    pairs = nq // (2 * HD)
    scale = HD**-0.5

    def seen(seg, keys):
        q = lax.broadcasted_iota(jnp.int32, (own, keys), 0)
        k = lax.broadcasted_iota(jnp.int32, (own, keys), 1)
        if seg == 0:
            q = jnp.where(q < slots, q + span, q - slots)
            slot = k
            token = k >= slots
            k = jnp.where(token, k - slots, k + span)
            return (k <= q) & (token | (slot < live_count))
        token = k < span
        ahead = k >= own
        slot = jnp.where(ahead, k - own, k - span)
        return (ahead | (k <= q)) & (token | (slot < live_count))

    def lanes(n):
        first = (lax.broadcasted_iota(jnp.int32, (n, 2 * HD), 1) < HD).astype(F32)
        return first.astype(BF), (1.0 - first).astype(BF)

    def attend(seg):
        at, keys = (s0, own) if seg == 0 else (t1, own + slots)
        q_rows, k_rows = pl.ds(at, own), pl.ds(at, keys)

        @pl.loop(0, pairs)
        def _(j):
            col = lambda g: pl.ds(pl.multiple_of(g * nq + j * 2 * HD, 2 * HD), 2 * HD)
            q, k, v = qkv[q_rows, col(0)], qkv[k_rows, col(1)], qkv[k_rows, col(2)]
            first = lanes(keys)
            allowed = seen(seg, keys)
            got = jnp.zeros((own, 2 * HD), F32)
            for h in range(2):
                pick = first[h]
                sc = dot_nt(q, k * pick) * scale
                sc = jnp.where(allowed, sc, NEGATIVE)
                e = jnp.exp(sc - jnp.max(sc, axis=1, keepdims=True))
                p = (e / jnp.sum(e, axis=1, keepdims=True)).astype(BF)
                probs[seg, 2 * j + h, :, pl.ds(0, keys)] = p
                got += jnp.dot(p, v * pick, preferred_element_type=F32)
            mix[q_rows, pl.ds(pl.multiple_of(j * 2 * HD, 2 * HD), 2 * HD)] = got.astype(BF)

    def attend_back(seg):
        at, keys = (s0, own) if seg == 0 else (t1, own + slots)
        q_rows, k_rows = pl.ds(at, own), pl.ds(at, keys)

        @pl.loop(0, pairs)
        def _(j):
            col = lambda g: pl.ds(pl.multiple_of(g * nq + j * 2 * HD, 2 * HD), 2 * HD)
            q, k, v = qkv[q_rows, col(0)], qkv[k_rows, col(1)], qkv[k_rows, col(2)]
            d = dmix[q_rows, pl.ds(pl.multiple_of(j * 2 * HD, 2 * HD), 2 * HD)]
            first_k, first_q = lanes(keys), lanes(own)
            dq = jnp.zeros((own, 2 * HD), F32)
            dk = jnp.zeros((keys, 2 * HD), F32)
            dv = jnp.zeros((keys, 2 * HD), F32)
            for h in range(2):
                pick_k, pick_q = first_k[h], first_q[h]
                p = probs[seg, 2 * j + h, :, pl.ds(0, keys)]
                pf = p.astype(F32)
                dp = dot_nt(d, v * pick_k)
                ds = (pf * (dp - jnp.sum(pf * dp, axis=1, keepdims=True))).astype(BF)
                dq += jnp.dot(ds, k * pick_k, preferred_element_type=F32)
                dk += dot_tn(ds, q * pick_q)
                dv += dot_tn(p, d * pick_q)
            dqkv[q_rows, col(0)] = (dq * scale).astype(BF)
            dqkv[k_rows, col(1)] = (dk * scale).astype(BF)
            dqkv[k_rows, col(2)] = dv.astype(BF)

    gifts_a, gifts_b, passed = [], [], []
    hu = nu // 2

    def share_feats_a(op, src, at, n):
        landing = lxx.at[op, pl.ds(at, n), my_cols]
        gifts_a.append((remote(src.at[pl.ds(at, n), my_cols], landing, at_p), landing))

    def share_units_a(src, col, at, n):
        its = pl.ds(pl.multiple_of((1 - zl) * hu, hu), hu)
        landing = rbx.at[pl.ds(at, n), pl.ds(col, hu)]
        gifts_a.append((remote(src.at[pl.ds(at, n), its], landing, at_p), None))

    def share_feats_b(src, dst, at, n):
        landing = dst.at[pl.ds(at, n), my_cols]
        gifts_b.append((remote(src.at[pl.ds(at, n), my_cols], landing, at_y), landing))

    def share_units_b(src, dst, at, n):
        gifts_b.append((remote(src.at[pl.ds(at, n), :], dst.at[pl.ds(at, n), :], at_y), None))

    def pass_on(gifts, most=1000):
        while gifts and most:
            most -= 1
            copy, landing = gifts.pop(0)
            copy.wait()
            if landing is not None:
                passed.append(remote(landing, landing, at_core))

    def pass_end():
        while passed:
            passed.pop(0).wait()

    share_qkv = lambda at, n: share_units_b(dqkv, ra_hbm, at, n)
    share_mix = lambda at, n: share_units_b(mix, mx_hbm, at, n)
    share_actv = lambda at, n: share_units_a(actv, 0, at, n)
    share_db = lambda at, n: share_units_a(db, hu, at, n)

    width = nq // 2
    chunk = feats >> bits
    near = chunk // 2
    chunks = 1 << (bits - 1)
    per = hu // width
    tiles_a, tiles_b = 2 * per, 4 * nq // width
    nh = len(halving)
    strips = Strips([wu, wd], width)
    recv_y = strips.take(tiles_a, chunks * chunk, near)
    send_y = strips.take(tiles_a, chunks * chunk, near)
    recv_za = [strips.take(tiles_a, chunks * chunk >> (k + 1), near) for k in range(nh)]
    recv_pb = strips.take(tiles_b, chunks * chunk // 2, near)
    recv_zb = [strips.take(tiles_b, chunks * chunk >> (k + 2), near) for k in range(nh)]
    recv_pa = strips.take(tiles_a, chunk, near)
    recv_xa = strips.take(tiles_a, chunk, near)
    recv_xb = strips.take(tiles_b, near, near)
    strips = Strips([wqkv, wo], width)
    send_za = [strips.take(tiles_a, chunks * chunk >> (k + 1), near) for k in range(nh)]
    send_pb = strips.take(tiles_b, chunks * chunk // 2, near)
    send_zb = [strips.take(tiles_b, chunks * chunk >> (k + 2), near) for k in range(nh)]
    send_pa = strips.take(tiles_a, chunk, near)

    def linked(src, dst, sem, partner):
        return pltpu.make_async_remote_copy(
            src_ref=src,
            dst_ref=dst,
            send_sem=sem.at[0],
            recv_sem=sem.at[1],
            device_id=partner,
            device_id_type=MESH,
        )

    copy_y = lambda i: linked(send_y(i), recv_y(i), sem_y.at[i], at_y)
    copy_za = lambda k, i: linked(send_za[k](i), recv_za[k](i), sem_za.at[k, i], at_h[k])
    copy_pa = lambda i: linked(send_pa(i), recv_pa(i), sem_pa.at[i], at_p)
    copy_pb = lambda i: linked(send_pb(i), recv_pb(i), sem_pb.at[i], at_p)
    copy_zb = lambda k, i: linked(send_zb[k](i), recv_zb[k](i), sem_zb.at[k, i], at_h[k])

    def block_product(l1, l2, r1, r2, c):
        def dots(cols):
            return dot_tn(l1(cols), r1) + dot_tn(l2(cols), r2)

        if chunk % 128 == 0:
            return dots(pl.ds(pl.multiple_of(c * chunk, chunk), chunk))
        both[...] = dots(pl.ds(pl.multiple_of((c // 2) * 2 * chunk, 2 * chunk), 2 * chunk))
        return both[pl.ds(pl.multiple_of((c % 2) * chunk, chunk), chunk), :]

    def products_a(i, parts):
        for op, (left, right) in enumerate(((gd, actv), (act2, db))):

            @pl.when(i // per == op)
            def _():
                mine = pl.ds(pl.multiple_of(zl * hu + (i - op * per) * width, width), width)
                its = pl.ds(pl.multiple_of(i * width, width), width)
                r1, r2 = right[:, mine], rbx[:, its]
                for n, which, put, after in parts:

                    @pl.loop(0, n)
                    def _(j):
                        l2 = lambda cols: lxx[op, :, cols]
                        put(j, block_product(lambda cols: left[:, cols], l2, r1, r2, which(j)))

                    after()

    def products_b(i, parts):
        groups = 3 * nq // width
        for late in range(2):

            @pl.when(i // groups == late)
            def _():
                cols = pl.ds(pl.multiple_of((i - late * groups) * width, width), width)
                r1, r2 = (mix[:, cols], dmix[:, cols]) if late else (dqkv[:, cols], qkv[:, cols])
                l1 = (lambda at: gm[:, at]) if late else (lambda at: act1[:, at])
                l2 = (lambda at: ar_full[pl.ds(0, p0), at]) if late else (lambda at: rows[:, at])
                for n, which, put, after in parts:

                    @pl.loop(0, n)
                    def _(j):
                        put(j, block_product(l1, l2, r1, r2, which(j)))

                    after()

    def rows_at(slab, i, lo, n):
        return slab.at(i, lo, n)

    def a_first(i):
        def put(j, v):
            send_y.at(i, j * chunk, chunk)[...] = v.astype(BF)

        products_a(i, [(chunks, lambda j: 2 * j + 1 - y, put, lambda: copy_y(i).start())])

    def a_second(i):
        copy_y(i).wait()
        bit = bit_of(b, halving[0])
        n = chunks // 2

        def total(j, v, at):
            return (v + recv_y.at(i, at * chunk, chunk)[...].astype(F32)).astype(BF)

        def give(j, v):
            send_za[0].at(i, j * chunk, chunk)[...] = total(j, v, (1 - bit) * n + j)

        def keep(j, v):
            x = total(j, v, bit * n + j)
            recv_y.at(i, j * chunk, chunk)[...] = x

        products_a(
            i,
            [
                (n, lambda j: 2 * ((1 - bit) * n + j) + y, give, lambda: copy_za(0, i).start()),
                (n, lambda j: 2 * (bit * n + j) + y, keep, lambda: None),
            ],
        )

    def halve(i, k, kept, at, recv, n, give, copy, start):
        def total(c):
            x = kept.at(i, (at + c) * chunk, chunk)[...].astype(F32)
            return (x + recv.at(i, c * chunk, chunk)[...].astype(F32)).astype(BF)

        bit = start
        for j in range(n // 2):
            give.at(i, j * chunk, chunk)[...] = total((1 - bit) * (n // 2) + j)
        copy().start()
        for j in range(n // 2):
            x = total(bit * (n // 2) + j)
            kept.at(i, (at + n + j) * chunk, chunk)[...] = x

    ends_a = [0]
    for k in range(nh + 1):
        ends_a.append(ends_a[-1] + (chunks >> (k + 1)))

    def a_third(k, i):
        copy_za(k, i).wait()
        n = chunks >> (k + 1)
        if k + 1 < nh:
            bit = bit_of(b, halving[k + 1])
            halve(i, k, recv_y, ends_a[k], recv_za[k], n, send_za[k + 1], lambda: copy_za(k + 1, i), bit)
        else:
            halve(i, k, recv_y, ends_a[k], recv_za[k], n, send_pa, lambda: copy_pa(i), zl)

    my_near = pl.multiple_of(s * near, near)
    its_near = pl.multiple_of((1 - s) * near, near)
    kept_a = lambda i, at: recv_y.at(i, ends_a[nh] * chunk + at, near)

    def copies_xa(i):
        return [
            linked(kept_a(i, its_near), recv_xa.at(i, zl * near, near), sem_xa.at[i, 0], at_x),
            linked(
                recv_pa.at(i, its_near, near),
                recv_xa.at(i, (1 - zl) * near, near),
                sem_xa.at[i, 1],
                at_x,
            ),
        ]

    def outs_a(i):
        def to(side, pair):
            col = 8 * nq + (1 - i // per) * 2 * nu + side * nu + pair * hu + (i % per) * width
            return w_hbm.at[:, pl.ds(pl.multiple_of(col, width), width)]

        pieces = [
            (kept_a(i, my_near), to(s, zl)),
            (recv_pa.at(i, my_near, near), to(s, 1 - zl)),
            (recv_xa.at(i, 0, near), to(1 - s, 0)),
            (recv_xa.at(i, near, near), to(1 - s, 1)),
        ]
        return [pltpu.make_async_copy(src, dst, sem_oa.at[i, k]) for k, (src, dst) in enumerate(pieces)]

    def a_fourth(i):
        copy_pa(i).wait()
        for copy in copies_xa(i) + outs_a(i)[:2]:
            copy.start()

    def a_fifth(i):
        for copy in copies_xa(i):
            copy.wait()
        for copy in outs_a(i)[2:]:
            copy.start()

    def b_first(i):
        n = chunks // 2

        def put(j, v):
            send_pb.at(i, j * chunk, chunk)[...] = v.astype(BF)

        products_b(i, [(n, lambda j: 2 * (2 * j + 1 - zl) + y, put, lambda: copy_pb(i).start())])

    def b_second(i):
        copy_pb(i).wait()
        bit = bit_of(b, halving[0])
        n = chunks // 4

        def total(v, at):
            return (v + recv_pb.at(i, at * chunk, chunk)[...].astype(F32)).astype(BF)

        def give(j, v):
            send_zb[0].at(i, j * chunk, chunk)[...] = total(v, (1 - bit) * n + j)

        def keep(j, v):
            x = total(v, bit * n + j)
            recv_pb.at(i, j * chunk, chunk)[...] = x

        products_b(
            i,
            [
                (n, lambda j: 2 * (2 * ((1 - bit) * n + j) + zl) + y, give, lambda: copy_zb(0, i).start()),
                (n, lambda j: 2 * (2 * (bit * n + j) + zl) + y, keep, lambda: None),
            ],
        )

    ends_b = [0]
    for k in range(nh):
        ends_b.append(ends_b[-1] + (chunks >> (k + 2)))
    kept_b = lambda i, at: recv_pb.at(i, ends_b[nh] * chunk + at, near)

    def copy_xb(i):
        return linked(kept_b(i, its_near), recv_xb(i), sem_xb.at[i], at_x)

    def outs_b(i):
        def to(side):
            col = (i // 2) * 2 * nq + side * nq + (i % 2) * width
            return w_hbm.at[:, pl.ds(pl.multiple_of(col, width), width)]

        return [
            pltpu.make_async_copy(kept_b(i, my_near), to(s), sem_ob.at[i, 0]),
            pltpu.make_async_copy(recv_xb(i), to(1 - s), sem_ob.at[i, 1]),
        ]

    def b_third(k, i):
        copy_zb(k, i).wait()
        n = chunks >> (k + 2)
        if k + 1 < nh:
            bit = bit_of(b, halving[k + 1])
            halve(i, k, recv_pb, ends_b[k], recv_zb[k], n, send_zb[k + 1], lambda: copy_zb(k + 1, i), bit)
        else:
            x = recv_pb.at(i, ends_b[k] * chunk, chunk)[...].astype(F32) + recv_zb[k](i)[...].astype(F32)
            recv_pb.at(i, ends_b[nh] * chunk, chunk)[...] = x.astype(BF)
            copy_xb(i).start()
            outs_b(i)[0].start()

    def b_fourth(i):
        copy_xb(i).wait()
        outs_b(i)[1].start()

    small_partners = [at_y] + at_h + [at_p, at_x]

    def small_step(k):
        copy = lambda k: linked(small_out, small_recv.at[k], sem_s.at[k], small_partners[k])
        if k > 0:
            copy(k - 1).wait()
            if k < len(small_partners):
                small_out[...] = small_out[...] + small_recv[k - 1]
        if k < len(small_partners):
            copy(k).start()
        else:
            small_final[s] = small_out[...]
            small_final[1 - s] = small_recv[k - 1]

    for copy in firsts:
        copy.wait()
    for copy in from_core:
        copy.wait()
    for copy, dst, at in from_x[:2]:
        copy.wait()
        block = dst.at[pl.ds(at + its_toks, toks), my_cols]
        forwards.append(remote(block, block, at_core))
    for copy in forwards:
        copy.wait()
    norm1(0, p0)
    share_feats_b(act1, la_hbm, 0, p0)
    for copy in weights[:3]:
        copy.wait()
    project(0, p0, 0, 3 * nq)
    forwards = []
    for copy, dst, at in from_x[2:]:
        copy.wait()
        block = dst.at[pl.ds(at + its_toks, toks), my_cols]
        forwards.append(remote(block, block, at_core))
    attend(0)
    share_mix(0, own)
    for copy in weights[3:4]:
        copy.wait()
    T = span
    a1 = Total(slots, 0, 0, whole(slots))
    a2 = Total(T, 2 * slots, 2 * slots, whole(T))
    a1.start(out_product(s0, slots))
    a2.start(out_product(t0, T))
    a1.middle()
    a2.middle()
    for copy in forwards + laters + late_core:
        copy.wait()
    gd[pl.ds(s1, slots), :] = (dsum[pl.ds(slots, slots), :].astype(F32) * row_live).astype(BF)
    share_feats_a(0, gd, t0, p0 - t0)
    a1.finish()
    a1.done()
    enter_ffn(a1, s0, slots)
    weights[4].wait()
    ffn(s0, slots, False)
    weights[5].wait()
    a3 = Total(slots, slots, slots, whole(slots))
    a3.start(down_product(s0, slots))
    a2.finish()
    a3.middle()
    a2.done()
    enter_ffn(a2, t0, T)
    outacc[0] = mid[pl.ds(t0 + my_toks, toks), my_cols]
    a3.finish()
    share_feats_a(1, act2, s0, own)
    a3.done()

    def summary(i):
        r = pl.ds(pl.multiple_of(s0 + i * step, step), step)
        f = pl.ds(pl.multiple_of(a3.full + i * step, step), step)
        p = pl.ds(pl.multiple_of(p0 + i * step, step), step)
        x = mid[r, :] + ar_full[f, :].astype(F32) + vec[5:6, :]
        on = (lax.broadcasted_iota(jnp.int32, (step, 1), 0) + i * step < live_count).astype(F32)
        rows[p, :] = (x * on).astype(BF)

    pl.loop(0, slots // step)(summary)
    sum_out[0] = rows[pl.ds(p0, slots), my_cols]
    norm1(p0, slots)
    share_feats_b(act1, la_hbm, p0, slots)
    project(p0, slots, nq, 3 * nq)
    attend(1)
    share_mix(t1, own)
    a5 = Total(own, 2 * slots + T, 2 * slots + T, whole(own))
    a5.start(out_product(t1, own))
    ffn(t0, T, True)
    share_actv(s0, own)
    share_db(t0, T)
    a5.middle()
    a6 = Total(T, 2 * slots, 2 * slots, whole(T))
    a6.start(up_back(t0, T))
    a6.middle()
    a5.finish()
    a4 = Total(T, 2 * slots + T + 2 * own, None, [(0, T, True)], 0)
    a4.start(down_product(t0, T))
    a5.done()
    enter_ffn(a5, t1, own)
    outacc[1] = mid[pl.ds(t1 + my_toks, toks), my_cols]
    outacc[2] = mid[pl.ds(s1, slots), my_cols]
    share_feats_a(1, act2, t1, own)
    ffn(t1, own, True)
    share_actv(t1, own)
    share_db(t1, own)
    a8 = Total(own, 2 * slots + T + own, 2 * slots + T + own, whole(own))
    a8.start(up_back(t1, own))
    a6.finish()
    a4.middle()
    a8.middle()
    a7 = Total(own, 2 * slots + 2 * T + 2 * own, None, [(0, T, True), (T, slots, False)], T)
    a7.start(down_product(t1, own))
    a7.middle()
    a6.done()
    leave_ffn(a6, t0, T)
    mix_back(t0, T)
    share_feats_b(gm, lm_hbm, t0, T)
    a8.finish()
    for copy in a4.xs:
        copy.wait()
    hid_out[0] = (outacc[0] + a4.sums(0, T, True) + vec[5:6, my_cols]).astype(BF)
    a8.done()
    leave_ffn(a8, t1, own)
    mix_back(t1, own)
    share_feats_b(gm, lm_hbm, t1, own)
    attend_back(1)
    share_qkv(t1, own + slots)
    a9 = Total(slots, 0, 0, whole(slots))
    a9.start(in_back(p0, slots, nq))
    a10 = Total(own, 2 * slots + T, 2 * slots + T, [(0, T, True), (T, slots, False)])
    a9.middle()
    a10.start(in_back(t1, own, 0))
    a9.finish()
    a10.middle()
    for copy in a7.xs:
        copy.wait()
    hid_out[1] = (outacc[1] + a7.sums(0, T, True) + vec[5:6, my_cols]).astype(BF)
    sum_out[1] = (
        (outacc[2] + a7.sums(T, slots, False) + vec[5:6, my_cols]) * row_live
    ).astype(BF)
    a9.done()
    first_only = (s == 0).astype(F32)

    def norm1_back(r, f, weight):
        d = ar_full[f, :].astype(F32)
        xhat = (rows[r, :].astype(F32) - stat[r, 0:1]) * stat[r, 1:2]
        gsum[pl.ds(0, 8), :] = gsum[pl.ds(0, 8), :] + fold(d * xhat) * weight
        gsum[pl.ds(8, 8), :] = gsum[pl.ds(8, 8), :] + fold(d) * weight
        return norm_back(d, xhat, stat[r, 1:2], vec[0:1, :])

    def prefix_back(i):
        r = pl.ds(pl.multiple_of(p0 + i * step, step), step)
        f = pl.ds(pl.multiple_of(a9.full + i * step, step), step)
        g = pl.ds(pl.multiple_of(s0 + i * step, step), step)
        on = (lax.broadcasted_iota(jnp.int32, (step, 1), 0) + i * step < live_count).astype(F32)
        d = norm1_back(r, f, first_only)
        gd[g, :] = ((dsum[pl.ds(pl.multiple_of(i * step, step), step), :].astype(F32) + d) * on).astype(BF)

    pl.loop(0, slots // step)(prefix_back)
    share_feats_a(0, gd, s0, slots)

    def last_before(c):
        cols = pl.ds(c, wide)
        r = pl.ds(s0, slots)
        db[r, cols] = (slope0[:, cols] * dot_nt(gd[r, :], wd[cols, :])).astype(BF)

    col_loop(nu, last_before)
    share_db(s0, slots)
    a11 = Total(slots, slots, slots, whole(slots))
    a11.start(up_back(s0, slots))
    askers = [at_x, at_p, at_y] + at_h
    for k, partner in enumerate(askers):
        pl.semaphore_signal(free.at[k], inc=1, device_id=partner, device_id_type=MESH)
    a10.finish()
    a11.middle()
    a10.done()

    def rows_back(total, seg):
        t_at, s_at = (t0, s0) if seg == 0 else (t1, s1)
        t_in, s_in = (slots, 0) if seg == 0 else (0, span)

        def tokens(i):
            r = pl.ds(pl.multiple_of(t_at + my_toks + i * step, step), step)
            f = pl.ds(pl.multiple_of(total.full + t_in + i * step, step), step)
            x = norm1_back(r, f, 1.0)
            mid[r, :] = mid[r, :] + x

        pl.loop(0, toks // step)(tokens)
        gin_out[seg] = mid[pl.ds(t_at + my_toks, toks), my_cols]

        def summaries(i):
            r = pl.ds(pl.multiple_of(s_at + i * step, step), step)
            f = pl.ds(pl.multiple_of(total.full + s_in + i * step, step), step)
            x = norm1_back(r, f, first_only) + mid[r, :]
            e = pl.ds(pl.multiple_of(i * step, step), step)
            emb_wide[e, :] = x if seg == 1 else emb_wide[e, :] + x

        pl.loop(0, slots // step)(summaries)

    emb_wide = slope0
    rows_back(a10, 1)
    pass_on(gifts_a)
    a11.finish()
    pass_end()
    for k in range(len(askers)):
        pl.semaphore_wait(free.at[k], 1)
    a_first(0)
    a11.done()
    leave_ffn(a11, s0, slots)
    mix_back(s0, slots)
    a_first(1)
    share_feats_b(gm, lm_hbm, s0, slots)
    attend_back(0)
    share_qkv(0, own)
    a12 = Total(own, 2 * slots + T + own, 2 * slots + T + own, [(0, slots, False), (slots, T, True)])
    a12.start(in_back(s0, own, 0))
    a12.middle()
    a_first(2)
    ones = jnp.ones((8, p0), BF)
    column = lambda ref, cols: jnp.dot(ones, ref[pl.ds(0, p0), cols], preferred_element_type=F32)[0:1, :]
    base = slots
    small_out[base + 2 : base + 3, :] = column(gm, my_quarter)
    small_out[base + 5 : base + 6, :] = column(gd, my_quarter)
    small_out[base + 3 : base + 4, :] = jnp.sum(fsum[pl.ds(0, 8), my_quarter], axis=0, keepdims=True)
    small_out[base + 4 : base + 5, :] = jnp.sum(fsum[pl.ds(8, 8), my_quarter], axis=0, keepdims=True)
    small_out[base + 6 : base + 7, :] = column(dqkv, pl.ds(0, nq))
    small_out[base + 7 : base + 8, :] = column(dqkv, pl.ds(2 * nq, nq)) + jnp.sum(
        dqkv[pl.ds(p0, slots), pl.ds(2 * nq, nq)].astype(F32), axis=0, keepdims=True
    )
    for k in range(nu // quarter):
        small_out[base + 8 + k : base + 9 + k, :] = column(db, pl.ds(k * quarter, quarter))
    small_out[base + 12 : base + 16, :] = jnp.zeros((4, quarter), F32)
    pass_on(gifts_b)
    a12.finish()
    a12.done()
    rows_back(a12, 0)
    small_out[pl.ds(0, slots), :] = emb_wide[:, my_quarter]
    its_quarter = pl.ds(pl.multiple_of(t * half + (1 - s) * quarter, quarter), quarter)
    gx_send[0:1, :] = jnp.sum(gsum[pl.ds(0, 8), its_quarter], axis=0, keepdims=True)
    gx_send[1:2, :] = jnp.sum(gsum[pl.ds(8, 8), its_quarter], axis=0, keepdims=True)
    gx_send[2:8, :] = jnp.zeros((6, quarter), F32)
    copy = remote(gx_send, gx_recv, at_x)
    copy.wait()
    small_out[base : base + 1, :] = gx_recv[0:1, :] + jnp.sum(gsum[pl.ds(0, 8), my_quarter], axis=0, keepdims=True)
    small_out[base + 1 : base + 2, :] = gx_recv[1:2, :] + jnp.sum(gsum[pl.ds(8, 8), my_quarter], axis=0, keepdims=True)
    small_step(0)
    pass_end()
    stage = [
        local(la_hbm, rows),
        local(lm_hbm, ar_full.at[pl.ds(0, p0), :]),
        local(ra_hbm, qkv),
        local(mx_hbm, dmix),
    ]
    for copy in stage:
        copy.wait()

    lead = 3

    def turn(it, lag, count, stage):
        @pl.when((it >= lag) & (it < lag + count))
        def _():
            stage(it - lag)

    turns = max(tiles_a + nh + 3, tiles_b + nh + 4)

    @pl.loop(0, turns)
    def _(it):
        @pl.when(it < tiles_a - lead)
        def _():
            a_first(it + lead)

        turn(it, 0, tiles_b, b_first)
        turn(it, 0, tiles_a, a_second)
        turn(it, 2, tiles_b, b_second)
        for k in range(nh):
            turn(it, k + 1, tiles_a, functools.partial(a_third, k))
        turn(it, nh + 1, tiles_a, a_fourth)
        turn(it, nh + 2, tiles_a, a_fifth)
        for k in range(nh):
            turn(it, k + 3, tiles_b, functools.partial(b_third, k))
        turn(it, nh + 3, tiles_b, b_fourth)
        for k in range(1, len(small_partners) + 1):

            @pl.when(it == 2 * k)
            def _():
                small_step(k)

    @pl.loop(0, tiles_a)
    def _(i):
        for copy in outs_a(i):
            copy.wait()

    @pl.loop(0, tiles_b)
    def _(i):
        for copy in outs_b(i):
            copy.wait()

def chain(count, emb, dsum, feat_vecs, bq, bv, bu, hid, dhid, wq, wk, wv, wo, wu, wd):
    bits = lax.axis_size("batch").bit_length() - 1
    toks, slots = hid.shape[1], emb.shape[0] + -emb.shape[0] % 64
    half = hid.shape[2]
    feats, quarter = 2 * half, half // 2
    nq, nu = wo.shape[0] // 2, wd.shape[0] // 2
    own = 2 * toks + slots
    main, end = 2 * own, 2 * own + slots
    sums = 2 * slots + 2 * toks + 2 * own
    chunk = feats >> bits
    nh = bits - 2
    ta, tb = 2 * nu // nq, 8
    vm = pltpu.VMEM
    sds = jax.ShapeDtypeStruct
    dma = pltpu.SemaphoreType.DMA
    scratch = [
        vm((feats, 3 * nq), BF),
        vm((nq, feats), BF),
        vm((feats, nu), BF),
        vm((nu, feats), BF),
        vm((end, feats), BF),
        vm((end, feats), BF),
        vm((end, 3 * nq), BF),
        vm((2, nq // HD, own, own + slots), BF),
        vm((main, nq), BF),
        vm((main, feats), F32),
        vm((main, feats), BF),
        vm((main, nu), BF),
        vm((main, nu), BF),
        vm((slots, nu), F32),
        vm((main, feats), BF),
        vm((main, feats), BF),
        vm((main, nq), BF),
        vm((end, 3 * nq), BF),
        vm((2 * slots, feats), BF),
        vm((8, feats), F32),
        vm((1, 3 * nq + nu), F32),
        vm((end, 128), F32),
        vm((3, toks, half), F32),
        vm((16, feats), F32),
        vm((16, feats), F32),
        vm((8, quarter), F32),
        vm((8, quarter), F32),
        vm((sums + 2 * toks + own, half), BF),
        vm((sums + 2 * toks + own, half), BF),
        vm((sums + 2 * toks + own, half), BF),
        vm((sums, feats), BF),
        vm((2 * toks + own, half), BF),
        vm((2, main, feats), BF),
        vm((main, nu), BF),
        vm((2 * chunk if chunk % 128 else 8, nq // 2), F32),
        vm((slots + 16, quarter), F32),
        vm((bits + 1, slots + 16, quarter), F32),
        dma((6,)),
        dma((16,)),
        dma((128, 2)),
        pltpu.SemaphoreType.REGULAR((3 + nh,)),
        dma((ta, 2)),
        dma((nh, ta, 2)),
        dma((ta, 2)),
        dma((ta, 2, 2)),
        dma((tb, 2)),
        dma((nh, tb, 2)),
        dma((tb, 2)),
        dma((ta, 4)),
        dma((tb, 2)),
        dma((bits + 1, 2)),
    ]
    vmem = pl.BlockSpec(memory_space=pltpu.VMEM)
    hbm = pl.BlockSpec(memory_space=pl.ANY)
    smem = pl.BlockSpec(memory_space=pltpu.SMEM)
    return pl.pallas_call(
        functools.partial(chain_kernel, bits),
        name="layer",
        out_shape=(
            sds((2, toks, half), BF),
            sds((2, slots, half), BF),
            sds((2, toks, half), F32),
            sds((2, slots + 16, quarter), F32),
            sds((chunk // 2, 8 * nq + 4 * nu), BF),
            sds((end, feats), BF),
            sds((main, feats), BF),
            sds((end, 3 * nq), BF),
            sds((main, nq), BF),
        ),
        in_specs=[smem, vmem, vmem, [vmem] * 6, vmem, vmem, vmem] + [hbm] * 8,
        out_specs=(vmem,) * 4 + (hbm,) * 5,
        scratch_shapes=scratch,
        compiler_params=pltpu.CompilerParams(
            collective_id=2, has_side_effects=True, vmem_limit_bytes=63 * 2**20
        ),
    )(count, emb, dsum, feat_vecs, bq, bv, bu, hid, dhid, wq, wk, wv, wo, wu, wd)


def place_kernel(hid, sums, gin, small, w, hid_o, sum_o, gin_o, emb_o, vec_o, bup_o, q_o, k_o, v_o, o_o, u_o, d_o):
    hid_o[0] = hid[...]
    used = sum_o.shape[2]
    sum_o[0] = sums[:, :used, :]
    gin_o[0] = gin[...]
    quarter = small.shape[2]
    base = small.shape[1] - 16
    nu = bup_o.shape[0] // 2
    for side in range(2):
        at = pl.ds(side * quarter, quarter)
        emb_o[:, at] = small[side, :used, :]
        for k, ref in enumerate(vec_o):
            ref[at] = small[side, base + k]
        for k in range(nu // quarter):
            bup_o[pl.ds(side * nu + k * quarter, quarter)] = small[side, base + 8 + k]
    n = q_o.shape[1]
    for k, ref in enumerate((q_o, k_o, v_o)):
        ref[...] = w[:, k * n : (k + 1) * n].astype(F32)
    o_o[...] = w[:, 3 * n : 4 * n].astype(F32).T
    u_o[...] = w[:, 4 * n : 4 * n + 2 * nu].astype(F32)
    d_o[...] = w[:, 4 * n + 2 * nu :].astype(F32).T


def place(hid, sums, gin, small, w, used):
    sds = jax.ShapeDtypeStruct
    _, toks, half = hid.shape
    rows = w.shape[0]
    nu = (w.shape[1] - 4 * half) // 4
    vmem = pl.BlockSpec(memory_space=pltpu.VMEM)
    return pl.pallas_call(
        place_kernel,
        name="place",
        out_shape=(
            sds((1, 2, toks, half), BF),
            sds((1, 2, used, half), BF),
            sds((1, 2, toks, half), F32),
            sds((used, half), F32),
            [sds((half,), F32)] * 8,
            sds((2 * nu,), F32),
            sds((rows, half), F32),
            sds((rows, half), F32),
            sds((rows, half), F32),
            sds((half, rows), F32),
            sds((rows, 2 * nu), F32),
            sds((2 * nu, rows), F32),
        ),
        in_specs=[vmem] * 5,
        out_specs=(vmem,) * 4 + ([vmem] * 8,) + (vmem,) * 7,
        compiler_params=pltpu.CompilerParams(vmem_limit_bytes=32 * 2**20),
    )(hid, sums, gin, small, w)


def local(
    hidden_in, summary_counts, summary_embed, ln1_gain, ln1_bias, w_query, b_query, w_key, w_value,
    b_value, w_out, b_out, ln2_gain, ln2_bias, w_up, b_up, w_down, b_down, d_hidden, d_summary,
):
    got = chain(
        summary_counts, summary_embed, d_summary,
        [ln1_gain, ln1_bias, ln2_gain, ln2_bias, b_out, b_down], b_query, b_value, b_up,
        hidden_in[0], d_hidden[0], w_query, w_key, w_value, w_out, w_up, w_down,
    )
    hid, sums, gin, emb, vecs, bup, gq, gk, gv, go, gu, gd = place(*got[:5], summary_embed.shape[0])
    return (
        hid, sums, gin, emb, vecs[0], vecs[1], gq, vecs[6], gk, gv,
        vecs[7], go, vecs[2], vecs[3], vecs[4], gu, bup, gd, vecs[5],
    )


def solution(mesh):
    return jax.shard_map(
        local,
        mesh=mesh,
        in_specs=(
            P("batch", None, "seq", "tensor"),
            P("batch"),
            P(None, "tensor"),
            P("tensor"),
            P("tensor"),
            P(None, "tensor"),
            P("tensor"),
            P(None, "tensor"),
            P(None, "tensor"),
            P("tensor"),
            P("tensor", None),
            P("tensor"),
            P("tensor"),
            P("tensor"),
            P(None, "tensor"),
            P("tensor"),
            P("tensor", None),
            P("tensor"),
            P("batch", None, "seq", "tensor"),
            P("batch", None, None, "tensor"),
        ),
        out_specs=(
            P("batch", None, "seq", "tensor"),
            P("batch", None, None, "tensor"),
            P("batch", None, "seq", "tensor"),
            P(None, "tensor"),
            P("tensor"),
            P("tensor"),
            P(("batch", "seq"), "tensor"),
            P("tensor"),
            P(("batch", "seq"), "tensor"),
            P(("batch", "seq"), "tensor"),
            P("tensor"),
            P("tensor", ("batch", "seq")),
            P("tensor"),
            P("tensor"),
            P("tensor"),
            P(("batch", "seq"), "tensor"),
            P("tensor"),
            P("tensor", ("batch", "seq")),
            P("tensor"),
        ),
        check_vma=False,
    )
```

```python
import functools

import jax
import jax.numpy as jnp
from jax import lax
from jax.experimental import pallas as pl
from jax.experimental.pallas import tpu as pltpu
from jax.sharding import PartitionSpec as P

HD = 64
EPSILON = 1e-05
NEGATIVE = -1e30
MESH = pl.DeviceIdType.MESH
BF = jnp.bfloat16
F32 = jnp.float32
PAIR_BIT = 1


def flip(index, bit):
    weight = 1 << bit
    return index + weight - 2 * weight * lax.rem(index // weight, 2)


def bit_of(index, bit):
    return lax.rem(index // (1 << bit), 2)


def dot_nt(a, b):
    return lax.dot_general(a, b, (((1,), (1,)), ((), ())), preferred_element_type=F32)


def dot_tn(a, b):
    return lax.dot_general(a, b, (((0,), (0,)), ((), ())), preferred_element_type=F32)


def dot_nt(a, b):
    return lax.dot_general(a, b, (((1,), (1,)), ((), ())), preferred_element_type=F32)


def dot_tn(a, b):
    return lax.dot_general(a, b, (((0,), (0,)), ((), ())), preferred_element_type=F32)


def grads_kernel(
    bits,
    tiles,
    width,
    la_ref,
    lx_ref,
    ra_ref,
    rb_ref,
    small_ref,
    gq_ref,
    gk_ref,
    gv_ref,
    go_ref,
    gu_ref,
    gd_ref,
    emb_ref,
    vec_refs,
    bup_ref,
    send0,
    recv0,
    keep0,
    both,
    sends,
    recvs,
    keeps,
    send_p,
    recv_p,
    keep_p,
    send_x,
    recv_x,
    small_cur,
    small_recv,
    sem0,
    sems,
    sem_p,
    sem_x,
    sem_s,
):
    b, s, t = lax.axis_index("batch"), lax.axis_index("seq"), lax.axis_index("tensor")
    halving = list(range(bits - 1, PAIR_BIT, -1))
    at_y = (flip(b, 0), s, t)
    at_p = (flip(b, PAIR_BIT), s, t)
    at_x = (b, 1 - s, t)
    at_h = [(flip(b, bit), s, t) for bit in halving]
    partners = [at_y, at_p, at_x] + at_h
    barrier = pltpu.get_barrier_semaphore()
    for partner in partners:
        pl.semaphore_signal(barrier, inc=1, device_id=partner, device_id_type=MESH)
    pl.semaphore_wait(barrier, len(partners))

    features = la_ref.shape[1]
    inner = ra_ref.shape[1] // width
    chunk = features // (1 << bits)
    half_count = 1 << (bits - 1)
    mine = bit_of(b, 0)

    def remote(src, dst, sem, partner):
        return pltpu.make_async_remote_copy(
            src_ref=src,
            dst_ref=dst,
            send_sem=sem.at[0],
            recv_sem=sem.at[1],
            device_id=partner,
            device_id_type=MESH,
        )

    def copy_y(i):
        return remote(send0.at[i], recv0.at[i], sem0.at[i], at_y)

    def copy_h(k, i):
        return remote(sends[k].at[i], recvs[k].at[i], sems[k].at[i], at_h[k])

    def copy_p(i):
        return remote(send_p.at[i], recv_p.at[i], sem_p.at[i], at_p)

    def copy_x(i):
        return remote(send_x.at[i], recv_x.at[i], sem_x.at[i], at_x)

    per = (tiles - inner - 1) // 2

    def product(i, side, put):
        def blocks(left, right):
            @pl.loop(0, half_count)
            def _(j):
                at = pl.ds(pl.multiple_of(j * chunk, chunk), chunk)
                if chunk % 128 == 0:
                    start = pl.multiple_of((2 * j + side) * chunk, chunk)
                    put(at, dot_tn(left(pl.ds(start, chunk)), right))
                else:
                    start = pl.multiple_of(2 * j * chunk, 2 * chunk)
                    both[...] = dot_tn(left(pl.ds(start, 2 * chunk)), right)
                    put(at, both[pl.ds(pl.multiple_of(side * chunk, chunk), chunk), :])

        @pl.when(i < inner)
        def _():
            cols = pl.ds(pl.multiple_of(i * width, width), width)
            blocks(lambda at: la_ref[:, at], ra_ref[:, cols])

        @pl.when(i >= inner)
        def _():
            k = i - inner
            cols = pl.ds(pl.multiple_of(k * width, width), width)
            op = (k + per - 1) // per
            blocks(lambda at: lx_ref[op, :, at], rb_ref[:, cols])

    small_cur[...] = small_ref[...]
    small_partners = [at_y] + at_h + [at_p]
    for k, partner in enumerate(small_partners):
        copy = remote(small_cur, small_recv.at[k], sem_s.at[k], partner)
        copy.start()

        if k == 0:

            @pl.loop(0, tiles)
            def _(i):
                def put(at, value):
                    send0[i, at, :] = value.astype(BF)

                product(i, 1 - mine, put)
                copy_y(i).start()

        copy.wait()
        small_cur[...] = small_cur[...] + small_recv[k]
    last = len(small_partners)
    copy = remote(small_cur, small_recv.at[last], sem_s.at[last], at_x)
    copy.start()
    copy.wait()
    used = emb_ref.shape[0]
    quarter = small_ref.shape[1]
    base = small_ref.shape[0] - 16
    for side, ref in ((s, small_cur), (1 - s, small_recv.at[last])):
        at = pl.ds(pl.multiple_of(side * quarter, quarter), quarter)
        emb_ref[:, at] = ref[pl.ds(0, used), :]
        for k, out in enumerate(vec_refs):
            out[:, at] = ref[base + k : base + k + 1, :]
        pieces = bup_ref.shape[1] // (2 * quarter)
        for k in range(pieces):
            at = pl.ds(pl.multiple_of((side * pieces + k) * quarter, quarter), quarter)
            bup_ref[:, at] = ref[base + 8 + k : base + 9 + k, :]

    stages = len(halving)

    def split(i, k, total, rows):
        bit = bit_of(b, halving[k])
        half = rows // 2
        keeps[k][i] = total(pl.multiple_of(bit * half, half), half)
        sends[k][i] = total(pl.multiple_of((1 - bit) * half, half), half).astype(BF)
        copy_h(k, i).start()

    def stage_first(i):
        copy_y(i).wait()

        def put(at, value):
            keep0[at, :] = value + recv0[i, at, :].astype(F32)

        product(i, mine, put)
        split(i, 0, lambda at, n: keep0[pl.ds(at, n), :], half_count * chunk)

    def stage_next(k, i):
        copy_h(k, i).wait()

        def total(at, n):
            return keeps[k][i, pl.ds(at, n), :] + recvs[k][i, pl.ds(at, n), :].astype(F32)

        rows = (half_count * chunk) >> (k + 1)
        if k + 1 < stages:
            split(i, k + 1, total, rows)
        else:
            bit = bit_of(b, PAIR_BIT)
            keep_p[i] = total(pl.multiple_of(bit * chunk, chunk), chunk)
            send_p[i] = total(pl.multiple_of((1 - bit) * chunk, chunk), chunk).astype(BF)
            copy_p(i).start()

    def write(i, side, pair, value):
        spot = pl.ds(pl.multiple_of((2 * side + pair) * width, width), width)
        for k, ref in enumerate((gq_ref, gk_ref, gv_ref)):

            @pl.when(i == k)
            def _():
                ref[:, spot] = value

        @pl.when(i == inner)
        def _():
            go_ref[spot, :] = value.T

        def unit(k):
            return pl.ds(pl.multiple_of(((2 * side + pair) * per + k) * width, width), width)

        @pl.when((i > inner) & (i <= inner + per))
        def _():
            gu_ref[:, unit(i - inner - 1)] = value

        @pl.when(i > inner + per)
        def _():
            gd_ref[unit(i - inner - 1 - per), :] = value.T

    def stage_pair(i):
        copy_p(i).wait()
        bit = bit_of(b, PAIR_BIT)
        half = chunk // 2
        mine_at = pl.multiple_of(s * half, half)
        other_at = pl.multiple_of((1 - s) * half, half)
        write(i, s, bit, keep_p[i, pl.ds(mine_at, half), :])
        write(i, s, 1 - bit, recv_p[i, pl.ds(mine_at, half), :].astype(F32))
        send_x[i, bit] = keep_p[i, pl.ds(other_at, half), :].astype(BF)
        send_x[i, 1 - bit] = recv_p[i, pl.ds(other_at, half), :]
        copy_x(i).start()

    def stage_last(i):
        copy_x(i).wait()
        for pair in range(2):
            write(i, 1 - s, pair, recv_x[i, pair].astype(F32))

    @pl.loop(0, tiles + stages + 2)
    def _(i):
        @pl.when(i < tiles)
        def _():
            stage_first(i)

        for k in range(stages):

            @pl.when((i >= k + 1) & (i < tiles + k + 1))
            def _():
                stage_next(k, i - (k + 1))

        @pl.when((i >= stages + 1) & (i < tiles + stages + 1))
        def _():
            stage_pair(i - (stages + 1))

        @pl.when(i >= stages + 2)
        def _():
            stage_last(i - (stages + 2))


class Strips:
    def __init__(self, refs, width):
        self.width = width
        self.free = [[ref, ref.shape[0], at, 0] for ref in refs for at in range(ref.shape[1] // width)]

    def take(self, tiles, n, unit):
        for k, (ref, height, at, used) in enumerate(self.free):
            if height < n:
                continue
            if used + tiles * n <= height:
                self.free[k][3] += tiles * n
                return Slab(ref, at, used, tiles, n, unit, self.width)
            per = height // n
            need = -(-tiles // per)
            run = self.free[k : k + need]
            if len(run) == need and all(r[0] is ref and r[3] == 0 for r in run):
                for r in run:
                    r[3] = height
                return Slab(ref, at, 0, per, n, unit, self.width)
        raise ValueError("no room")


class Slab:
    def __init__(self, ref, strip, start, per, n, unit, width):
        self.ref, self.strip, self.start, self.per = ref, strip, start, per
        self.n, self.unit, self.width = n, unit, width

    def at(self, i, lo, n):
        first = pl.multiple_of(self.start + (i % self.per) * self.n + lo, self.unit)
        col = pl.multiple_of((self.strip + i // self.per) * self.width, self.width)
        return self.ref.at[pl.ds(first, n), pl.ds(col, self.width)]

    def __call__(self, i):
        return self.at(i, 0, self.n)


def chain_kernel(
    bits,
    count_ref,
    emb_ref,
    dsum_ref,
    feat_refs,
    bq_ref,
    bv_ref,
    bu_ref,
    hid_hbm,
    dhid_hbm,
    wq_hbm,
    wk_hbm,
    wv_hbm,
    wo_hbm,
    wu_hbm,
    wd_hbm,
    hid_out,
    sum_out,
    gin_out,
    small_final,
    w_hbm,
    la_hbm,
    lm_hbm,
    ra_hbm,
    mx_hbm,
    wqkv,
    wo,
    wu,
    wd,
    rows,
    act1,
    qkv,
    probs,
    mix,
    mid,
    act2,
    actv,
    db,
    slope0,
    gd,
    gm,
    dmix,
    dqkv,
    dsum,
    vec,
    bias,
    stat,
    outacc,
    fsum,
    gsum,
    gx_send,
    gx_recv,
    ar_send,
    ar_core,
    ar_x,
    ar_full,
    ar_own,
    lxx,
    rbx,
    both,
    small_out,
    small_recv,
    wsem,
    lsem,
    rsem,
    free,
    sem_y,
    sem_za,
    sem_pa,
    sem_xa,
    sem_pb,
    sem_zb,
    sem_xb,
    sem_oa,
    sem_ob,
    sem_s,
):
    b, s, t = lax.axis_index("batch"), lax.axis_index("seq"), lax.axis_index("tensor")
    at_core = (b, s, 1 - t)
    at_x = (b, 1 - s, t)
    at_p = (flip(b, PAIR_BIT), s, t)
    at_y = (flip(b, 0), s, t)
    halving = list(range(bits - 1, PAIR_BIT, -1))
    at_h = [(flip(b, bit), s, t) for bit in halving]
    zl, y = bit_of(b, PAIR_BIT), bit_of(b, 0)
    barrier = pltpu.get_barrier_semaphore()
    partners = [at_core, at_x, at_p, at_y] + at_h
    for partner in partners:
        pl.semaphore_signal(barrier, inc=1, device_id=partner, device_id_type=MESH)

    toks = hid_hbm.shape[1]
    slots = slope0.shape[0]
    used = emb_ref.shape[0]
    feats = rows.shape[1]
    half = feats // 2
    quarter = feats // 4
    span = 2 * toks
    s0, t0, t1, s1, p0 = 0, slots, slots + span, slots + 2 * span, 2 * slots + 2 * span
    own = slots + span
    end = p0 + slots
    nq = wo.shape[0]
    nu = wu.shape[1]
    my_cols = pl.ds(pl.multiple_of(t * half, half), half)
    its_cols = pl.ds(pl.multiple_of((1 - t) * half, half), half)
    my_toks = pl.multiple_of(s * toks, toks)
    its_toks = pl.multiple_of((1 - s) * toks, toks)
    my_quarter = pl.ds(pl.multiple_of(t * half + s * quarter, quarter), quarter)

    counter = {"l": 0, "r": 0}

    def local(src, dst):
        counter["l"] += 1
        copy = pltpu.make_async_copy(src, dst, lsem.at[counter["l"] - 1])
        copy.start()
        return copy

    def remote(src, dst, partner):
        counter["r"] += 1
        at = counter["r"] - 1
        copy = pltpu.make_async_remote_copy(
            src_ref=src,
            dst_ref=dst,
            send_sem=rsem.at[at, 0],
            recv_sem=rsem.at[at, 1],
            device_id=partner,
            device_id_type=MESH,
        )
        copy.start()
        return copy

    part = lambda ref, n, axis: (
        ref.at[:, pl.ds(pl.multiple_of(s * n, n), n)]
        if axis
        else ref.at[pl.ds(pl.multiple_of(s * n, n), n), :]
    )
    weights = []
    for at, (src, dst) in enumerate(
        (
            (part(wq_hbm, nq, 1), wqkv.at[:, pl.ds(0, nq)]),
            (part(wk_hbm, nq, 1), wqkv.at[:, pl.ds(nq, nq)]),
            (part(wv_hbm, nq, 1), wqkv.at[:, pl.ds(2 * nq, nq)]),
            (part(wo_hbm, nq, 0), wo),
            (part(wu_hbm, nu, 1), wu),
            (part(wd_hbm, nu, 0), wd),
        )
    ):
        copy = pltpu.make_async_copy(src, dst, wsem.at[at])
        weights.append(copy)

    firsts = []
    for seg, at in enumerate((t0, t1)):
        firsts.append(local(hid_hbm.at[seg], rows.at[pl.ds(at + my_toks, toks), my_cols]))
    laters = []
    for seg, at in enumerate((t0, t1)):
        laters.append(local(dhid_hbm.at[seg], gd.at[pl.ds(at + my_toks, toks), my_cols]))
    for copy in weights[:3]:
        copy.start()
    for at in (s0, s1):
        rows[pl.ds(at, slots), my_cols] = jnp.zeros((slots, half), BF)
        rows[pl.ds(at, used), my_cols] = emb_ref[...]
    for seg in range(2):
        dsum[pl.ds(seg * slots, slots), my_cols] = jnp.zeros((slots, half), BF)
        dsum[pl.ds(seg * slots, used), my_cols] = dsum_ref[:, seg, :]
    for k, ref in enumerate(feat_refs):
        vec[k : k + 1, my_cols] = ref[...].astype(F32)[None]
    pl.semaphore_wait(barrier, len(partners))

    def in_x(src, dst, at):
        return remote(src, dst.at[pl.ds(at + my_toks, toks), my_cols], at_x)

    def in_core(block):
        return remote(block, block, at_core)

    def in_pass(dst, at):
        return in_core(dst.at[pl.ds(at + its_toks, toks), my_cols])

    x_hid = [in_x(hid_hbm.at[0], rows, t0)]
    from_core = [
        in_core(rows.at[pl.ds(s0, slots), my_cols]),
        in_core(vec.at[:, my_cols]),
        remote(hid_hbm.at[0], rows.at[pl.ds(t0 + my_toks, toks), my_cols], at_core),
    ]
    late_core = [
        in_core(rows.at[pl.ds(s1, slots), my_cols]),
        remote(hid_hbm.at[1], rows.at[pl.ds(t1 + my_toks, toks), my_cols], at_core),
        in_core(dsum.at[:, my_cols]),
    ]
    for src, dst, at in ((dhid_hbm.at[0], gd, t0), (dhid_hbm.at[1], gd, t1)):
        late_core.append(remote(src, dst.at[pl.ds(at + my_toks, toks), my_cols], at_core))
    for copy in weights[3:]:
        copy.start()

    live_count = count_ref[0]
    row_live = (lax.broadcasted_iota(jnp.int32, (slots, 1), 0) < live_count).astype(F32)
    dqkv[pl.ds(p0, slots), pl.ds(0, nq)] = jnp.zeros((slots, nq), BF)
    bias[:, pl.ds(nq, nq)] = jnp.zeros((1, nq), F32)
    for ref, at, n in ((bq_ref, 0, nq), (bv_ref, 2 * nq, nq), (bu_ref, 3 * nq, nu)):
        x = ref[...].astype(F32)[None]
        bias[:, pl.ds(at, n)] = jnp.where(s == 0, x[:, :n], x[:, n:])
    fsum[...] = jnp.zeros_like(fsum)
    gsum[...] = jnp.zeros_like(gsum)

    step = 16
    inverse = 1.0 / feats

    def row_loop(start, n, body):
        @pl.loop(0, n // step)
        def _(i):
            body(pl.ds(pl.multiple_of(start + i * step, step), step))

    def mean(x):
        return jnp.sum(x, axis=1, keepdims=True) * inverse

    def stats(x):
        m = mean(x)
        return m, lax.rsqrt(mean(x * x) - m * m + EPSILON)

    def norm1(start, n):
        def body(at):
            x = rows[at, :].astype(F32)
            m, r = stats(x)
            act1[at, :] = ((x - m) * r * vec[0:1, :] + vec[1:2, :]).astype(BF)
            stat[at, 0:1] = m
            stat[at, 1:2] = r

        row_loop(start, n, body)

    def norm_back(d, xhat, r, gain):
        q = d * gain
        return r * (q - mean(q) - xhat * mean(q * xhat))

    def fold(x):
        return jnp.sum(x.reshape(step // 8, 8, x.shape[1]), axis=0)

    wide = 512

    def col_loop(n, body):
        @pl.loop(0, n // wide)
        def _(j):
            body(pl.multiple_of(j * wide, wide))

    def project(at, n, lo, hi):
        def body(c):
            cols = pl.ds(pl.multiple_of(lo + c, wide), wide)
            x = jnp.dot(act1[pl.ds(at, n), :], wqkv[:, cols], preferred_element_type=F32)
            qkv[pl.ds(at, n), cols] = (x + bias[:, cols]).astype(BF)

        col_loop(hi - lo, body)

    class Total:
        def __init__(self, n, at, full, pieces, own_at=0):
            self.n, self.at, self.full, self.own_at = n, at, full, own_at
            self.pieces = pieces

        def mine(self, r, n):
            if self.full is None:
                return ar_own.at[pl.ds(self.own_at + r, n), :]
            return ar_full.at[pl.ds(self.full + r, n), my_cols]

        def start(self, product):
            at = pl.ds(self.at, self.n)

            def other(c):
                x = product(pl.multiple_of((1 - t) * half + c, wide), wide)
                ar_send[at, pl.ds(c, wide)] = x.astype(BF)

            col_loop(half, other)
            self.core = remote(ar_send.at[at, :], ar_core.at[at, :], at_core)

            def this(c):
                x = product(pl.multiple_of(t * half + c, wide), wide)
                if self.full is None:
                    ar_own[pl.ds(self.own_at, self.n), pl.ds(c, wide)] = x.astype(BF)
                else:
                    cols = pl.ds(pl.multiple_of(t * half + c, wide), wide)
                    ar_full[pl.ds(self.full, self.n), cols] = x.astype(BF)

            col_loop(half, this)

        def middle(self):
            self.core.wait()
            self.xs = []
            for base, n, scatter in self.pieces:
                at = pl.ds(self.at + base, n)
                ar_core[at, :] = (
                    self.mine(base, n)[...].astype(F32) + ar_core[at, :].astype(F32)
                ).astype(BF)
                if scatter:
                    src = ar_core.at[pl.ds(self.at + base + its_toks, toks), :]
                    dst = ar_x.at[pl.ds(self.at + base, toks), :]
                else:
                    src, dst = ar_core.at[at, :], ar_x.at[at, :]
                self.xs.append(remote(src, dst, at_x))

        def sums(self, base, n, scatter):
            if scatter:
                near = ar_core[pl.ds(self.at + base + my_toks, toks), :]
                far = ar_x[pl.ds(self.at + base, toks), :]
            else:
                near = ar_core[pl.ds(self.at + base, n), :]
                far = ar_x[pl.ds(self.at + base, n), :]
            return near.astype(F32) + far.astype(F32)

        def finish(self):
            self.backs = []
            for (base, n, scatter), copy in zip(self.pieces, self.xs):
                copy.wait()
                n = toks if scatter else n
                block = ar_full.at[pl.ds(self.full + base, n), my_cols]
                block[...] = self.sums(base, n, scatter).astype(BF)
                self.backs.append(remote(block, block, at_core))

        def done(self):
            for copy in self.backs:
                copy.wait()

        def flow(self, body):
            self.backs = []
            for k, ((base, n, _), copy) in enumerate(zip(self.pieces, self.xs)):
                copy.wait()
                block = ar_full.at[pl.ds(self.full + base, n), my_cols]
                block[...] = self.sums(base, n, False).astype(BF)
                self.backs.append(remote(block, block, at_core))
                if k:
                    self.backs[k - 1].wait()
                    body(*self.pieces[k - 1][:2])
            self.backs[-1].wait()
            body(*self.pieces[-1][:2])

    whole = lambda n: [(i, 64, False) for i in range(0, n, 64)]

    def out_product(at, n):
        return lambda c, w: jnp.dot(
            mix[pl.ds(at, n), :], wo[:, pl.ds(c, w)], preferred_element_type=F32
        )

    def down_product(at, n):
        return lambda c, w: jnp.dot(
            actv[pl.ds(at, n), :], wd[:, pl.ds(c, w)], preferred_element_type=F32
        )

    def up_back(at, n):
        return lambda c, w: dot_nt(db[pl.ds(at, n), :], wu[pl.ds(c, w), :])

    def in_back(at, n, lo):
        return lambda c, w: dot_nt(
            dqkv[pl.ds(at, n), pl.ds(lo, 3 * nq - lo)], wqkv[pl.ds(c, w), pl.ds(lo, 3 * nq - lo)]
        )

    def enter_ffn(total, at, n, base=0):
        def body(i):
            r = pl.ds(pl.multiple_of(at + base + i * step, step), step)
            f = pl.ds(pl.multiple_of(total.full + base + i * step, step), step)
            x = rows[r, :].astype(F32) + ar_full[f, :].astype(F32) + vec[4:5, :]
            m, rs = stats(x)
            mid[r, :] = x
            act2[r, :] = ((x - m) * rs * vec[2:3, :] + vec[3:4, :]).astype(BF)
            stat[r, 2:3] = m
            stat[r, 3:4] = rs

        pl.loop(0, n // step)(body)

    def gelu(v):
        c = 0.7978845608028654
        th = jnp.tanh(c * (v + 0.044715 * (v * v * v)))
        act = 0.5 * v * (1.0 + th)
        sl = 0.5 * (1.0 + th) + (0.5 * c) * v * (1.0 - th * th) * (1.0 + (3 * 0.044715) * v * v)
        return act, sl

    def ffn(at, n, back, lo, hi):
        r = pl.ds(at, n)

        def body(c):
            c = pl.multiple_of(lo + c, wide)
            cols = pl.ds(c, wide)
            v = jnp.dot(act2[r, :], wu[:, cols], preferred_element_type=F32)
            act, sl = gelu(v + bias[:, pl.ds(pl.multiple_of(3 * nq + c, wide), wide)])
            actv[r, cols] = act.astype(BF)
            if back == 1:
                db[r, cols] = (sl * dot_nt(gd[r, :], wd[cols, :])).astype(BF)
            elif back == 2:
                db[r, cols] = (sl * db[r, cols].astype(F32)).astype(BF)
            else:
                slope0[:, cols] = sl

        col_loop(hi - lo, body)

    def leave_ffn(total, at, n, base=0):
        def body(i):
            r = pl.ds(pl.multiple_of(at + base + i * step, step), step)
            f = pl.ds(pl.multiple_of(total.full + base + i * step, step), step)
            d = ar_full[f, :].astype(F32)
            xhat = (mid[r, :] - stat[r, 2:3]) * stat[r, 3:4]
            fsum[pl.ds(0, 8), :] = fsum[pl.ds(0, 8), :] + fold(d * xhat)
            fsum[pl.ds(8, 8), :] = fsum[pl.ds(8, 8), :] + fold(d)
            dm = gd[r, :].astype(F32) + norm_back(d, xhat, stat[r, 3:4], vec[2:3, :])
            mid[r, :] = dm
            gm[r, :] = dm.astype(BF)

        pl.loop(0, n // step)(body)

    def mix_back(at, n):
        dmix[pl.ds(at, n), :] = dot_nt(gm[pl.ds(at, n), :], wo[...]).astype(BF)

    pairs = nq // (2 * HD)
    scale = HD**-0.5

    def seen(seg, keys):
        q = lax.broadcasted_iota(jnp.int32, (own, keys), 0)
        k = lax.broadcasted_iota(jnp.int32, (own, keys), 1)
        if seg == 0:
            q = jnp.where(q < slots, q + span, q - slots)
            slot = k
            token = k >= slots
            k = jnp.where(token, k - slots, k + span)
            return (k <= q) & (token | (slot < live_count))
        token = k < span
        ahead = k >= own
        slot = jnp.where(ahead, k - own, k - span)
        return (ahead | (k <= q)) & (token | (slot < live_count))

    def lanes(n):
        first = (lax.broadcasted_iota(jnp.int32, (n, 2 * HD), 1) < HD).astype(F32)
        return first.astype(BF), (1.0 - first).astype(BF)

    def attend(seg):
        at, keys = (s0, own) if seg == 0 else (t1, own + slots)
        q_rows, k_rows = pl.ds(at, own), pl.ds(at, keys)

        @pl.loop(0, pairs)
        def _(j):
            col = lambda g: pl.ds(pl.multiple_of(g * nq + j * 2 * HD, 2 * HD), 2 * HD)
            q, k, v = qkv[q_rows, col(0)], qkv[k_rows, col(1)], qkv[k_rows, col(2)]
            first = lanes(keys)
            allowed = seen(seg, keys)
            got = jnp.zeros((own, 2 * HD), F32)
            for h in range(2):
                pick = first[h]
                sc = dot_nt(q, k * pick) * scale
                sc = jnp.where(allowed, sc, NEGATIVE)
                e = jnp.exp(sc - jnp.max(sc, axis=1, keepdims=True))
                p = (e / jnp.sum(e, axis=1, keepdims=True)).astype(BF)
                probs[seg, 2 * j + h, :, pl.ds(0, keys)] = p
                got += jnp.dot(p, v * pick, preferred_element_type=F32)
            mix[q_rows, pl.ds(pl.multiple_of(j * 2 * HD, 2 * HD), 2 * HD)] = got.astype(BF)

    def attend_back(seg):
        at, keys = (s0, own) if seg == 0 else (t1, own + slots)
        q_rows, k_rows = pl.ds(at, own), pl.ds(at, keys)

        @pl.loop(0, pairs)
        def _(j):
            col = lambda g: pl.ds(pl.multiple_of(g * nq + j * 2 * HD, 2 * HD), 2 * HD)
            q, k, v = qkv[q_rows, col(0)], qkv[k_rows, col(1)], qkv[k_rows, col(2)]
            d = dmix[q_rows, pl.ds(pl.multiple_of(j * 2 * HD, 2 * HD), 2 * HD)]
            first_k, first_q = lanes(keys), lanes(own)
            dq = jnp.zeros((own, 2 * HD), F32)
            dk = jnp.zeros((keys, 2 * HD), F32)
            dv = jnp.zeros((keys, 2 * HD), F32)
            for h in range(2):
                pick_k, pick_q = first_k[h], first_q[h]
                p = probs[seg, 2 * j + h, :, pl.ds(0, keys)]
                pf = p.astype(F32)
                dp = dot_nt(d, v * pick_k)
                ds = (pf * (dp - jnp.sum(pf * dp, axis=1, keepdims=True))).astype(BF)
                dq += jnp.dot(ds, k * pick_k, preferred_element_type=F32)
                dk += dot_tn(ds, q * pick_q)
                dv += dot_tn(p, d * pick_q)
            dqkv[q_rows, col(0)] = (dq * scale).astype(BF)
            dqkv[k_rows, col(1)] = (dk * scale).astype(BF)
            dqkv[k_rows, col(2)] = dv.astype(BF)

    gifts_a, gifts_b, passed = [], [], []
    hu = nu // 2
    chunk = feats >> bits
    chunks = 1 << (bits - 1)

    def share_feats_a(op, src, at, n):
        landing = lxx.at[op, pl.ds(at, n), my_cols]
        gifts_a.append((remote(src.at[pl.ds(at, n), my_cols], landing, at_p), landing))

    def share_units_a(src, col, at, n):
        its = pl.ds(pl.multiple_of((1 - zl) * hu, hu), hu)
        landing = rbx.at[pl.ds(at, n), pl.ds(col, hu)]
        gifts_a.append((remote(src.at[pl.ds(at, n), its], landing, at_p), None))

    def share_feats_b(src, dst, at, n):
        some = [(my_cols, my_cols)]
        if chunk % 128 == 0:
            block = lambda c: pl.ds(pl.multiple_of(c * chunk, chunk), chunk)
            some = [2 * (t * chunks // 2 + m) for m in range(chunks // 2)]
            some = [(block(c + 1 - y), block(c + y)) for c in some]
        for out, back in some:
            copy = remote(src.at[pl.ds(at, n), out], dst.at[pl.ds(at, n), out], at_y)
            gifts_b.append((copy, dst.at[pl.ds(at, n), back]))

    def share_units_b(src, dst, at, n):
        gifts_b.append((remote(src.at[pl.ds(at, n), :], dst.at[pl.ds(at, n), :], at_y), None))

    def pass_on(gifts, most=1000):
        while gifts and most:
            most -= 1
            copy, landing = gifts.pop(0)
            copy.wait()
            if landing is not None:
                passed.append(remote(landing, landing, at_core))

    def pass_end():
        while passed:
            passed.pop(0).wait()

    share_qkv = lambda at, n: share_units_b(dqkv, ra_hbm, at, n)
    share_mix = lambda at, n: share_units_b(mix, mx_hbm, at, n)
    share_actv = lambda at, n: share_units_a(actv, 0, at, n)
    share_db = lambda at, n: share_units_a(db, hu, at, n)

    width = nq // 2
    near = chunk // 2
    per = hu // width
    tiles_a, tiles_b = 2 * per, 4 * nq // width
    nh = len(halving)
    strips = Strips([wu, wd], width)
    recv_y = strips.take(tiles_a, chunks * chunk, near)
    send_y = strips.take(tiles_a, chunks * chunk, near)
    recv_za = [strips.take(tiles_a, chunks * chunk >> (k + 1), near) for k in range(nh)]
    recv_pb = strips.take(tiles_b, chunks * chunk // 2, near)
    recv_zb = [strips.take(tiles_b, chunks * chunk >> (k + 2), near) for k in range(nh)]
    recv_pa = strips.take(tiles_a, chunk, near)
    recv_xa = strips.take(tiles_a, chunk, near)
    recv_xb = strips.take(tiles_b, near, near)
    strips = Strips([wqkv, wo], width)
    send_za = [strips.take(tiles_a, chunks * chunk >> (k + 1), near) for k in range(nh)]
    send_pb = strips.take(tiles_b, chunks * chunk // 2, near)
    send_zb = [strips.take(tiles_b, chunks * chunk >> (k + 2), near) for k in range(nh)]
    send_pa = strips.take(tiles_a, chunk, near)

    def linked(src, dst, sem, partner):
        return pltpu.make_async_remote_copy(
            src_ref=src,
            dst_ref=dst,
            send_sem=sem.at[0],
            recv_sem=sem.at[1],
            device_id=partner,
            device_id_type=MESH,
        )

    copy_y = lambda i: linked(send_y(i), recv_y(i), sem_y.at[i], at_y)
    copy_za = lambda k, i: linked(send_za[k](i), recv_za[k](i), sem_za.at[k, i], at_h[k])
    copy_pa = lambda i: linked(send_pa(i), recv_pa(i), sem_pa.at[i], at_p)
    copy_pb = lambda i: linked(send_pb(i), recv_pb(i), sem_pb.at[i], at_p)
    copy_zb = lambda k, i: linked(send_zb[k](i), recv_zb[k](i), sem_zb.at[k, i], at_h[k])

    def block_product(l1, l2, r1, r2, c):
        def dots(cols):
            return dot_tn(l1(cols), r1) + dot_tn(l2(cols), r2)

        if chunk % 128 == 0:
            return dots(pl.ds(pl.multiple_of(c * chunk, chunk), chunk))
        both[...] = dots(pl.ds(pl.multiple_of((c // 2) * 2 * chunk, 2 * chunk), 2 * chunk))
        return both[pl.ds(pl.multiple_of((c % 2) * chunk, chunk), chunk), :]

    def products_a(i, parts):
        for op, (left, right) in enumerate(((gd, actv), (act2, db))):

            @pl.when(i // per == op)
            def _():
                mine = pl.ds(pl.multiple_of(zl * hu + (i - op * per) * width, width), width)
                its = pl.ds(pl.multiple_of(i * width, width), width)
                r1, r2 = right[:, mine], rbx[:, its]
                for n, which, put, after in parts:

                    @pl.loop(0, n)
                    def _(j):
                        l2 = lambda cols: lxx[op, :, cols]
                        put(j, block_product(lambda cols: left[:, cols], l2, r1, r2, which(j)))

                    after()

    def products_b(i, parts):
        groups = nq // width
        for op in range(2):

            @pl.when(jnp.minimum(i // groups, 1) == op)
            def _():
                cols = pl.ds(pl.multiple_of((i - op * groups) * width, width), width)
                r1, r2 = (dqkv[:, cols], qkv[:, cols]) if op else (mix[:, cols], dmix[:, cols])
                l1 = (lambda at: act1[:, at]) if op else (lambda at: gm[:, at])
                l2 = (lambda at: rows[:, at]) if op else (lambda at: ar_full[pl.ds(0, p0), at])
                for n, which, put, after in parts:

                    @pl.loop(0, n)
                    def _(j):
                        put(j, block_product(l1, l2, r1, r2, which(j)))

                    after()

    def rows_at(slab, i, lo, n):
        return slab.at(i, lo, n)

    def a_first(i):
        def put(j, v):
            send_y.at(i, j * chunk, chunk)[...] = v.astype(BF)

        products_a(i, [(chunks, lambda j: 2 * j + 1 - y, put, lambda: copy_y(i).start())])

    def a_second(i):
        copy_y(i).wait()
        bit = bit_of(b, halving[0])
        n = chunks // 2

        def total(j, v, at):
            return (v + recv_y.at(i, at * chunk, chunk)[...].astype(F32)).astype(BF)

        def give(j, v):
            send_za[0].at(i, j * chunk, chunk)[...] = total(j, v, (1 - bit) * n + j)

        def keep(j, v):
            x = total(j, v, bit * n + j)
            recv_y.at(i, j * chunk, chunk)[...] = x

        products_a(
            i,
            [
                (n, lambda j: 2 * ((1 - bit) * n + j) + y, give, lambda: copy_za(0, i).start()),
                (n, lambda j: 2 * (bit * n + j) + y, keep, lambda: None),
            ],
        )

    def halve(i, k, kept, at, recv, n, give, copy, start):
        def total(c):
            x = kept.at(i, (at + c) * chunk, chunk)[...].astype(F32)
            return (x + recv.at(i, c * chunk, chunk)[...].astype(F32)).astype(BF)

        bit = start
        for j in range(n // 2):
            give.at(i, j * chunk, chunk)[...] = total((1 - bit) * (n // 2) + j)
        copy().start()
        for j in range(n // 2):
            x = total(bit * (n // 2) + j)
            kept.at(i, (at + n + j) * chunk, chunk)[...] = x

    ends_a = [0]
    for k in range(nh + 1):
        ends_a.append(ends_a[-1] + (chunks >> (k + 1)))

    def a_third(k, i):
        copy_za(k, i).wait()
        n = chunks >> (k + 1)
        if k + 1 < nh:
            bit = bit_of(b, halving[k + 1])
            halve(i, k, recv_y, ends_a[k], recv_za[k], n, send_za[k + 1], lambda: copy_za(k + 1, i), bit)
        else:
            halve(i, k, recv_y, ends_a[k], recv_za[k], n, send_pa, lambda: copy_pa(i), zl)

    my_near = pl.multiple_of(s * near, near)
    its_near = pl.multiple_of((1 - s) * near, near)
    kept_a = lambda i, at: recv_y.at(i, ends_a[nh] * chunk + at, near)

    def copies_xa(i):
        return [
            linked(kept_a(i, its_near), recv_xa.at(i, zl * near, near), sem_xa.at[i, 0], at_x),
            linked(
                recv_pa.at(i, its_near, near),
                recv_xa.at(i, (1 - zl) * near, near),
                sem_xa.at[i, 1],
                at_x,
            ),
        ]

    def outs_a(i, picks):
        def to(side, pair):
            col = 8 * nq + (1 - i // per) * 2 * nu + side * nu + pair * hu + (i % per) * width
            return w_hbm.at[:, pl.ds(pl.multiple_of(col, width), width)]

        pieces = [
            (kept_a(i, my_near), to(s, zl)),
            (recv_pa.at(i, my_near, near), to(s, 1 - zl)),
            (recv_xa.at(i, 0, near), to(1 - s, 0)),
            (recv_xa.at(i, near, near), to(1 - s, 1)),
        ]
        return [pltpu.make_async_copy(*pieces[k], sem_oa.at[i, k]) for k in picks]

    def a_fourth(i):
        copy_pa(i).wait()
        for copy in copies_xa(i) + outs_a(i, (0, 1)):
            copy.start()

    def a_fifth(i):
        for copy in copies_xa(i):
            copy.wait()
        for copy in outs_a(i, (2, 3)):
            copy.start()

    def b_first(i):
        n = chunks // 2

        def put(j, v):
            send_pb.at(i, j * chunk, chunk)[...] = v.astype(BF)

        products_b(i, [(n, lambda j: 2 * (2 * j + 1 - zl) + y, put, lambda: copy_pb(i).start())])

    def b_second(i):
        copy_pb(i).wait()
        bit = bit_of(b, halving[0])
        n = chunks // 4

        def total(v, at):
            return (v + recv_pb.at(i, at * chunk, chunk)[...].astype(F32)).astype(BF)

        def give(j, v):
            send_zb[0].at(i, j * chunk, chunk)[...] = total(v, (1 - bit) * n + j)

        def keep(j, v):
            x = total(v, bit * n + j)
            recv_pb.at(i, j * chunk, chunk)[...] = x

        products_b(
            i,
            [
                (n, lambda j: 2 * (2 * ((1 - bit) * n + j) + zl) + y, give, lambda: copy_zb(0, i).start()),
                (n, lambda j: 2 * (2 * (bit * n + j) + zl) + y, keep, lambda: None),
            ],
        )

    ends_b = [0]
    for k in range(nh):
        ends_b.append(ends_b[-1] + (chunks >> (k + 2)))
    kept_b = lambda i, at: recv_pb.at(i, ends_b[nh] * chunk + at, near)

    def copy_xb(i):
        return linked(kept_b(i, its_near), recv_xb(i), sem_xb.at[i], at_x)

    def outs_b(i, picks):
        def to(side):
            groups = nq // width
            op = (i // groups + 3) % 4
            col = op * 2 * nq + side * nq + (i % groups) * width
            return w_hbm.at[:, pl.ds(pl.multiple_of(col, width), width)]

        pieces = [(kept_b(i, my_near), to(s)), (recv_xb(i), to(1 - s))]
        return [pltpu.make_async_copy(*pieces[k], sem_ob.at[i, k]) for k in picks]

    def b_third(k, i):
        copy_zb(k, i).wait()
        n = chunks >> (k + 2)
        if k + 1 < nh:
            bit = bit_of(b, halving[k + 1])
            halve(i, k, recv_pb, ends_b[k], recv_zb[k], n, send_zb[k + 1], lambda: copy_zb(k + 1, i), bit)
        else:
            x = recv_pb.at(i, ends_b[k] * chunk, chunk)[...].astype(F32) + recv_zb[k](i)[...].astype(F32)
            recv_pb.at(i, ends_b[nh] * chunk, chunk)[...] = x.astype(BF)
            copy_xb(i).start()
            outs_b(i, (0,))[0].start()

    def b_fourth(i):
        copy_xb(i).wait()
        outs_b(i, (1,))[0].start()

    small_partners = [at_y] + at_h + [at_p, at_x]

    def small_step(k):
        copy = lambda k: linked(small_out, small_recv.at[k], sem_s.at[k], small_partners[k])
        if k > 0:
            copy(k - 1).wait()
            if k < len(small_partners):
                small_out[...] = small_out[...] + small_recv[k - 1]
        if k < len(small_partners):
            copy(k).start()
        else:
            small_final[s] = small_out[...]
            small_final[1 - s] = small_recv[k - 1]

    for copy in firsts + from_core:
        copy.wait()
    norm1(s0, slots)
    norm1(t0 + my_toks, toks)
    x_hid[0].wait()
    forward = in_pass(rows, t0)
    x_hid.append(in_x(hid_hbm.at[1], rows, t1))
    x_dhid = [in_x(dhid_hbm.at[0], gd, t0), in_x(dhid_hbm.at[1], gd, t1)]
    forward.wait()
    norm1(t0 + its_toks, toks)
    share_feats_b(act1, la_hbm, 0, own)
    for copy in weights[:3]:
        copy.wait()
    project(0, own, 0, 3 * nq)
    attend(0)
    share_mix(0, own)
    for copy in weights[3:4]:
        copy.wait()
    T = span
    a1 = Total(slots, 0, 0, whole(slots))
    a2 = Total(T, 2 * slots, 2 * slots, whole(T))
    a1.start(out_product(s0, slots))
    a2.start(out_product(t0, T))
    a1.middle()
    a2.middle()
    x_hid[1].wait()
    forward = in_pass(rows, t1)
    for copy in late_core + laters:
        copy.wait()
    forward.wait()
    norm1(t1, own)
    share_feats_b(act1, la_hbm, t1, own)
    project(t1, own, 0, 3 * nq)
    a1.finish()
    a1.done()
    enter_ffn(a1, s0, slots)
    weights[4].wait()
    forwards = []
    for copy, at in zip(x_dhid, (t0, t1)):
        copy.wait()
        forwards.append(in_pass(gd, at))
    gd[pl.ds(s1, slots), :] = (dsum[pl.ds(slots, slots), :].astype(F32) * row_live).astype(BF)
    ffn(s0, slots, 0, 0, nu)
    for copy in forwards:
        copy.wait()
    share_feats_a(0, gd, t0, p0 - t0)
    weights[5].wait()
    a3 = Total(slots, slots, slots, whole(slots))
    a3.start(down_product(s0, slots))
    a2.finish()
    a3.middle()
    a2.done()
    enter_ffn(a2, t0, T)
    outacc[0] = mid[pl.ds(t0 + my_toks, toks), my_cols]

    def early_before(c):
        cols, r = pl.ds(c, wide), pl.ds(t1, own)
        db[r, cols] = dot_nt(gd[r, :], wd[cols, :]).astype(BF)

    col_loop(nu, early_before)
    a3.finish()
    share_feats_a(1, act2, s0, own)
    a3.done()

    def summary(i):
        r = pl.ds(pl.multiple_of(s0 + i * step, step), step)
        f = pl.ds(pl.multiple_of(a3.full + i * step, step), step)
        p = pl.ds(pl.multiple_of(p0 + i * step, step), step)
        x = mid[r, :] + ar_full[f, :].astype(F32) + vec[5:6, :]
        on = (lax.broadcasted_iota(jnp.int32, (step, 1), 0) + i * step < live_count).astype(F32)
        rows[p, :] = (x * on).astype(BF)

    pl.loop(0, slots // step)(summary)
    sum_out[0] = rows[pl.ds(p0, slots), my_cols]
    norm1(p0, slots)
    share_feats_b(act1, la_hbm, p0, slots)
    project(p0, slots, nq, 3 * nq)
    attend(1)
    share_mix(t1, own)
    a5 = Total(own, 2 * slots + T, 2 * slots + T, whole(own))
    a5.start(out_product(t1, own))
    ffn(t0, T, 1, 0, nu // 4)
    a5.middle()
    ffn(t0, T, 1, nu // 4, nu)
    share_actv(s0, own)
    share_db(t0, T)
    a6 = Total(T, 2 * slots, 2 * slots, whole(T))
    a6.start(up_back(t0, T))
    a6.middle()
    a4 = Total(T, 2 * slots + T + 2 * own, None, [(0, T, True)], 0)
    a4.start(down_product(t0, T))
    a5.flow(lambda base, n: enter_ffn(a5, t1, n, base))
    a4.middle()
    outacc[1] = mid[pl.ds(t1 + my_toks, toks), my_cols]
    outacc[2] = mid[pl.ds(s1, slots), my_cols]
    share_feats_a(1, act2, t1, own)
    ffn(t1, own, 2, 0, nu)
    share_actv(t1, own)
    a8 = Total(own, 2 * slots + T + own, 2 * slots + T + own, whole(own))
    a8.start(up_back(t1, own))
    a6.finish()
    a8.middle()
    a7 = Total(own, 2 * slots + 2 * T + 2 * own, None, [(0, T, True), (T, slots, False)], T)
    a7.start(down_product(t1, own))
    a6.done()
    leave_ffn(a6, t0, T)
    mix_back(t0, T)
    share_feats_b(gm, lm_hbm, t0, T)
    a8.flow(lambda base, n: leave_ffn(a8, t1, n, base))
    a7.middle()
    mix_back(t1, own)
    share_feats_b(gm, lm_hbm, t1, own)
    early_b = len(gifts_b)
    attend_back(1)
    share_qkv(t1, own + slots)
    a9 = Total(slots, 0, 0, whole(slots))
    a9.start(in_back(p0, slots, nq))
    a10 = Total(own, 2 * slots + T, 2 * slots + T, [(0, T, True), (T, slots, False)])
    a9.middle()
    a10.start(in_back(t1, own, 0))
    pass_on(gifts_b, early_b)
    a9.finish()
    a10.middle()
    for copy in a4.xs + a7.xs:
        copy.wait()
    hid_out[0] = (outacc[0] + a4.sums(0, T, True) + vec[5:6, my_cols]).astype(BF)
    hid_out[1] = (outacc[1] + a7.sums(0, T, True) + vec[5:6, my_cols]).astype(BF)
    sum_out[1] = (
        (outacc[2] + a7.sums(T, slots, False) + vec[5:6, my_cols]) * row_live
    ).astype(BF)
    a9.done()
    first_only = (s == 0).astype(F32)

    def norm1_back(r, f, weight):
        d = ar_full[f, :].astype(F32)
        xhat = (rows[r, :].astype(F32) - stat[r, 0:1]) * stat[r, 1:2]
        gsum[pl.ds(0, 8), :] = gsum[pl.ds(0, 8), :] + fold(d * xhat) * weight
        gsum[pl.ds(8, 8), :] = gsum[pl.ds(8, 8), :] + fold(d) * weight
        return norm_back(d, xhat, stat[r, 1:2], vec[0:1, :])

    def prefix_back(i):
        r = pl.ds(pl.multiple_of(p0 + i * step, step), step)
        f = pl.ds(pl.multiple_of(a9.full + i * step, step), step)
        g = pl.ds(pl.multiple_of(s0 + i * step, step), step)
        on = (lax.broadcasted_iota(jnp.int32, (step, 1), 0) + i * step < live_count).astype(F32)
        d = norm1_back(r, f, first_only)
        gd[g, :] = ((dsum[pl.ds(pl.multiple_of(i * step, step), step), :].astype(F32) + d) * on).astype(BF)

    pl.loop(0, slots // step)(prefix_back)
    share_feats_a(0, gd, s0, slots)
    late_gifts = 1 + len(gifts_a)
    share_db(t1, own)

    def last_before(c):
        cols = pl.ds(c, wide)
        r = pl.ds(s0, slots)
        db[r, cols] = (slope0[:, cols] * dot_nt(gd[r, :], wd[cols, :])).astype(BF)

    col_loop(nu, last_before)
    share_db(s0, slots)
    a11 = Total(slots, slots, slots, whole(slots))
    a11.start(up_back(s0, slots))
    askers = [at_x, at_p, at_y] + at_h
    for k, partner in enumerate(askers):
        pl.semaphore_signal(free.at[k], inc=1, device_id=partner, device_id_type=MESH)
    a10.finish()
    a11.middle()
    pass_on(gifts_a, late_gifts - 1)
    a10.done()
    pass_end()
    for k in range(len(askers)):
        pl.semaphore_wait(free.at[k], 1)
    a_first(0)

    def rows_back(total, seg):
        t_at, s_at = (t0, s0) if seg == 0 else (t1, s1)
        t_in, s_in = (slots, 0) if seg == 0 else (0, span)

        def tokens(i):
            r = pl.ds(pl.multiple_of(t_at + my_toks + i * step, step), step)
            f = pl.ds(pl.multiple_of(total.full + t_in + i * step, step), step)
            x = norm1_back(r, f, 1.0)
            mid[r, :] = mid[r, :] + x

        pl.loop(0, toks // step)(tokens)
        gin_out[seg] = mid[pl.ds(t_at + my_toks, toks), my_cols]

        def summaries(i):
            r = pl.ds(pl.multiple_of(s_at + i * step, step), step)
            f = pl.ds(pl.multiple_of(total.full + s_in + i * step, step), step)
            x = norm1_back(r, f, first_only) + mid[r, :]
            e = pl.ds(pl.multiple_of(i * step, step), step)
            emb_wide[e, :] = x if seg == 1 else emb_wide[e, :] + x

        pl.loop(0, slots // step)(summaries)

    emb_wide = slope0
    rows_back(a10, 1)
    a11.finish()
    a11.done()
    leave_ffn(a11, s0, slots)
    mix_back(s0, slots)
    share_feats_b(gm, lm_hbm, s0, slots)
    attend_back(0)
    a_first(1)
    a12 = Total(own, 2 * slots + T + own, 2 * slots + T + own, [(0, slots, False), (slots, T, True)])
    a12.start(in_back(s0, own, 0))
    pass_on(gifts_b)
    a12.middle()
    stage = [
        local(ra_hbm.at[pl.ds(t1, own + slots), :], qkv.at[pl.ds(t1, own + slots), :]),
        local(mx_hbm, dmix),
    ]
    pass_end()
    stage.append(local(lm_hbm, ar_full.at[pl.ds(0, p0), :]))
    a_second(0)
    for copy in stage:
        copy.wait()
    b_first(0)
    b_first(1)
    ones = jnp.ones((8, p0), BF)
    column = lambda ref, cols: jnp.dot(ones, ref[pl.ds(0, p0), cols], preferred_element_type=F32)[0:1, :]
    base = slots
    small_out[base + 2 : base + 3, :] = column(gm, my_quarter)
    small_out[base + 5 : base + 6, :] = column(gd, my_quarter)
    small_out[base + 3 : base + 4, :] = jnp.sum(fsum[pl.ds(0, 8), my_quarter], axis=0, keepdims=True)
    small_out[base + 4 : base + 5, :] = jnp.sum(fsum[pl.ds(8, 8), my_quarter], axis=0, keepdims=True)
    small_out[base + 6 : base + 7, :] = column(dqkv, pl.ds(0, nq))
    small_out[base + 7 : base + 8, :] = column(dqkv, pl.ds(2 * nq, nq)) + jnp.sum(
        dqkv[pl.ds(p0, slots), pl.ds(2 * nq, nq)].astype(F32), axis=0, keepdims=True
    )
    for k in range(nu // quarter):
        small_out[base + 8 + k : base + 9 + k, :] = column(db, pl.ds(k * quarter, quarter))
    small_out[base + 12 : base + 16, :] = jnp.zeros((4, quarter), F32)
    a12.finish()
    a12.done()
    rows_back(a12, 0)
    small_out[pl.ds(0, slots), :] = emb_wide[:, my_quarter]
    its_quarter = pl.ds(pl.multiple_of(t * half + (1 - s) * quarter, quarter), quarter)
    gx_send[0:1, :] = jnp.sum(gsum[pl.ds(0, 8), its_quarter], axis=0, keepdims=True)
    gx_send[1:2, :] = jnp.sum(gsum[pl.ds(8, 8), its_quarter], axis=0, keepdims=True)
    gx_send[2:8, :] = jnp.zeros((6, quarter), F32)
    copy = remote(gx_send, gx_recv, at_x)
    copy.wait()
    small_out[base : base + 1, :] = gx_recv[0:1, :] + jnp.sum(gsum[pl.ds(0, 8), my_quarter], axis=0, keepdims=True)
    small_out[base + 1 : base + 2, :] = gx_recv[1:2, :] + jnp.sum(gsum[pl.ds(8, 8), my_quarter], axis=0, keepdims=True)
    stage = [local(la_hbm, rows)]
    small_step(0)
    pass_on(gifts_a)
    a_second(1)
    share_qkv(0, own)
    b_second(0)
    b_second(1)
    a_first(2)
    a_third(0, 0)
    pass_on(gifts_b)
    stage.append(local(ra_hbm.at[pl.ds(s0, own), :], qkv.at[pl.ds(s0, own), :]))
    a_first(3)
    for copy in stage:
        copy.wait()

    def turn(it, lag, first, count, stage):
        @pl.when((it >= first + lag) & (it < lag + count))
        def _():
            stage(it - lag)

    turns = max(tiles_a + 2 * nh + 2, tiles_b + 2 * nh + 1)

    @pl.loop(0, turns)
    def _(it):
        turn(it, -4, 4, tiles_a, a_first)
        turn(it, -2, 2, tiles_b, b_first)
        turn(it, -2, 2, tiles_a, a_second)
        turn(it, -1, 2, tiles_b, b_second)
        for k in range(nh):
            turn(it, 2 * k, 0 if k else 1, tiles_a, functools.partial(a_third, k))
        turn(it, 2 * nh, 0, tiles_a, a_fourth)
        turn(it, 2 * nh + 2, 0, tiles_a, a_fifth)
        for k in range(nh):
            turn(it, 1 + 2 * k, 0, tiles_b, functools.partial(b_third, k))
        turn(it, 1 + 2 * nh, 0, tiles_b, b_fourth)
        for k in range(1, len(small_partners) + 1):

            @pl.when(it == 2 * k - 1)
            def _():
                small_step(k)

    @pl.loop(0, tiles_a)
    def _(i):
        for copy in outs_a(i, range(4)):
            copy.wait()

    @pl.loop(0, tiles_b)
    def _(i):
        for copy in outs_b(i, range(2)):
            copy.wait()

def chain(count, emb, dsum, feat_vecs, bq, bv, bu, hid, dhid, wq, wk, wv, wo, wu, wd):
    bits = lax.axis_size("batch").bit_length() - 1
    toks, slots = hid.shape[1], emb.shape[0] + -emb.shape[0] % 64
    half = hid.shape[2]
    feats, quarter = 2 * half, half // 2
    nq, nu = wo.shape[0] // 2, wd.shape[0] // 2
    own = 2 * toks + slots
    main, end = 2 * own, 2 * own + slots
    sums = 2 * slots + 2 * toks + 2 * own
    chunk = feats >> bits
    nh = bits - 2
    ta, tb = 2 * nu // nq, 8
    vm = pltpu.VMEM
    sds = jax.ShapeDtypeStruct
    dma = pltpu.SemaphoreType.DMA
    scratch = [
        vm((feats, 3 * nq), BF),
        vm((nq, feats), BF),
        vm((feats, nu), BF),
        vm((nu, feats), BF),
        vm((end, feats), BF),
        vm((end, feats), BF),
        vm((end, 3 * nq), BF),
        vm((2, nq // HD, own, own + slots), BF),
        vm((main, nq), BF),
        vm((main, feats), F32),
        vm((main, feats), BF),
        vm((main, nu), BF),
        vm((main, nu), BF),
        vm((slots, nu), F32),
        vm((main, feats), BF),
        vm((main, feats), BF),
        vm((main, nq), BF),
        vm((end, 3 * nq), BF),
        vm((2 * slots, feats), BF),
        vm((8, feats), F32),
        vm((1, 3 * nq + nu), F32),
        vm((end, 128), F32),
        vm((3, toks, half), F32),
        vm((16, feats), F32),
        vm((16, feats), F32),
        vm((8, quarter), F32),
        vm((8, quarter), F32),
        vm((sums + 2 * toks + own, half), BF),
        vm((sums + 2 * toks + own, half), BF),
        vm((sums + 2 * toks + own, half), BF),
        vm((sums, feats), BF),
        vm((2 * toks + own, half), BF),
        vm((2, main, feats), BF),
        vm((main, nu), BF),
        vm((2 * chunk if chunk % 128 else 8, nq // 2), F32),
        vm((slots + 16, quarter), F32),
        vm((bits + 1, slots + 16, quarter), F32),
        dma((6,)),
        dma((24,)),
        dma((192, 2)),
        pltpu.SemaphoreType.REGULAR((3 + nh,)),
        dma((ta, 2)),
        dma((nh, ta, 2)),
        dma((ta, 2)),
        dma((ta, 2, 2)),
        dma((tb, 2)),
        dma((nh, tb, 2)),
        dma((tb, 2)),
        dma((ta, 4)),
        dma((tb, 2)),
        dma((bits + 1, 2)),
    ]
    vmem = pl.BlockSpec(memory_space=pltpu.VMEM)
    hbm = pl.BlockSpec(memory_space=pl.ANY)
    smem = pl.BlockSpec(memory_space=pltpu.SMEM)
    return pl.pallas_call(
        functools.partial(chain_kernel, bits),
        name="layer",
        out_shape=(
            sds((2, toks, half), BF),
            sds((2, slots, half), BF),
            sds((2, toks, half), F32),
            sds((2, slots + 16, quarter), F32),
            sds((chunk // 2, 8 * nq + 4 * nu), BF),
            sds((end, feats), BF),
            sds((main, feats), BF),
            sds((end, 3 * nq), BF),
            sds((main, nq), BF),
        ),
        in_specs=[smem, vmem, vmem, [vmem] * 6, vmem, vmem, vmem] + [hbm] * 8,
        out_specs=(vmem,) * 4 + (hbm,) * 5,
        scratch_shapes=scratch,
        compiler_params=pltpu.CompilerParams(
            collective_id=2, has_side_effects=True, vmem_limit_bytes=63 * 2**20
        ),
    )(count, emb, dsum, feat_vecs, bq, bv, bu, hid, dhid, wq, wk, wv, wo, wu, wd)


def place_kernel(hid, sums, gin, small, w, hid_o, sum_o, gin_o, emb_o, vec_o, bup_o, q_o, k_o, v_o, o_o, u_o, d_o):
    hid_o[0] = hid[...]
    used = sum_o.shape[0]
    for seg in range(2):
        sum_o[:, seg, :] = sums[seg, :used, :]
    gin_o[0] = gin[...]
    quarter = small.shape[2]
    base = small.shape[1] - 16
    nu = bup_o.shape[0] // 2
    for side in range(2):
        at = pl.ds(side * quarter, quarter)
        emb_o[:, at] = small[side, :used, :]
        for k, ref in enumerate(vec_o):
            ref[at] = small[side, base + k]
        for k in range(nu // quarter):
            bup_o[pl.ds(side * nu + k * quarter, quarter)] = small[side, base + 8 + k]
    n = q_o.shape[1]
    for k, ref in enumerate((q_o, k_o, v_o)):
        ref[...] = w[:, k * n : (k + 1) * n].astype(F32)
    o_o[...] = w[:, 3 * n : 4 * n].astype(F32).T
    u_o[...] = w[:, 4 * n : 4 * n + 2 * nu].astype(F32)
    d_o[...] = w[:, 4 * n + 2 * nu :].astype(F32).T


def place(hid, sums, gin, small, w, used):
    sds = jax.ShapeDtypeStruct
    _, toks, half = hid.shape
    rows = w.shape[0]
    nu = (w.shape[1] - 4 * half) // 4
    vmem = pl.BlockSpec(memory_space=pltpu.VMEM)
    return pl.pallas_call(
        place_kernel,
        name="place",
        out_shape=(
            sds((1, 2, toks, half), BF),
            sds((used, 2, half), BF),
            sds((1, 2, toks, half), F32),
            sds((used, half), F32),
            [sds((half,), F32)] * 8,
            sds((2 * nu,), F32),
            sds((rows, half), F32),
            sds((rows, half), F32),
            sds((rows, half), F32),
            sds((half, rows), F32),
            sds((rows, 2 * nu), F32),
            sds((2 * nu, rows), F32),
        ),
        in_specs=[vmem] * 5,
        out_specs=(vmem,) * 4 + ([vmem] * 8,) + (vmem,) * 7,
        compiler_params=pltpu.CompilerParams(vmem_limit_bytes=60 * 2**20),
    )(hid, sums, gin, small, w)


def local(
    hidden_in, summary_counts, summary_embed, ln1_gain, ln1_bias, w_query, b_query, w_key, w_value,
    b_value, w_out, b_out, ln2_gain, ln2_bias, w_up, b_up, w_down, b_down, d_hidden, d_summary,
):
    got = chain(
        summary_counts, summary_embed, d_summary[0].transpose(1, 0, 2),
        [ln1_gain, ln1_bias, ln2_gain, ln2_bias, b_out, b_down], b_query, b_value, b_up,
        hidden_in[0], d_hidden[0], w_query, w_key, w_value, w_out, w_up, w_down,
    )
    hid, sums, gin, emb, vecs, bup, gq, gk, gv, go, gu, gd = place(*got[:5], summary_embed.shape[0])
    return (
        hid, sums.transpose(1, 0, 2)[None], gin, emb, vecs[0], vecs[1], gq, vecs[6], gk, gv,
        vecs[7], go, vecs[2], vecs[3], vecs[4], gu, bup, gd, vecs[5],
    )


def solution(mesh):
    return jax.shard_map(
        local,
        mesh=mesh,
        in_specs=(
            P("batch", None, "seq", "tensor"),
            P("batch"),
            P(None, "tensor"),
            P("tensor"),
            P("tensor"),
            P(None, "tensor"),
            P("tensor"),
            P(None, "tensor"),
            P(None, "tensor"),
            P("tensor"),
            P("tensor", None),
            P("tensor"),
            P("tensor"),
            P("tensor"),
            P(None, "tensor"),
            P("tensor"),
            P("tensor", None),
            P("tensor"),
            P("batch", None, "seq", "tensor"),
            P("batch", None, None, "tensor"),
        ),
        out_specs=(
            P("batch", None, "seq", "tensor"),
            P("batch", None, None, "tensor"),
            P("batch", None, "seq", "tensor"),
            P(None, "tensor"),
            P("tensor"),
            P("tensor"),
            P(("batch", "seq"), "tensor"),
            P("tensor"),
            P(("batch", "seq"), "tensor"),
            P(("batch", "seq"), "tensor"),
            P("tensor"),
            P("tensor", ("batch", "seq")),
            P("tensor"),
            P("tensor"),
            P("tensor"),
            P(("batch", "seq"), "tensor"),
            P("tensor"),
            P("tensor", ("batch", "seq")),
            P("tensor"),
        ),
        check_vma=False,
    )
```

```python
import functools

import jax
import jax.numpy as jnp
from jax import lax
from jax.experimental import pallas as pl
from jax.experimental.pallas import tpu as pltpu
from jax.sharding import PartitionSpec as P

HD = 64
EPSILON = 1e-05
NEGATIVE = -1e30
MESH = pl.DeviceIdType.MESH
BF = jnp.bfloat16
F32 = jnp.float32
PAIR_BIT = 1


def flip(index, bit):
    weight = 1 << bit
    return index + weight - 2 * weight * lax.rem(index // weight, 2)


def bit_of(index, bit):
    return lax.rem(index // (1 << bit), 2)


def dot_nt(a, b):
    return lax.dot_general(a, b, (((1,), (1,)), ((), ())), preferred_element_type=F32)


def dot_tn(a, b):
    return lax.dot_general(a, b, (((0,), (0,)), ((), ())), preferred_element_type=F32)


class Strips:
    def __init__(self, refs, width):
        self.width = width
        self.free = [[ref, ref.shape[0], at, 0] for ref in refs for at in range(ref.shape[1] // width)]

    def take(self, tiles, n, unit):
        for k, (ref, height, at, used) in enumerate(self.free):
            if height < n:
                continue
            if used + tiles * n <= height:
                self.free[k][3] += tiles * n
                return Slab(ref, at, used, tiles, n, unit, self.width)
            per = height // n
            need = -(-tiles // per)
            run = self.free[k : k + need]
            if len(run) == need and all(r[0] is ref and r[3] == 0 for r in run):
                for r in run:
                    r[3] = height
                run[-1][3] = (tiles - per * (need - 1)) * n
                return Slab(ref, at, 0, per, n, unit, self.width)
        raise ValueError("no room")


class Slab:
    def __init__(self, ref, strip, start, per, n, unit, width):
        self.ref, self.strip, self.start, self.per = ref, strip, start, per
        self.n, self.unit, self.width = n, unit, width

    def at(self, i, lo, n):
        first = pl.multiple_of(self.start + (i % self.per) * self.n + lo, self.unit)
        col = pl.multiple_of((self.strip + i // self.per) * self.width, self.width)
        return self.ref.at[pl.ds(first, n), pl.ds(col, self.width)]

    def __call__(self, i):
        return self.at(i, 0, self.n)


def chain_kernel(
    bits,
    count_ref,
    emb_ref,
    dsum_ref,
    feat_refs,
    bq_ref,
    bv_ref,
    bu_ref,
    hid_hbm,
    dhid_hbm,
    wq_hbm,
    wk_hbm,
    wv_hbm,
    wo_hbm,
    wu_hbm,
    wd_hbm,
    hid_out,
    sum_out,
    gin_hbm,
    small_final,
    w_hbm,
    la_hbm,
    lm_hbm,
    ra_hbm,
    mx_hbm,
    ye_hbm,
    ls_hbm,
    rs_hbm,
    wqkv,
    wo,
    wu,
    wd,
    rows,
    act1,
    qkv,
    probs,
    mix,
    mid,
    act2,
    actv,
    db,
    slope0,
    gd,
    gm,
    dmix,
    dqkv,
    dsum,
    vec,
    bias,
    stat,
    outacc,
    fsum,
    gsum,
    gx_send,
    gx_recv,
    ar_send,
    ar_core,
    ar_x,
    ar_full,
    ar_own,
    lxx,
    rbx,
    both,
    small_out,
    wsem,
    lsem,
    rsem,
    free,
    sem_y,
    sem_za,
    sem_pa,
    sem_xa,
    sem_pb,
    sem_zb,
    sem_xb,
    sem_oa,
    sem_ob,
    sem_s,
    early,
):
    b, s, t = lax.axis_index("batch"), lax.axis_index("seq"), lax.axis_index("tensor")
    at_core = (b, s, 1 - t)
    at_x = (b, 1 - s, t)
    at_p = (flip(b, PAIR_BIT), s, t)
    at_y = (flip(b, 0), s, t)
    halving = list(range(bits - 1, PAIR_BIT, -1))
    at_h = [(flip(b, bit), s, t) for bit in halving]
    zl, y = bit_of(b, PAIR_BIT), bit_of(b, 0)
    halving_down = list(range(bits - 2, 0, -1))
    at_d = (flip(b, bits - 1), s, t)
    zd = bit_of(b, bits - 1)
    barrier = pltpu.get_barrier_semaphore()
    partners = [at_core, at_x, at_p, at_y] + at_h
    for partner in partners:
        pl.semaphore_signal(barrier, inc=1, device_id=partner, device_id_type=MESH)

    toks = hid_hbm.shape[1]
    slots = slope0.shape[0]
    used = emb_ref.shape[0]
    feats = rows.shape[1]
    half = feats // 2
    quarter = feats // 4
    span = 2 * toks
    s0, t0, t1, s1, p0 = 0, slots, slots + span, slots + 2 * span, 2 * slots + 2 * span
    own = slots + span
    end = p0 + slots
    nq = wo.shape[0]
    nu = wu.shape[1]
    my_cols = pl.ds(pl.multiple_of(t * half, half), half)
    its_cols = pl.ds(pl.multiple_of((1 - t) * half, half), half)
    my_toks = pl.multiple_of(s * toks, toks)
    its_toks = pl.multiple_of((1 - s) * toks, toks)
    my_quarter = pl.ds(pl.multiple_of(t * half + s * quarter, quarter), quarter)

    counter = {"l": 0, "r": 0}

    def local(src, dst):
        counter["l"] += 1
        copy = pltpu.make_async_copy(src, dst, lsem.at[counter["l"] - 1])
        copy.start()
        return copy

    def remote(src, dst, partner):
        counter["r"] += 1
        at = counter["r"] - 1
        copy = pltpu.make_async_remote_copy(
            src_ref=src,
            dst_ref=dst,
            send_sem=rsem.at[at, 0],
            recv_sem=rsem.at[at, 1],
            device_id=partner,
            device_id_type=MESH,
        )
        copy.start()
        return copy

    part = lambda ref, n, axis: (
        ref.at[:, pl.ds(pl.multiple_of(s * n, n), n)]
        if axis
        else ref.at[pl.ds(pl.multiple_of(s * n, n), n), :]
    )
    weights = []
    for at, (src, dst) in enumerate(
        (
            (part(wq_hbm, nq, 1), wqkv.at[:, pl.ds(0, nq)]),
            (part(wk_hbm, nq, 1), wqkv.at[:, pl.ds(nq, nq)]),
            (part(wv_hbm, nq, 1), wqkv.at[:, pl.ds(2 * nq, nq)]),
            (part(wo_hbm, nq, 0), wo),
            (part(wu_hbm, nu, 1), wu),
            (part(wd_hbm, nu, 0), wd),
        )
    ):
        copy = pltpu.make_async_copy(src, dst, wsem.at[at])
        weights.append(copy)

    firsts = []
    for seg, at in enumerate((t0, t1)):
        firsts.append(local(hid_hbm.at[seg], rows.at[pl.ds(at + my_toks, toks), my_cols]))
    laters = []
    for seg, at in enumerate((t0, t1)):
        laters.append(local(dhid_hbm.at[seg], gd.at[pl.ds(at + my_toks, toks), my_cols]))
    for copy in weights[:3]:
        copy.start()
    for at in (s0, s1):
        rows[pl.ds(at, slots), my_cols] = jnp.zeros((slots, half), BF)
        rows[pl.ds(at, used), my_cols] = emb_ref[...]
    for seg in range(2):
        dsum[pl.ds(seg * slots, slots), my_cols] = jnp.zeros((slots, half), BF)
        dsum[pl.ds(seg * slots, used), my_cols] = dsum_ref[:, seg, :]
    for k, ref in enumerate(feat_refs):
        vec[k : k + 1, my_cols] = ref[...].astype(F32)[None]
    pl.semaphore_wait(barrier, len(partners))

    def in_x(src, dst, at):
        return remote(src, dst.at[pl.ds(at + my_toks, toks), my_cols], at_x)

    def in_core(block):
        return remote(block, block, at_core)

    def in_pass(dst, at):
        return in_core(dst.at[pl.ds(at + its_toks, toks), my_cols])

    x_hid = [in_x(hid_hbm.at[0], rows, t0)]
    from_core = [
        in_core(rows.at[pl.ds(s0, slots), my_cols]),
        in_core(vec.at[:, my_cols]),
        remote(hid_hbm.at[0], rows.at[pl.ds(t0 + my_toks, toks), my_cols], at_core),
    ]
    late_core = [
        in_core(rows.at[pl.ds(s1, slots), my_cols]),
        remote(hid_hbm.at[1], rows.at[pl.ds(t1 + my_toks, toks), my_cols], at_core),
        in_core(dsum.at[:, my_cols]),
    ]
    for src, dst, at in ((dhid_hbm.at[0], gd, t0), (dhid_hbm.at[1], gd, t1)):
        late_core.append(remote(src, dst.at[pl.ds(at + my_toks, toks), my_cols], at_core))
    for copy in weights[3:]:
        copy.start()

    live_count = count_ref[0]
    row_live = (lax.broadcasted_iota(jnp.int32, (slots, 1), 0) < live_count).astype(F32)
    dqkv[pl.ds(p0, slots), pl.ds(0, nq)] = jnp.zeros((slots, nq), BF)
    bias[:, pl.ds(nq, nq)] = jnp.zeros((1, nq), F32)
    for ref, at, n in ((bq_ref, 0, nq), (bv_ref, 2 * nq, nq), (bu_ref, 3 * nq, nu)):
        x = ref[...].astype(F32)[None]
        bias[:, pl.ds(at, n)] = jnp.where(s == 0, x[:, :n], x[:, n:])
    fsum[...] = jnp.zeros_like(fsum)
    gsum[...] = jnp.zeros_like(gsum)

    step = 16
    inverse = 1.0 / feats

    def row_loop(start, n, body):
        @pl.loop(0, n // step)
        def _(i):
            body(pl.ds(pl.multiple_of(start + i * step, step), step))

    def mean(x):
        return jnp.sum(x, axis=1, keepdims=True) * inverse

    def stats(x):
        m = mean(x)
        return m, lax.rsqrt(mean(x * x) - m * m + EPSILON)

    def norm1(start, n):
        def body(at):
            x = rows[at, :].astype(F32)
            m, r = stats(x)
            act1[at, :] = ((x - m) * r * vec[0:1, :] + vec[1:2, :]).astype(BF)
            stat[at, 0:1] = m
            stat[at, 1:2] = r

        row_loop(start, n, body)

    def norm_back(d, xhat, r, gain):
        q = d * gain
        return r * (q - mean(q) - xhat * mean(q * xhat))

    def fold(x):
        return jnp.sum(x.reshape(step // 8, 8, x.shape[1]), axis=0)

    wide = 512

    def col_loop(n, body):
        @pl.loop(0, n // wide)
        def _(j):
            body(pl.multiple_of(j * wide, wide))

    def project(at, n, lo, hi):
        def body(c):
            cols = pl.ds(pl.multiple_of(lo + c, wide), wide)
            x = jnp.dot(act1[pl.ds(at, n), :], wqkv[:, cols], preferred_element_type=F32)
            qkv[pl.ds(at, n), cols] = (x + bias[:, cols]).astype(BF)

        col_loop(hi - lo, body)

    class Total:
        def __init__(self, n, at, full, pieces, own_at=0):
            self.n, self.at, self.full, self.own_at = n, at, full, own_at
            self.pieces = pieces

        def mine(self, r, n):
            if self.full is None:
                return ar_own.at[pl.ds(self.own_at + r, n), :]
            return ar_full.at[pl.ds(self.full + r, n), my_cols]

        def start(self, product):
            at = pl.ds(self.at, self.n)

            def other(c):
                x = product(pl.multiple_of((1 - t) * half + c, wide), wide)
                ar_send[at, pl.ds(c, wide)] = x.astype(BF)

            col_loop(half, other)
            self.core = remote(ar_send.at[at, :], ar_core.at[at, :], at_core)

            def this(c):
                x = product(pl.multiple_of(t * half + c, wide), wide)
                if self.full is None:
                    ar_own[pl.ds(self.own_at, self.n), pl.ds(c, wide)] = x.astype(BF)
                else:
                    cols = pl.ds(pl.multiple_of(t * half + c, wide), wide)
                    ar_full[pl.ds(self.full, self.n), cols] = x.astype(BF)

            col_loop(half, this)

        def middle(self):
            self.core.wait()
            self.xs = []
            for base, n, scatter in self.pieces:
                at = pl.ds(self.at + base, n)
                ar_core[at, :] = (
                    self.mine(base, n)[...].astype(F32) + ar_core[at, :].astype(F32)
                ).astype(BF)
                if scatter:
                    src = ar_core.at[pl.ds(self.at + base + its_toks, toks), :]
                    dst = ar_x.at[pl.ds(self.at + base, toks), :]
                else:
                    src, dst = ar_core.at[at, :], ar_x.at[at, :]
                self.xs.append(remote(src, dst, at_x))

        def sums(self, base, n, scatter):
            if scatter:
                near = ar_core[pl.ds(self.at + base + my_toks, toks), :]
                far = ar_x[pl.ds(self.at + base, toks), :]
            else:
                near = ar_core[pl.ds(self.at + base, n), :]
                far = ar_x[pl.ds(self.at + base, n), :]
            return near.astype(F32) + far.astype(F32)

        def finish(self):
            self.backs = []
            for (base, n, scatter), copy in zip(self.pieces, self.xs):
                copy.wait()
                n = toks if scatter else n
                block = ar_full.at[pl.ds(self.full + base, n), my_cols]
                block[...] = self.sums(base, n, scatter).astype(BF)
                self.backs.append(remote(block, block, at_core))

        def done(self):
            for copy in self.backs:
                copy.wait()

        def flow(self, body, before_last=lambda: None):
            self.backs = []
            for k, ((base, n, _), copy) in enumerate(zip(self.pieces, self.xs)):
                if k == len(self.pieces) - 1:
                    before_last()
                copy.wait()
                block = ar_full.at[pl.ds(self.full + base, n), my_cols]
                block[...] = self.sums(base, n, False).astype(BF)
                self.backs.append(remote(block, block, at_core))
                if k:
                    self.backs[k - 1].wait()
                    body(*self.pieces[k - 1][:2])
            self.backs[-1].wait()
            body(*self.pieces[-1][:2])

    whole = lambda n: [(i, 64, False) for i in range(0, n, 64)]

    def out_product(at, n):
        return lambda c, w: jnp.dot(
            mix[pl.ds(at, n), :], wo[:, pl.ds(c, w)], preferred_element_type=F32
        )

    def down_product(at, n):
        return lambda c, w: jnp.dot(
            actv[pl.ds(at, n), :], wd[:, pl.ds(c, w)], preferred_element_type=F32
        )

    def up_back(at, n):
        return lambda c, w: dot_nt(db[pl.ds(at, n), :], wu[pl.ds(c, w), :])

    def in_back(at, n, lo):
        return lambda c, w: dot_nt(
            dqkv[pl.ds(at, n), pl.ds(lo, 3 * nq - lo)], wqkv[pl.ds(c, w), pl.ds(lo, 3 * nq - lo)]
        )

    def enter_ffn(total, at, n, base=0):
        def body(i):
            r = pl.ds(pl.multiple_of(at + base + i * step, step), step)
            f = pl.ds(pl.multiple_of(total.full + base + i * step, step), step)
            x = rows[r, :].astype(F32) + ar_full[f, :].astype(F32) + vec[4:5, :]
            m, rs = stats(x)
            mid[r, :] = x
            act2[r, :] = ((x - m) * rs * vec[2:3, :] + vec[3:4, :]).astype(BF)
            stat[r, 2:3] = m
            stat[r, 3:4] = rs

        pl.loop(0, n // step)(body)

    def gelu(v):
        c = 0.7978845608028654
        th = jnp.tanh(c * (v + 0.044715 * (v * v * v)))
        act = 0.5 * v * (1.0 + th)
        sl = 0.5 * (1.0 + th) + (0.5 * c) * v * (1.0 - th * th) * (1.0 + (3 * 0.044715) * v * v)
        return act, sl

    def ffn(at, n, back, lo, hi):
        r = pl.ds(at, n)

        def body(c):
            c = pl.multiple_of(lo + c, wide)
            cols = pl.ds(c, wide)
            v = jnp.dot(act2[r, :], wu[:, cols], preferred_element_type=F32)
            act, sl = gelu(v + bias[:, pl.ds(pl.multiple_of(3 * nq + c, wide), wide)])
            actv[r, cols] = act.astype(BF)
            if back == 1:
                db[r, cols] = (sl * dot_nt(gd[r, :], wd[cols, :])).astype(BF)
            elif back == 2:
                db[r, cols] = (sl * db[r, cols].astype(F32)).astype(BF)
            else:
                slope0[:, cols] = sl

        col_loop(hi - lo, body)

    def leave_ffn(total, at, n, base=0):
        def body(i):
            r = pl.ds(pl.multiple_of(at + base + i * step, step), step)
            f = pl.ds(pl.multiple_of(total.full + base + i * step, step), step)
            d = ar_full[f, :].astype(F32)
            xhat = (mid[r, :] - stat[r, 2:3]) * stat[r, 3:4]
            fsum[pl.ds(0, 8), :] = fsum[pl.ds(0, 8), :] + fold(d * xhat)
            fsum[pl.ds(8, 8), :] = fsum[pl.ds(8, 8), :] + fold(d)
            dm = gd[r, :].astype(F32) + norm_back(d, xhat, stat[r, 3:4], vec[2:3, :])
            mid[r, :] = dm
            gm[r, :] = dm.astype(BF)

        pl.loop(0, n // step)(body)

    def mix_back(at, n):
        dmix[pl.ds(at, n), :] = dot_nt(gm[pl.ds(at, n), :], wo[...]).astype(BF)

    pairs = nq // (2 * HD)
    scale = HD**-0.5

    def seen(seg, keys):
        q = lax.broadcasted_iota(jnp.int32, (own, keys), 0)
        k = lax.broadcasted_iota(jnp.int32, (own, keys), 1)
        if seg == 0:
            q = jnp.where(q < slots, q + span, q - slots)
            slot = k
            token = k >= slots
            k = jnp.where(token, k - slots, k + span)
            return (k <= q) & (token | (slot < live_count))
        token = k < span
        ahead = k >= own
        slot = jnp.where(ahead, k - own, k - span)
        return (ahead | (k <= q)) & (token | (slot < live_count))

    def lanes(n):
        first = (lax.broadcasted_iota(jnp.int32, (n, 2 * HD), 1) < HD).astype(F32)
        return first.astype(BF), (1.0 - first).astype(BF)

    def attend(seg):
        at, keys = (s0, own) if seg == 0 else (t1, own + slots)
        q_rows, k_rows = pl.ds(at, own), pl.ds(at, keys)

        @pl.loop(0, pairs)
        def _(j):
            col = lambda g: pl.ds(pl.multiple_of(g * nq + j * 2 * HD, 2 * HD), 2 * HD)
            q, k, v = qkv[q_rows, col(0)], qkv[k_rows, col(1)], qkv[k_rows, col(2)]
            first = lanes(keys)
            allowed = seen(seg, keys)
            got = jnp.zeros((own, 2 * HD), F32)
            for h in range(2):
                pick = first[h]
                sc = dot_nt(q, k * pick) * scale
                sc = jnp.where(allowed, sc, NEGATIVE)
                e = jnp.exp(sc - jnp.max(sc, axis=1, keepdims=True))
                p = (e / jnp.sum(e, axis=1, keepdims=True)).astype(BF)
                probs[seg, 2 * j + h, :, pl.ds(0, keys)] = p
                got += jnp.dot(p, v * pick, preferred_element_type=F32)
            mix[q_rows, pl.ds(pl.multiple_of(j * 2 * HD, 2 * HD), 2 * HD)] = got.astype(BF)

    def attend_back(seg):
        at, keys = (s0, own) if seg == 0 else (t1, own + slots)
        q_rows, k_rows = pl.ds(at, own), pl.ds(at, keys)

        @pl.loop(0, pairs)
        def _(j):
            col = lambda g: pl.ds(pl.multiple_of(g * nq + j * 2 * HD, 2 * HD), 2 * HD)
            q, k, v = qkv[q_rows, col(0)], qkv[k_rows, col(1)], qkv[k_rows, col(2)]
            d = dmix[q_rows, pl.ds(pl.multiple_of(j * 2 * HD, 2 * HD), 2 * HD)]
            first_k, first_q = lanes(keys), lanes(own)
            dq = jnp.zeros((own, 2 * HD), F32)
            dk = jnp.zeros((keys, 2 * HD), F32)
            dv = jnp.zeros((keys, 2 * HD), F32)
            for h in range(2):
                pick_k, pick_q = first_k[h], first_q[h]
                p = probs[seg, 2 * j + h, :, pl.ds(0, keys)]
                pf = p.astype(F32)
                dp = dot_nt(d, v * pick_k)
                ds = (pf * (dp - jnp.sum(pf * dp, axis=1, keepdims=True))).astype(BF)
                dq += jnp.dot(ds, k * pick_k, preferred_element_type=F32)
                dk += dot_tn(ds, q * pick_q)
                dv += dot_tn(p, d * pick_q)
            dqkv[q_rows, col(0)] = (dq * scale).astype(BF)
            dqkv[k_rows, col(1)] = (dk * scale).astype(BF)
            dqkv[k_rows, col(2)] = dv.astype(BF)

    gifts_a, gifts_b, passed = [], [], []
    hu = nu // 2
    chunk = feats >> bits
    chunks = 1 << (bits - 1)

    def share_feats_a(op, src, at, n):
        landing = lxx.at[op, pl.ds(at, n), my_cols]
        partner = at_d if op else at_p
        gifts_a.append((remote(src.at[pl.ds(at, n), my_cols], landing, partner), landing))

    def share_units_a(op, src, at, n):
        side = zd if op else zl
        its = pl.ds(pl.multiple_of((1 - side) * hu, hu), hu)
        landing = rbx.at[pl.ds(at, n), pl.ds(op * hu, hu)]
        partner = at_d if op else at_p
        gifts_a.append((remote(src.at[pl.ds(at, n), its], landing, partner), None))

    y_blocks = [(my_cols, my_cols)]
    if chunk % 128 == 0:
        block = lambda c: pl.ds(pl.multiple_of(c * chunk, chunk), chunk)
        y_blocks = [2 * (t * chunks // 2 + m) for m in range(chunks // 2)]
        y_blocks = [(block(c + 1 - y), block(c + y)) for c in y_blocks]

    def share_feats_b(src, dst, at, n):
        for out, back in y_blocks:
            copy = remote(src.at[pl.ds(at, n), out], dst.at[pl.ds(at, n), out], at_y)
            gifts_b.append((copy, dst.at[pl.ds(at, n), back]))

    def share_units_b(src, dst, at, n):
        gifts_b.append((remote(src.at[pl.ds(at, n), :], dst.at[pl.ds(at, n), :], at_y), None))

    def pass_on(gifts, most=1000):
        while gifts and most:
            most -= 1
            copy, landing = gifts.pop(0)
            copy.wait()
            if landing is not None:
                passed.append(remote(landing, landing, at_core))

    def pass_end():
        while passed:
            passed.pop(0).wait()

    def share_thin(src, dst, at, n, partner):
        block = dst.at[pl.ds(at, n), my_quarter]
        return remote(src.at[pl.ds(at, n), my_quarter], block, partner)

    gifts_q, thin_act1, thin_act2 = [], [], []
    hq = nq // 2

    def share_qkv(at, n):
        for g in range(3):
            its = pl.ds(pl.multiple_of(g * nq + (1 - zl) * hq, hq), hq)
            landing = ra_hbm.at[pl.ds(at, n), pl.ds(g * hq, hq)]
            gifts_q.append(remote(dqkv.at[pl.ds(at, n), its], landing, at_p))

    share_mix = lambda at, n: share_units_b(mix, mx_hbm, at, n)
    share_actv = lambda at, n: share_units_a(0, actv, at, n)
    share_db = lambda at, n: share_units_a(1, db, at, n)

    width = nq // 2
    near = chunk // 2
    per = hu // width
    tiles_a, tiles_b = 2 * per + 3, nq // width
    assert per == 4 and hq == width

    def kind_of(i):
        later = (i // per + 1) // 2
        return 1 - later, later * (i % 2), (1 - later) * i + later * ((i - per) // 2)


    nh = len(halving)
    strips = Strips([wu, wd], width)
    recv_y = strips.take(tiles_a, chunks * chunk, near)
    slots_y = 4
    send_y = strips.take(slots_y, chunks * chunk, near)
    recv_za = [strips.take(tiles_a, chunks * chunk >> (k + 1), near) for k in range(nh)]
    recv_pb = strips.take(tiles_b, chunks * chunk // 2, near)
    recv_zb = [strips.take(tiles_b, chunks * chunk >> (k + 2), near) for k in range(nh)]
    recv_px = strips.take(tiles_a, 2 * chunk, near)
    send_zd = strips.take(per, chunks * chunk // 2, near)
    recv_xb = strips.take(tiles_b, near, near)
    strips = Strips([wqkv, wo], width)
    send_za = [strips.take(tiles_a, chunks * chunk >> (k + 1), near) for k in range(nh)]
    send_pb = strips.take(tiles_b, chunks * chunk // 2, near)
    send_zb = [strips.take(tiles_b, chunks * chunk >> (k + 2), near) for k in range(nh)]
    send_pa = strips.take(tiles_a, chunk, near)

    def linked(src, dst, sem, partner):
        return pltpu.make_async_remote_copy(
            src_ref=src,
            dst_ref=dst,
            send_sem=sem.at[0],
            recv_sem=sem.at[1],
            device_id=partner,
            device_id_type=MESH,
        )

    copy_y = lambda i: linked(send_y(i % slots_y), recv_y(i), sem_y.at[i], at_y)
    def by_kind(i, far, close):
        down, inner, _ = kind_of(i)
        return close + (1 - down - inner) * (far - close)

    def copy_za(k, i, down=False):
        to = by_kind(i, flip(b, halving_down[k]), flip(b, halving[k]))
        src = send_zd if down else send_za[k]
        return linked(src(i), recv_za[k](i), sem_za.at[k, i], (to, s, t))

    def copy_pa(i):
        to = by_kind(i, at_d[0], at_p[0])
        return linked(send_pa(i), recv_px.at(i, 0, chunk), sem_pa.at[i], (to, s, t))

    def place_bit(j, k, value):
        low = 1 << k
        return (j // low) * 2 * low + value * low + j % low

    copy_pb = lambda i: linked(send_pb(i), recv_pb(i), sem_pb.at[i], at_p)
    copy_zb = lambda k, i: linked(send_zb[k](i), recv_zb[k](i), sem_zb.at[k, i], at_h[k])

    def block_product(lefts, rights, c):
        def dots(cols):
            x = dot_tn(lefts[0](cols), rights[0])
            for left, right in zip(lefts[1:], rights[1:]):
                x = x + dot_tn(left(cols), right)
            return x

        if chunk % 128 == 0:
            return dots(pl.ds(pl.multiple_of(c * chunk, chunk), chunk))
        both[...] = dots(pl.ds(pl.multiple_of((c // 2) * 2 * chunk, 2 * chunk), 2 * chunk))
        return both[pl.ds(pl.multiple_of((c % 2) * chunk, chunk), chunk), :]

    main = p0

    def products_a(i, parts, early=False):
        down, inner, k = kind_of(i)
        tile = lambda c: pl.ds(pl.multiple_of(c, width), width)
        cases = (
            (gd, lxx.at[0], actv, zl * hu + k * width, rbx, k * width),
            (act2, lxx.at[1], db, zd * hu + k * width, rbx, hu + k * width),
            (act1, rows, dqkv, k * nq + zl * hq, qkv, k * width),
        )
        for op, (near_l, far_l, near_r, near_at, far_r, far_at) in enumerate(cases):

            @pl.when((1 - down) * (1 + inner) == op)
            def _():
                at = pl.ds(slots, main - slots) if early and op == 0 else slice(None)
                rights = [near_r[at, tile(near_at)], far_r[at, tile(far_at)]]
                lefts = [lambda cols: near_l[at, cols], lambda cols: far_l[at, cols]]
                if op == 0 and not early:
                    rights.append(ar_own[pl.ds(0, 2 * slots), tile(k * width)])
                    lefts.append(lambda cols: dsum[:, cols])
                for n, which, put, after in parts(op):

                    @pl.loop(0, n)
                    def _(j):
                        put(j, block_product(lefts, rights, which(j)))

                    after()

    def products_b(i, parts):
        cols = pl.ds(pl.multiple_of(i * width, width), width)
        r1, r2 = mix[:, cols], dmix[:, cols]
        l1, l2 = (lambda at: gm[:, at]), (lambda at: ar_full[pl.ds(0, p0), at])
        for n, which, put, after in parts:

            @pl.loop(0, n)
            def _(j):
                put(j, block_product((l1, l2), (r1, r2), which(j)))

            after()

    def copy_early(i):
        return linked(early.at[i % 2], ye_hbm.at[i], sem_y.at[i], at_y)

    def a_early(i):
        def put(j, v):
            early[i % 2, pl.ds(pl.multiple_of(j * chunk, chunk), chunk), :] = v.astype(BF)

        if i >= 2:
            copy_early(i - 2).wait_send()
        part = (chunks, lambda j: 2 * j + 1 - y, put, lambda: copy_early(i).start())
        products_a(i, lambda op: [part], True)

    def early_in(i):
        if i >= 2:
            copy_early(i).wait_send()
        copy_early(i).wait_recv()
        return local(ye_hbm.at[i], recv_y(i))

    def a_first(i):
        def put(j, v):
            send_y.at(i % slots_y, j * chunk, chunk)[...] = v.astype(BF)

        part = (chunks, lambda j: 2 * j + 1 - y, put, lambda: copy_y(i).start())
        products_a(i, lambda op: [part])

    def a_second(i, came=None):
        (copy_y(i) if came is None else came).wait()
        n = chunks // 2

        def parts(op):
            bit = bit_of(b, (halving_down if op == 1 else halving)[0])
            k = bits - 3 if op == 1 else bits - 2
            other = lambda j: place_bit(j, k, 1 - bit)
            mine = lambda j: place_bit(j, k, bit)

            def total(v, at):
                return (v + recv_y.at(i, at * chunk, chunk)[...].astype(F32)).astype(BF)

            def give(j, v):
                give_to = send_za[0] if op else send_zd
                give_to.at(i, j * chunk, chunk)[...] = total(v, other(j))

            def keep(j, v):
                x = total(v, mine(j))
                recv_y.at(i, j * chunk, chunk)[...] = x

            return [
                (n, lambda j: 2 * other(j) + y, give, lambda: copy_za(0, i, op == 0).start()),
                (n, lambda j: 2 * mine(j) + y, keep, lambda: None),
            ]

        products_a(i, parts)

    def halve(i, kept, at, recv, n, give, copy, k, bit):
        def total(c):
            x = kept.at(i, (at + c) * chunk, chunk)[...].astype(F32)
            return (x + recv.at(i, c * chunk, chunk)[...].astype(F32)).astype(BF)

        for j in range(n // 2):
            give.at(i, j * chunk, chunk)[...] = total(place_bit(j, k, 1 - bit))
        copy().start()
        for j in range(n // 2):
            x = total(place_bit(j, k, bit))
            kept.at(i, (at + n + j) * chunk, chunk)[...] = x

    ends_a = [0]
    for k in range(nh + 1):
        ends_a.append(ends_a[-1] + (chunks >> (k + 1)))

    def a_third(k, i):
        copy_za(k, i).wait()
        n = chunks >> (k + 1)
        if k + 1 == nh:
            side = by_kind(i, zd, zl)
            halve(i, recv_y, ends_a[k], recv_za[k], n, send_pa, lambda: copy_pa(i), 0, side)
            return
        for op in range(2):

            @pl.when(by_kind(i, 1, 0) == op)
            def _():
                bit = bit_of(b, (halving_down if op else halving)[k + 1])
                at = bits - 4 - k if op else bits - 3 - k
                after = lambda: copy_za(k + 1, i)
                halve(i, recv_y, ends_a[k], recv_za[k], n, send_za[k + 1], after, at, bit)

    my_near = pl.multiple_of(s * near, near)
    its_near = pl.multiple_of((1 - s) * near, near)
    kept_a = lambda i, at: recv_y.at(i, ends_a[nh] * chunk + at, near)

    def copies_xa(i):
        side = by_kind(i, zd, zl)
        return [
            linked(kept_a(i, its_near), recv_px.at(i, chunk + side * near, near), sem_xa.at[i, 0], at_x),
            linked(
                recv_px.at(i, its_near, near),
                recv_px.at(i, chunk + (1 - side) * near, near),
                sem_xa.at[i, 1],
                at_x,
            ),
        ]

    def outs_a(i, picks):
        def to(side, pair):
            down, inner, k = kind_of(i)
            ffn_col = 8 * nq + down * 2 * nu + side * nu + pair * hu + k * width
            col = (1 - inner) * ffn_col + inner * (k * 2 * nq + side * nq + pair * hq)
            return w_hbm.at[:, pl.ds(pl.multiple_of(col, width), width)]

        pieces = [
            (kept_a(i, my_near), to(s, by_kind(i, zd, zl))),
            (recv_px.at(i, my_near, near), to(s, 1 - by_kind(i, zd, zl))),
            (recv_px.at(i, chunk, near), to(1 - s, 0)),
            (recv_px.at(i, chunk + near, near), to(1 - s, 1)),
        ]
        return [pltpu.make_async_copy(*pieces[k], sem_oa.at[i, k]) for k in picks]

    def a_fourth(i):
        copy_pa(i).wait()
        for copy in copies_xa(i) + outs_a(i, (0, 1)):
            copy.start()

    def a_fifth(i):
        for copy in copies_xa(i):
            copy.wait()
        for copy in outs_a(i, (2, 3)):
            copy.start()

    def b_first(i):
        n = chunks // 2

        def put(j, v):
            send_pb.at(i, j * chunk, chunk)[...] = v.astype(BF)

        products_b(i, [(n, lambda j: 2 * (2 * j + 1 - zl) + y, put, lambda: copy_pb(i).start())])

    def b_second(i):
        copy_pb(i).wait()
        bit = bit_of(b, halving[0])
        n = chunks // 4

        def total(v, at):
            return (v + recv_pb.at(i, at * chunk, chunk)[...].astype(F32)).astype(BF)

        def give(j, v):
            send_zb[0].at(i, j * chunk, chunk)[...] = total(v, (1 - bit) * n + j)

        def keep(j, v):
            x = total(v, bit * n + j)
            recv_pb.at(i, j * chunk, chunk)[...] = x

        products_b(
            i,
            [
                (n, lambda j: 2 * (2 * ((1 - bit) * n + j) + zl) + y, give, lambda: copy_zb(0, i).start()),
                (n, lambda j: 2 * (2 * (bit * n + j) + zl) + y, keep, lambda: None),
            ],
        )

    ends_b = [0]
    for k in range(nh):
        ends_b.append(ends_b[-1] + (chunks >> (k + 2)))
    kept_b = lambda i, at: recv_pb.at(i, ends_b[nh] * chunk + at, near)

    def copy_xb(i):
        return linked(kept_b(i, its_near), recv_xb(i), sem_xb.at[i], at_x)

    def outs_b(i, picks):
        def to(side):
            col = 6 * nq + side * nq + i * width
            return w_hbm.at[:, pl.ds(pl.multiple_of(col, width), width)]

        pieces = [(kept_b(i, my_near), to(s)), (recv_xb(i), to(1 - s))]
        return [pltpu.make_async_copy(*pieces[k], sem_ob.at[i, k]) for k in picks]

    def b_third(k, i):
        copy_zb(k, i).wait()
        n = chunks >> (k + 2)
        if k + 1 < nh:
            bit = bit_of(b, halving[k + 1])
            after = lambda: copy_zb(k + 1, i)
            halve(i, recv_pb, ends_b[k], recv_zb[k], n, send_zb[k + 1], after, bits - 4 - k, bit)
        else:
            x = recv_pb.at(i, ends_b[k] * chunk, chunk)[...].astype(F32) + recv_zb[k](i)[...].astype(F32)
            recv_pb.at(i, ends_b[nh] * chunk, chunk)[...] = x.astype(BF)
            copy_xb(i).start()
            outs_b(i, (0,))[0].start()

    def b_fourth(i):
        copy_xb(i).wait()
        outs_b(i, (1,))[0].start()

    small_partners = [at_y] + at_h + [at_p, at_x]

    def small_in(k):
        at = pl.ds((k // 2) * small_out.shape[0], small_out.shape[0])
        return outacc.at[at, pl.ds((k % 2) * quarter, quarter)]

    def small_step(k):
        copy = lambda k: linked(small_out, small_in(k), sem_s.at[k], small_partners[k])
        if k > 0:
            copy(k - 1).wait()
            if k < len(small_partners):
                small_out[...] = small_out[...] + small_in(k - 1)[...]
        if k < len(small_partners):
            copy(k).start()
        else:
            small_final[s] = small_out[...]
            small_final[1 - s] = small_in(k - 1)[...]

    for copy in firsts + from_core:
        copy.wait()
    norm1(s0, slots)
    norm1(t0 + my_toks, toks)
    x_hid[0].wait()
    forward = in_pass(rows, t0)
    x_hid.append(in_x(hid_hbm.at[1], rows, t1))
    x_dhid = [in_x(dhid_hbm.at[0], gd, t0), in_x(dhid_hbm.at[1], gd, t1)]
    forward.wait()
    norm1(t0 + its_toks, toks)
    thin_act1.append(share_thin(act1, la_hbm, 0, own, at_p))
    for copy in weights[:3]:
        copy.wait()
    project(0, own, 0, 3 * nq)
    attend(0)
    share_mix(0, own)
    for copy in weights[3:4]:
        copy.wait()
    T = span
    a1 = Total(slots, 0, 0, whole(slots))
    a2 = Total(T, 2 * slots, 2 * slots, whole(T))
    a1.start(out_product(s0, slots))
    a2.start(out_product(t0, T))
    a1.middle()
    a2.middle()
    x_hid[1].wait()
    forward = in_pass(rows, t1)
    for copy in late_core + laters:
        copy.wait()
    forward.wait()
    norm1(t1, own)
    thin_act1.append(share_thin(act1, la_hbm, t1, own, at_p))
    project(t1, own, 0, 3 * nq)
    a1.finish()
    a1.done()
    enter_ffn(a1, s0, slots)
    weights[4].wait()
    forwards = []
    for copy, at in zip(x_dhid, (t0, t1)):
        copy.wait()
        forwards.append(in_pass(gd, at))
    gd[pl.ds(s1, slots), :] = (dsum[pl.ds(slots, slots), :].astype(F32) * row_live).astype(BF)
    ffn(s0, slots, 0, 0, nu)
    for copy in forwards:
        copy.wait()
    share_feats_a(0, gd, t0, p0 - t0)
    weights[5].wait()
    a3 = Total(slots, slots, slots, whole(slots))
    a3.start(down_product(s0, slots))
    a2.finish()
    a3.middle()
    a2.done()
    enter_ffn(a2, t0, T)
    outacc[pl.ds(0 * toks, toks), :] = mid[pl.ds(t0 + my_toks, toks), my_cols]

    def early_before(c):
        cols, r = pl.ds(c, wide), pl.ds(t1, own)
        db[r, cols] = dot_nt(gd[r, :], wd[cols, :]).astype(BF)

    col_loop(nu, early_before)
    a3.finish()
    thin_act2.append(share_thin(act2, lxx.at[1], s0, own, at_d))
    a3.done()

    def summary(i):
        r = pl.ds(pl.multiple_of(s0 + i * step, step), step)
        f = pl.ds(pl.multiple_of(a3.full + i * step, step), step)
        p = pl.ds(pl.multiple_of(p0 + i * step, step), step)
        x = mid[r, :] + ar_full[f, :].astype(F32) + vec[5:6, :]
        on = (lax.broadcasted_iota(jnp.int32, (step, 1), 0) + i * step < live_count).astype(F32)
        rows[p, :] = (x * on).astype(BF)

    pl.loop(0, slots // step)(summary)
    sum_out[0] = rows[pl.ds(p0, slots), my_cols]
    norm1(p0, slots)
    thin_act1.append(share_thin(act1, la_hbm, p0, slots, at_p))
    project(p0, slots, nq, 3 * nq)
    attend(1)
    share_mix(t1, own)
    a5 = Total(own, 2 * slots + T, 2 * slots + T, whole(own))
    a5.start(out_product(t1, own))
    ffn(t0, T, 1, 0, nu // 4)
    a5.middle()
    ffn(t0, T, 1, nu // 4, nu)
    share_actv(s0, own)
    side = pl.ds(pl.multiple_of(zl * hu, hu), hu)
    rs_own = remote(actv.at[pl.ds(s0, slots), side], rs_hbm.at[pl.ds(0, slots), :], at_y)
    a6 = Total(T, 2 * slots, 2 * slots, whole(T))
    a6.start(up_back(t0, T))
    a6.middle()
    a4 = Total(T, 2 * slots + T + 2 * own, None, [(0, T, True)], 0)
    a4.start(down_product(t0, T))
    a5.flow(lambda base, n: enter_ffn(a5, t1, n, base))
    a4.middle()
    outacc[pl.ds(1 * toks, toks), :] = mid[pl.ds(t1 + my_toks, toks), my_cols]
    outacc[pl.ds(2 * toks, toks), :] = mid[pl.ds(s1, slots), my_cols]
    pass_on(gifts_a, 1)
    ffn(t1, own, 2, 0, nu)
    share_actv(t1, own)
    a8 = Total(own, 2 * slots + T + own, 2 * slots + T + own, whole(own))
    a8.start(up_back(t1, own))
    a6.finish()
    a8.middle()
    a7 = Total(own, 2 * slots + 2 * T + 2 * own, None, [(0, T, True), (T, slots, False)], T)
    a7.start(down_product(t1, own))
    a6.done()
    leave_ffn(a6, t0, T)
    mix_back(t0, T)
    share_feats_b(gm, lm_hbm, t0, T)

    def begin_down():
        pass_on(gifts_a)
        pass_end()
        a_early(0)
        thin_act2.append(share_thin(act2, lxx.at[1], t1, own, at_d))
        share_db(t0, T)
        share_db(t1, own)

    a8.flow(lambda base, n: leave_ffn(a8, t1, n, base), begin_down)
    far = rbx.at[pl.ds(s0, slots), pl.ds(0, hu)]
    rs_far = remote(far, rs_hbm.at[pl.ds(slots, slots), :], at_y)
    a7.middle()
    mix_back(t1, own)
    share_feats_b(gm, lm_hbm, t1, own)
    attend_back(1)
    a9 = Total(slots, 0, 0, whole(slots))
    a9.start(in_back(p0, slots, nq))
    a10 = Total(own, 2 * slots + T, 2 * slots + T, [(0, T, True), (T, slots, False)])
    a9.middle()
    a10.start(in_back(t1, own, 0))
    a9.finish()
    a10.middle()
    for copy in a4.xs + a7.xs:
        copy.wait()
    hid_out[0] = (outacc[pl.ds(0 * toks, toks), :] + a4.sums(0, T, True) + vec[5:6, my_cols]).astype(BF)
    hid_out[1] = (outacc[pl.ds(1 * toks, toks), :] + a7.sums(0, T, True) + vec[5:6, my_cols]).astype(BF)
    sum_out[1] = (
        (outacc[pl.ds(2 * toks, toks), :] + a7.sums(T, slots, False) + vec[5:6, my_cols]) * row_live
    ).astype(BF)
    a9.done()
    first_only = (s == 0).astype(F32)

    def norm1_back(r, f, weight):
        d = ar_full[f, :].astype(F32)
        xhat = (rows[r, :].astype(F32) - stat[r, 0:1]) * stat[r, 1:2]
        gsum[pl.ds(0, 8), :] = gsum[pl.ds(0, 8), :] + fold(d * xhat) * weight
        gsum[pl.ds(8, 8), :] = gsum[pl.ds(8, 8), :] + fold(d) * weight
        return norm_back(d, xhat, stat[r, 1:2], vec[0:1, :])

    def prefix_back(i):
        r = pl.ds(pl.multiple_of(p0 + i * step, step), step)
        f = pl.ds(pl.multiple_of(a9.full + i * step, step), step)
        g = pl.ds(pl.multiple_of(s0 + i * step, step), step)
        on = (lax.broadcasted_iota(jnp.int32, (step, 1), 0) + i * step < live_count).astype(F32)
        d = norm1_back(r, f, first_only)
        gd[g, :] = ((dsum[pl.ds(pl.multiple_of(i * step, step), step), :].astype(F32) + d) * on).astype(BF)

    pl.loop(0, slots // step)(prefix_back)
    before_gifts = len(gifts_a)
    share_feats_a(0, gd, s0, slots)
    late_gifts = gifts_a.pop(before_gifts)
    ls_near = [
        remote(gd.at[pl.ds(s0, slots), out], ls_hbm.at[pl.ds(0, slots), out], at_y)
        for out, _ in y_blocks
    ]

    def last_before(c):
        cols = pl.ds(c, wide)
        r = pl.ds(s0, slots)
        db[r, cols] = (slope0[:, cols] * dot_nt(gd[r, :], wd[cols, :])).astype(BF)

    col_loop(nu, last_before)
    share_db(s0, slots)
    a11 = Total(slots, slots, slots, whole(slots))
    a11.start(up_back(s0, slots))
    askers = [at_x, at_p, at_y] + at_h
    for k, partner in enumerate(askers):
        pl.semaphore_signal(free.at[k], inc=1, device_id=partner, device_id_type=MESH)
    a10.finish()
    a11.middle()
    late_gifts[0].wait()
    share_qkv(t1, own + slots)
    passed.append(remote(late_gifts[1], late_gifts[1], at_core))
    ls_far = [
        remote(lxx.at[0, pl.ds(s0, slots), out], ls_hbm.at[pl.ds(slots, slots), out], at_y)
        for out, _ in y_blocks
    ]
    a10.done()
    gin_copies = []

    def rows_back(total, seg):
        t_at, s_at = (t0, s0) if seg == 0 else (t1, s1)
        t_in, s_in = (slots, 0) if seg == 0 else (0, span)

        def tokens(i):
            r = pl.ds(pl.multiple_of(t_at + my_toks + i * step, step), step)
            f = pl.ds(pl.multiple_of(total.full + t_in + i * step, step), step)
            x = norm1_back(r, f, 1.0)
            mid[r, :] = mid[r, :] + x

        pl.loop(0, toks // step)(tokens)
        gin_copies.append(local(mid.at[pl.ds(t_at + my_toks, toks), my_cols], gin_hbm.at[seg]))

        def summaries(i):
            r = pl.ds(pl.multiple_of(s_at + i * step, step), step)
            f = pl.ds(pl.multiple_of(total.full + s_in + i * step, step), step)
            x = norm1_back(r, f, first_only) + mid[r, :]
            e = pl.ds(pl.multiple_of(i * step, step), step)
            emb_wide[e, :] = x if seg == 1 else emb_wide[e, :] + x

        pl.loop(0, slots // step)(summaries)

    emb_wide = slope0
    for copy in [rs_own, rs_far]:
        copy.wait()
    for copy in ls_near:
        copy.wait()
    for copy in ls_far:
        copy.wait()
    ls_core = remote(ls_hbm.at[:, my_cols], ls_hbm.at[:, my_cols], at_core)
    rs_in = local(rs_hbm, ar_own.at[pl.ds(0, 2 * slots), :])
    came = [early_in(0)]
    a_early(1)
    rows_back(a10, 1)
    pass_end()
    ls_core.wait()
    ls_in = local(ls_hbm, dsum)
    a11.finish()
    for k in range(len(askers)):
        pl.semaphore_wait(free.at[k], 1)
    a11.done()
    rs_in.wait()
    ls_in.wait()
    a_second(0, came[0])
    for copy in thin_act1:
        copy.wait()
    x_act1 = remote(la_hbm.at[:, my_quarter], la_hbm.at[:, my_quarter], at_x)
    leave_ffn(a11, s0, slots)
    mix_back(s0, slots)
    share_feats_b(gm, lm_hbm, s0, slots)
    a_early(2)
    attend_back(0)
    share_qkv(0, own)
    a12 = Total(own, 2 * slots + T + own, 2 * slots + T + own, [(0, slots, False), (slots, T, True)])
    a12.start(in_back(s0, own, 0))
    a12.middle()
    x_act1.wait()
    core_act1 = remote(la_hbm.at[:, my_cols], la_hbm.at[:, my_cols], at_core)
    a_second(1, early_in(1))
    a_early(3)
    for copy in thin_act2:
        copy.wait()
    to_x = remote(lxx.at[1, :, my_quarter], lxx.at[1, :, my_quarter], at_x)
    pass_on(gifts_b)
    stage = [local(mx_hbm, dmix)]
    pass_end()
    stage.append(local(lm_hbm, ar_full.at[pl.ds(0, p0), :]))
    a12.finish()
    for copy in stage:
        copy.wait()
    b_first(0)
    b_first(1)
    ones = jnp.ones((8, p0), BF)
    column = lambda ref, cols: jnp.dot(ones, ref[pl.ds(0, p0), cols], preferred_element_type=F32)[0:1, :]
    base = slots
    small_out[base + 2 : base + 3, :] = column(gm, my_quarter)
    small_out[base + 5 : base + 6, :] = column(gd, my_quarter)
    small_out[base + 3 : base + 4, :] = jnp.sum(fsum[pl.ds(0, 8), my_quarter], axis=0, keepdims=True)
    small_out[base + 4 : base + 5, :] = jnp.sum(fsum[pl.ds(8, 8), my_quarter], axis=0, keepdims=True)
    small_out[base + 6 : base + 7, :] = column(dqkv, pl.ds(0, nq))
    small_out[base + 7 : base + 8, :] = column(dqkv, pl.ds(2 * nq, nq)) + jnp.sum(
        dqkv[pl.ds(p0, slots), pl.ds(2 * nq, nq)].astype(F32), axis=0, keepdims=True
    )
    for k in range(nu // quarter):
        small_out[base + 8 + k : base + 9 + k, :] = column(db, pl.ds(k * quarter, quarter))
    small_out[base + 12 : base + 16, :] = jnp.zeros((4, quarter), F32)
    a12.done()
    rows_back(a12, 0)
    small_out[pl.ds(0, slots), :] = emb_wide[:, my_quarter]
    its_quarter = pl.ds(pl.multiple_of(t * half + (1 - s) * quarter, quarter), quarter)
    gx_send[0:1, :] = jnp.sum(gsum[pl.ds(0, 8), its_quarter], axis=0, keepdims=True)
    gx_send[1:2, :] = jnp.sum(gsum[pl.ds(8, 8), its_quarter], axis=0, keepdims=True)
    gx_send[2:8, :] = jnp.zeros((6, quarter), F32)
    copy = remote(gx_send, gx_recv, at_x)
    copy.wait()
    small_out[base : base + 1, :] = gx_recv[0:1, :] + jnp.sum(gsum[pl.ds(0, 8), my_quarter], axis=0, keepdims=True)
    small_out[base + 1 : base + 2, :] = gx_recv[1:2, :] + jnp.sum(gsum[pl.ds(8, 8), my_quarter], axis=0, keepdims=True)
    small_step(0)
    to_x.wait()
    to_core = remote(lxx.at[1, :, my_cols], lxx.at[1, :, my_cols], at_core)
    pass_on(gifts_a)
    to_core.wait()
    a_first(4)
    a_second(2, early_in(2))
    for copy in gifts_q:
        copy.wait()
    core_act1.wait()
    stage = [local(la_hbm, rows), local(ra_hbm, qkv.at[:, pl.ds(0, 3 * hq)])]
    a_third(0, 0)
    for copy in stage:
        copy.wait()
    a_second(3, early_in(3))
    a_first(5)
    a_third(0, 1)

    def turn(it, lag, first, count, stage):
        @pl.when((it >= first + lag) & (it < lag + count))
        def _():
            stage(it - lag)

    turns = tiles_a + 2 * nh

    @pl.loop(0, turns)
    def _(it):
        turn(it, -4, 4, tiles_a, a_second)
        turn(it, -6, 6, tiles_a, a_first)
        turn(it, 1, 0, tiles_b, b_second)
        for k in range(nh):
            turn(it, 2 * k - 2, 0 if k else 2, tiles_a, functools.partial(a_third, k))
        turn(it, 2 * nh - 2, 0, tiles_a, a_fourth)
        turn(it, 2 * nh, 0, tiles_a, a_fifth)
        for k in range(nh):
            turn(it, 3 + 2 * k, 0, tiles_b, functools.partial(b_third, k))
        turn(it, 3 + 2 * nh, 0, tiles_b, b_fourth)
        for k in range(1, len(small_partners) + 1):

            @pl.when(it == 2 * k - 1)
            def _():
                small_step(k)

    assert counter["l"] <= lsem.shape[0] and counter["r"] <= rsem.shape[0]

    for copy in gin_copies:
        copy.wait()

    @pl.loop(0, tiles_a)
    def _(i):
        for copy in outs_a(i, range(4)):
            copy.wait()

    @pl.loop(0, tiles_b)
    def _(i):
        for copy in outs_b(i, range(2)):
            copy.wait()

def chain(count, emb, dsum, feat_vecs, bq, bv, bu, hid, dhid, wq, wk, wv, wo, wu, wd):
    bits = lax.axis_size("batch").bit_length() - 1
    toks, slots = hid.shape[1], emb.shape[0] + -emb.shape[0] % 64
    half = hid.shape[2]
    feats, quarter = 2 * half, half // 2
    nq, nu = wo.shape[0] // 2, wd.shape[0] // 2
    own = 2 * toks + slots
    main, end = 2 * own, 2 * own + slots
    sums = 2 * slots + 2 * toks + 2 * own
    chunk = feats >> bits
    nh = bits - 2
    ta, tb = 2 * nu // nq + 3, 2
    vm = pltpu.VMEM
    sds = jax.ShapeDtypeStruct
    dma = pltpu.SemaphoreType.DMA
    scratch = [
        vm((feats, 3 * nq), BF),
        vm((nq, feats), BF),
        vm((feats, nu), BF),
        vm((nu, feats), BF),
        vm((end, feats), BF),
        vm((end, feats), BF),
        vm((end, 3 * nq), BF),
        vm((2, nq // HD, own, own + slots), BF),
        vm((main, nq), BF),
        vm((main, feats), F32),
        vm((main, feats), BF),
        vm((main, nu), BF),
        vm((main, nu), BF),
        vm((slots, nu), F32),
        vm((main, feats), BF),
        vm((main, feats), BF),
        vm((main, nq), BF),
        vm((end, 3 * nq), BF),
        vm((2 * slots, feats), BF),
        vm((8, feats), F32),
        vm((1, 3 * nq + nu), F32),
        vm((end, 128), F32),
        vm((max(3 * toks, (slots + 16) * ((bits + 2) // 2)), half), F32),
        vm((16, feats), F32),
        vm((16, feats), F32),
        vm((8, quarter), F32),
        vm((8, quarter), F32),
        vm((sums + 2 * toks + own, half), BF),
        vm((sums + 2 * toks + own, half), BF),
        vm((sums + 2 * toks + own, half), BF),
        vm((sums, feats), BF),
        vm((2 * toks + own, half), BF),
        vm((2, main, feats), BF),
        vm((main, nu), BF),
        vm((2 * chunk if chunk % 128 else 8, nq // 2), F32),
        vm((slots + 16, quarter), F32),
        dma((6,)),
        dma((16,)),
        dma((113, 2)),
        pltpu.SemaphoreType.REGULAR((3 + nh,)),
        dma((ta, 2)),
        dma((nh, ta, 2)),
        dma((ta, 2)),
        dma((ta, 2, 2)),
        dma((tb, 2)),
        dma((nh, tb, 2)),
        dma((tb, 2)),
        dma((ta, 4)),
        dma((tb, 2)),
        dma((bits + 1, 2)),
        vm((2, feats // 2, nq // 2), BF),
    ]
    vmem = pl.BlockSpec(memory_space=pltpu.VMEM)
    hbm = pl.BlockSpec(memory_space=pl.ANY)
    smem = pl.BlockSpec(memory_space=pltpu.SMEM)
    return pl.pallas_call(
        functools.partial(chain_kernel, bits),
        name="layer",
        out_shape=(
            sds((2, toks, half), BF),
            sds((2, slots, half), BF),
            sds((2, toks, half), F32),
            sds((2, slots + 16, quarter), F32),
            sds((chunk // 2, 8 * nq + 4 * nu), BF),
            sds((end, feats), BF),
            sds((main, feats), BF),
            sds((end, 3 * nq // 2), BF),
            sds((main, nq), BF),
            sds((4, feats // 2, nq // 2), BF),
            sds((2 * slots, feats), BF),
            sds((2 * slots, nu // 2), BF),
        ),
        in_specs=[smem, vmem, vmem, [vmem] * 6, vmem, vmem, vmem] + [hbm] * 8,
        out_specs=(vmem, vmem, hbm, vmem) + (hbm,) * 8,
        scratch_shapes=scratch,
        compiler_params=pltpu.CompilerParams(
            collective_id=2, has_side_effects=True, vmem_limit_bytes=63 * 2**20
        ),
    )(count, emb, dsum, feat_vecs, bq, bv, bu, hid, dhid, wq, wk, wv, wo, wu, wd)


def place_kernel(hid, sums, gin, small, w, hid_o, sum_o, gin_o, emb_o, vec_o, bup_o, q_o, k_o, v_o, o_o, u_o, d_o):
    hid_o[0] = hid[...]
    used = sum_o.shape[0]
    for seg in range(2):
        sum_o[:, seg, :] = sums[seg, :used, :]
    gin_o[0] = gin[...]
    quarter = small.shape[2]
    base = small.shape[1] - 16
    nu = bup_o.shape[0] // 2
    for side in range(2):
        at = pl.ds(side * quarter, quarter)
        emb_o[:, at] = small[side, :used, :]
        for k, ref in enumerate(vec_o):
            ref[at] = small[side, base + k]
        for k in range(nu // quarter):
            bup_o[pl.ds(side * nu + k * quarter, quarter)] = small[side, base + 8 + k]
    n = q_o.shape[1]
    for k, ref in enumerate((q_o, k_o, v_o)):
        ref[...] = w[:, k * n : (k + 1) * n].astype(F32)
    o_o[...] = w[:, 3 * n : 4 * n].astype(F32).T
    u_o[...] = w[:, 4 * n : 4 * n + 2 * nu].astype(F32)
    d_o[...] = w[:, 4 * n + 2 * nu :].astype(F32).T


def place(hid, sums, gin, small, w, used):
    sds = jax.ShapeDtypeStruct
    _, toks, half = hid.shape
    rows = w.shape[0]
    nu = (w.shape[1] - 4 * half) // 4
    vmem = pl.BlockSpec(memory_space=pltpu.VMEM)
    return pl.pallas_call(
        place_kernel,
        name="place",
        out_shape=(
            sds((1, 2, toks, half), BF),
            sds((used, 2, half), BF),
            sds((1, 2, toks, half), F32),
            sds((used, half), F32),
            [sds((half,), F32)] * 8,
            sds((2 * nu,), F32),
            sds((rows, half), F32),
            sds((rows, half), F32),
            sds((rows, half), F32),
            sds((half, rows), F32),
            sds((rows, 2 * nu), F32),
            sds((2 * nu, rows), F32),
        ),
        in_specs=[vmem] * 5,
        out_specs=(vmem,) * 4 + ([vmem] * 8,) + (vmem,) * 7,
        compiler_params=pltpu.CompilerParams(vmem_limit_bytes=60 * 2**20),
    )(hid, sums, gin, small, w)


def local(
    hidden_in, summary_counts, summary_embed, ln1_gain, ln1_bias, w_query, b_query, w_key, w_value,
    b_value, w_out, b_out, ln2_gain, ln2_bias, w_up, b_up, w_down, b_down, d_hidden, d_summary,
):
    got = chain(
        summary_counts, summary_embed, d_summary[0].transpose(1, 0, 2),
        [ln1_gain, ln1_bias, ln2_gain, ln2_bias, b_out, b_down], b_query, b_value, b_up,
        hidden_in[0], d_hidden[0], w_query, w_key, w_value, w_out, w_up, w_down,
    )
    hid, sums, gin, emb, vecs, bup, gq, gk, gv, go, gu, gd = place(*got[:5], summary_embed.shape[0])
    return (
        hid, sums.transpose(1, 0, 2)[None], gin, emb, vecs[0], vecs[1], gq, vecs[6], gk, gv,
        vecs[7], go, vecs[2], vecs[3], vecs[4], gu, bup, gd, vecs[5],
    )


def solution(mesh):
    return jax.shard_map(
        local,
        mesh=mesh,
        in_specs=(
            P("batch", None, "seq", "tensor"),
            P("batch"),
            P(None, "tensor"),
            P("tensor"),
            P("tensor"),
            P(None, "tensor"),
            P("tensor"),
            P(None, "tensor"),
            P(None, "tensor"),
            P("tensor"),
            P("tensor", None),
            P("tensor"),
            P("tensor"),
            P("tensor"),
            P(None, "tensor"),
            P("tensor"),
            P("tensor", None),
            P("tensor"),
            P("batch", None, "seq", "tensor"),
            P("batch", None, None, "tensor"),
        ),
        out_specs=(
            P("batch", None, "seq", "tensor"),
            P("batch", None, None, "tensor"),
            P("batch", None, "seq", "tensor"),
            P(None, "tensor"),
            P("tensor"),
            P("tensor"),
            P(("batch", "seq"), "tensor"),
            P("tensor"),
            P(("batch", "seq"), "tensor"),
            P(("batch", "seq"), "tensor"),
            P("tensor"),
            P("tensor", ("batch", "seq")),
            P("tensor"),
            P("tensor"),
            P("tensor"),
            P(("batch", "seq"), "tensor"),
            P("tensor"),
            P("tensor", ("batch", "seq")),
            P("tensor"),
        ),
        check_vma=False,
    )
```

```python
import functools

import jax
import jax.numpy as jnp
from jax import lax
from jax.experimental import pallas as pl
from jax.experimental.pallas import tpu as pltpu
from jax.sharding import PartitionSpec as P

HD = 64
EPSILON = 1e-05
NEGATIVE = -1e30
MESH = pl.DeviceIdType.MESH
BF = jnp.bfloat16
F32 = jnp.float32
PAIR_BIT = 1


def flip(index, bit):
    weight = 1 << bit
    return index + weight - 2 * weight * lax.rem(index // weight, 2)


def bit_of(index, bit):
    return lax.rem(index // (1 << bit), 2)


def dot_nt(a, b):
    return lax.dot_general(a, b, (((1,), (1,)), ((), ())), preferred_element_type=F32)


def dot_tn(a, b):
    return lax.dot_general(a, b, (((0,), (0,)), ((), ())), preferred_element_type=F32)


class Strips:
    def __init__(self, refs, width):
        self.width = width
        self.free = [[ref, ref.shape[0], at, 0] for ref in refs for at in range(ref.shape[1] // width)]

    def take(self, tiles, n, unit):
        for k, (ref, height, at, used) in enumerate(self.free):
            if height < n:
                continue
            if used + tiles * n <= height:
                self.free[k][3] += tiles * n
                return Slab(ref, at, used, tiles, n, unit, self.width)
            per = height // n
            need = -(-tiles // per)
            run = self.free[k : k + need]
            if len(run) == need and all(r[0] is ref and r[3] == 0 for r in run):
                for r in run:
                    r[3] = height
                run[-1][3] = (tiles - per * (need - 1)) * n
                return Slab(ref, at, 0, per, n, unit, self.width)
        raise ValueError("no room")


class Slab:
    def __init__(self, ref, strip, start, per, n, unit, width):
        self.ref, self.strip, self.start, self.per = ref, strip, start, per
        self.n, self.unit, self.width = n, unit, width

    def at(self, i, lo, n):
        first = pl.multiple_of(self.start + (i % self.per) * self.n + lo, self.unit)
        col = pl.multiple_of((self.strip + i // self.per) * self.width, self.width)
        return self.ref.at[pl.ds(first, n), pl.ds(col, self.width)]

    def __call__(self, i):
        return self.at(i, 0, self.n)


def chain_kernel(
    bits,
    count_ref,
    emb_ref,
    dsum_ref,
    feat_refs,
    bq_ref,
    bv_ref,
    bu_ref,
    hid_hbm,
    dhid_hbm,
    wq_hbm,
    wk_hbm,
    wv_hbm,
    wo_hbm,
    wu_hbm,
    wd_hbm,
    hid_out,
    sum_out,
    gin_hbm,
    small_final,
    w_hbm,
    la_hbm,
    lm_hbm,
    ra_hbm,
    mx_hbm,
    ye_hbm,
    ls_hbm,
    rs_hbm,
    wqkv,
    wo,
    wu,
    wd,
    rows,
    act1,
    qkv,
    probs,
    mix,
    mid,
    act2,
    actv,
    db,
    slope0,
    gd,
    gm,
    dmix,
    dqkv,
    dsum,
    vec,
    bias,
    stat,
    outacc,
    fsum,
    gsum,
    gx_send,
    gx_recv,
    ar_send,
    ar_core,
    ar_x,
    ar_full,
    ar_own,
    lxx,
    rbx,
    both,
    small_out,
    wsem,
    lsem,
    rsem,
    free,
    sem_y,
    sem_za,
    sem_pa,
    sem_xa,
    sem_pb,
    sem_zb,
    sem_xb,
    sem_oa,
    sem_ob,
    sem_s,
    early,
    emb_v,
    dsum_v,
    vecs_v,
    isem,
):
    b, s, t = lax.axis_index("batch"), lax.axis_index("seq"), lax.axis_index("tensor")
    at_core = (b, s, 1 - t)
    at_x = (b, 1 - s, t)
    at_p = (flip(b, PAIR_BIT), s, t)
    at_y = (flip(b, 0), s, t)
    halving = list(range(bits - 1, PAIR_BIT, -1))
    at_h = [(flip(b, bit), s, t) for bit in halving]
    zl, y = bit_of(b, PAIR_BIT), bit_of(b, 0)
    halving_down = list(range(bits - 2, 0, -1))
    at_d = (flip(b, bits - 1), s, t)
    zd = bit_of(b, bits - 1)
    count = len(feat_refs)
    small_ins = [(emb_ref, emb_v), (dsum_ref, dsum_v)]
    small_ins += list(zip(list(feat_refs) + [bq_ref, bv_ref, bu_ref], vecs_v))
    small_ins = [
        pltpu.make_async_copy(src, dst, isem.at[k]) for k, (src, dst) in enumerate(small_ins)
    ]
    for copy in small_ins:
        copy.start()
    feat_refs, (bq_ref, bv_ref, bu_ref) = vecs_v[:count], vecs_v[count:]
    emb_ref, dsum_ref = emb_v, dsum_v
    barrier = pltpu.get_barrier_semaphore()
    partners = [at_core, at_x, at_p, at_y] + at_h
    for partner in partners:
        pl.semaphore_signal(barrier, inc=1, device_id=partner, device_id_type=MESH)

    toks = hid_hbm.shape[1]
    slots = slope0.shape[0]
    used = emb_ref.shape[0]
    feats = rows.shape[1]
    half = feats // 2
    quarter = feats // 4
    span = 2 * toks
    s0, t0, t1, s1, p0 = 0, slots, slots + span, slots + 2 * span, 2 * slots + 2 * span
    own = slots + span
    end = p0 + slots
    nq = wo.shape[0]
    nu = wu.shape[1]
    my_cols = pl.ds(pl.multiple_of(t * half, half), half)
    its_cols = pl.ds(pl.multiple_of((1 - t) * half, half), half)
    my_toks = pl.multiple_of(s * toks, toks)
    its_toks = pl.multiple_of((1 - s) * toks, toks)
    my_quarter = pl.ds(pl.multiple_of(t * half + s * quarter, quarter), quarter)

    counter = {"l": 0, "r": 0}

    def local(src, dst):
        counter["l"] += 1
        copy = pltpu.make_async_copy(src, dst, lsem.at[counter["l"] - 1])
        copy.start()
        return copy

    def remote(src, dst, partner):
        counter["r"] += 1
        at = counter["r"] - 1
        copy = pltpu.make_async_remote_copy(
            src_ref=src,
            dst_ref=dst,
            send_sem=rsem.at[at, 0],
            recv_sem=rsem.at[at, 1],
            device_id=partner,
            device_id_type=MESH,
        )
        copy.start()
        return copy

    part = lambda ref, n, axis: (
        ref.at[:, pl.ds(pl.multiple_of(s * n, n), n)]
        if axis
        else ref.at[pl.ds(pl.multiple_of(s * n, n), n), :]
    )
    weights = []
    for at, (src, dst) in enumerate(
        (
            (part(wq_hbm, nq, 1), wqkv.at[:, pl.ds(0, nq)]),
            (part(wk_hbm, nq, 1), wqkv.at[:, pl.ds(nq, nq)]),
            (part(wv_hbm, nq, 1), wqkv.at[:, pl.ds(2 * nq, nq)]),
            (part(wo_hbm, nq, 0), wo),
            (part(wu_hbm, nu, 1), wu),
            (part(wd_hbm, nu, 0), wd),
        )
    ):
        copy = pltpu.make_async_copy(src, dst, wsem.at[at])
        weights.append(copy)

    firsts = []
    for seg, at in enumerate((t0, t1)):
        firsts.append(local(hid_hbm.at[seg], rows.at[pl.ds(at + my_toks, toks), my_cols]))
    laters = []
    for seg, at in enumerate((t0, t1)):
        laters.append(local(dhid_hbm.at[seg], gd.at[pl.ds(at + my_toks, toks), my_cols]))
    for copy in weights[:3]:
        copy.start()
    for copy in small_ins:
        copy.wait()
    for at in (s0, s1):
        rows[pl.ds(at, slots), my_cols] = jnp.zeros((slots, half), BF)
        rows[pl.ds(at, used), my_cols] = emb_ref[...]
    for seg in range(2):
        dsum[pl.ds(seg * slots, slots), my_cols] = jnp.zeros((slots, half), BF)
        dsum[pl.ds(seg * slots, used), my_cols] = dsum_ref[:, seg, :]
    for k, ref in enumerate(feat_refs):
        vec[k : k + 1, my_cols] = ref[...].astype(F32)[None]
    pl.semaphore_wait(barrier, len(partners))

    def in_x(src, dst, at):
        return remote(src, dst.at[pl.ds(at + my_toks, toks), my_cols], at_x)

    def in_core(block):
        return remote(block, block, at_core)

    def in_pass(dst, at):
        return in_core(dst.at[pl.ds(at + its_toks, toks), my_cols])

    x_hid = [in_x(hid_hbm.at[0], rows, t0)]
    from_core = [
        in_core(rows.at[pl.ds(s0, slots), my_cols]),
        in_core(vec.at[:, my_cols]),
        remote(hid_hbm.at[0], rows.at[pl.ds(t0 + my_toks, toks), my_cols], at_core),
    ]
    late_core = [
        in_core(rows.at[pl.ds(s1, slots), my_cols]),
        remote(hid_hbm.at[1], rows.at[pl.ds(t1 + my_toks, toks), my_cols], at_core),
        in_core(dsum.at[:, my_cols]),
    ]
    for src, dst, at in ((dhid_hbm.at[0], gd, t0), (dhid_hbm.at[1], gd, t1)):
        late_core.append(remote(src, dst.at[pl.ds(at + my_toks, toks), my_cols], at_core))
    for copy in weights[3:]:
        copy.start()

    live_count = count_ref[0]
    row_live = (lax.broadcasted_iota(jnp.int32, (slots, 1), 0) < live_count).astype(F32)
    dqkv[pl.ds(p0, slots), pl.ds(0, nq)] = jnp.zeros((slots, nq), BF)
    bias[:, pl.ds(nq, nq)] = jnp.zeros((1, nq), F32)
    for ref, at, n in ((bq_ref, 0, nq), (bv_ref, 2 * nq, nq), (bu_ref, 3 * nq, nu)):
        x = ref[...].astype(F32)[None]
        bias[:, pl.ds(at, n)] = jnp.where(s == 0, x[:, :n], x[:, n:])
    fsum[...] = jnp.zeros_like(fsum)
    gsum[...] = jnp.zeros_like(gsum)

    step = 16
    inverse = 1.0 / feats

    def row_loop(start, n, body):
        @pl.loop(0, n // step)
        def _(i):
            body(pl.ds(pl.multiple_of(start + i * step, step), step))

    def mean(x):
        return jnp.sum(x, axis=1, keepdims=True) * inverse

    def stats(x):
        m = mean(x)
        return m, lax.rsqrt(mean(x * x) - m * m + EPSILON)

    def norm1(start, n):
        def body(at):
            x = rows[at, :].astype(F32)
            m, r = stats(x)
            act1[at, :] = ((x - m) * r * vec[0:1, :] + vec[1:2, :]).astype(BF)
            stat[at, 0:1] = m
            stat[at, 1:2] = r

        row_loop(start, n, body)

    def norm_back(d, xhat, r, gain):
        q = d * gain
        return r * (q - mean(q) - xhat * mean(q * xhat))

    def fold(x):
        return jnp.sum(x.reshape(step // 8, 8, x.shape[1]), axis=0)

    wide = 512

    def col_loop(n, body):
        @pl.loop(0, n // wide)
        def _(j):
            body(pl.multiple_of(j * wide, wide))

    def project(at, n, lo, hi):
        def body(c):
            cols = pl.ds(pl.multiple_of(lo + c, wide), wide)
            x = jnp.dot(act1[pl.ds(at, n), :], wqkv[:, cols], preferred_element_type=F32)
            qkv[pl.ds(at, n), cols] = (x + bias[:, cols]).astype(BF)

        col_loop(hi - lo, body)

    class Total:
        def __init__(self, n, at, full, pieces, own_at=0):
            self.n, self.at, self.full, self.own_at = n, at, full, own_at
            self.pieces = pieces

        def mine(self, r, n):
            if self.full is None:
                return ar_own.at[pl.ds(self.own_at + r, n), :]
            return ar_full.at[pl.ds(self.full + r, n), my_cols]

        def start(self, product):
            at = pl.ds(self.at, self.n)

            def other(c):
                x = product(pl.multiple_of((1 - t) * half + c, wide), wide)
                ar_send[at, pl.ds(c, wide)] = x.astype(BF)

            col_loop(half, other)
            self.core = remote(ar_send.at[at, :], ar_core.at[at, :], at_core)

            def this(c):
                x = product(pl.multiple_of(t * half + c, wide), wide)
                if self.full is None:
                    ar_own[pl.ds(self.own_at, self.n), pl.ds(c, wide)] = x.astype(BF)
                else:
                    cols = pl.ds(pl.multiple_of(t * half + c, wide), wide)
                    ar_full[pl.ds(self.full, self.n), cols] = x.astype(BF)

            col_loop(half, this)

        def middle(self):
            self.core.wait()
            self.xs = []
            for base, n, scatter in self.pieces:
                at = pl.ds(self.at + base, n)
                ar_core[at, :] = (
                    self.mine(base, n)[...].astype(F32) + ar_core[at, :].astype(F32)
                ).astype(BF)
                if scatter:
                    src = ar_core.at[pl.ds(self.at + base + its_toks, toks), :]
                    dst = ar_x.at[pl.ds(self.at + base, toks), :]
                else:
                    src, dst = ar_core.at[at, :], ar_x.at[at, :]
                self.xs.append(remote(src, dst, at_x))

        def sums(self, base, n, scatter):
            if scatter:
                near = ar_core[pl.ds(self.at + base + my_toks, toks), :]
                far = ar_x[pl.ds(self.at + base, toks), :]
            else:
                near = ar_core[pl.ds(self.at + base, n), :]
                far = ar_x[pl.ds(self.at + base, n), :]
            return near.astype(F32) + far.astype(F32)

        def finish(self):
            self.backs = []
            for (base, n, scatter), copy in zip(self.pieces, self.xs):
                copy.wait()
                n = toks if scatter else n
                block = ar_full.at[pl.ds(self.full + base, n), my_cols]
                block[...] = self.sums(base, n, scatter).astype(BF)
                self.backs.append(remote(block, block, at_core))

        def done(self):
            for copy in self.backs:
                copy.wait()

        def flow(self, body, before_last=lambda: None):
            self.backs = []
            for k, ((base, n, _), copy) in enumerate(zip(self.pieces, self.xs)):
                if k == len(self.pieces) - 1:
                    before_last()
                copy.wait()
                block = ar_full.at[pl.ds(self.full + base, n), my_cols]
                block[...] = self.sums(base, n, False).astype(BF)
                self.backs.append(remote(block, block, at_core))
                if k:
                    self.backs[k - 1].wait()
                    body(*self.pieces[k - 1][:2])
            self.backs[-1].wait()
            body(*self.pieces[-1][:2])

    whole = lambda n: [(i, 64, False) for i in range(0, n, 64)]

    def out_product(at, n):
        return lambda c, w: jnp.dot(
            mix[pl.ds(at, n), :], wo[:, pl.ds(c, w)], preferred_element_type=F32
        )

    def down_product(at, n):
        return lambda c, w: jnp.dot(
            actv[pl.ds(at, n), :], wd[:, pl.ds(c, w)], preferred_element_type=F32
        )

    def up_back(at, n):
        return lambda c, w: dot_nt(db[pl.ds(at, n), :], wu[pl.ds(c, w), :])

    def in_back(at, n, lo):
        return lambda c, w: dot_nt(
            dqkv[pl.ds(at, n), pl.ds(lo, 3 * nq - lo)], wqkv[pl.ds(c, w), pl.ds(lo, 3 * nq - lo)]
        )

    def enter_ffn(total, at, n, base=0):
        def body(i):
            r = pl.ds(pl.multiple_of(at + base + i * step, step), step)
            f = pl.ds(pl.multiple_of(total.full + base + i * step, step), step)
            x = rows[r, :].astype(F32) + ar_full[f, :].astype(F32) + vec[4:5, :]
            m, rs = stats(x)
            mid[r, :] = x
            act2[r, :] = ((x - m) * rs * vec[2:3, :] + vec[3:4, :]).astype(BF)
            stat[r, 2:3] = m
            stat[r, 3:4] = rs

        pl.loop(0, n // step)(body)

    def gelu(v):
        c = 0.7978845608028654
        th = jnp.tanh(c * (v + 0.044715 * (v * v * v)))
        act = 0.5 * v * (1.0 + th)
        sl = 0.5 * (1.0 + th) + (0.5 * c) * v * (1.0 - th * th) * (1.0 + (3 * 0.044715) * v * v)
        return act, sl

    def ffn(at, n, back, lo, hi):
        r = pl.ds(at, n)

        def body(c):
            c = pl.multiple_of(lo + c, wide)
            cols = pl.ds(c, wide)
            v = jnp.dot(act2[r, :], wu[:, cols], preferred_element_type=F32)
            act, sl = gelu(v + bias[:, pl.ds(pl.multiple_of(3 * nq + c, wide), wide)])
            actv[r, cols] = act.astype(BF)
            if back == 1:
                db[r, cols] = (sl * dot_nt(gd[r, :], wd[cols, :])).astype(BF)
            elif back == 2:
                db[r, cols] = (sl * db[r, cols].astype(F32)).astype(BF)
            else:
                slope0[:, cols] = sl

        col_loop(hi - lo, body)

    def leave_ffn(total, at, n, base=0):
        def body(i):
            r = pl.ds(pl.multiple_of(at + base + i * step, step), step)
            f = pl.ds(pl.multiple_of(total.full + base + i * step, step), step)
            d = ar_full[f, :].astype(F32)
            xhat = (mid[r, :] - stat[r, 2:3]) * stat[r, 3:4]
            fsum[pl.ds(0, 8), :] = fsum[pl.ds(0, 8), :] + fold(d * xhat)
            fsum[pl.ds(8, 8), :] = fsum[pl.ds(8, 8), :] + fold(d)
            dm = gd[r, :].astype(F32) + norm_back(d, xhat, stat[r, 3:4], vec[2:3, :])
            mid[r, :] = dm
            gm[r, :] = dm.astype(BF)

        pl.loop(0, n // step)(body)

    def mix_back(at, n):
        dmix[pl.ds(at, n), :] = dot_nt(gm[pl.ds(at, n), :], wo[...]).astype(BF)

    pairs = nq // (2 * HD)
    scale = HD**-0.5

    def seen(seg, keys):
        q = lax.broadcasted_iota(jnp.int32, (own, keys), 0)
        k = lax.broadcasted_iota(jnp.int32, (own, keys), 1)
        if seg == 0:
            q = jnp.where(q < slots, q + span, q - slots)
            slot = k
            token = k >= slots
            k = jnp.where(token, k - slots, k + span)
            return (k <= q) & (token | (slot < live_count))
        token = k < span
        ahead = k >= own
        slot = jnp.where(ahead, k - own, k - span)
        return (ahead | (k <= q)) & (token | (slot < live_count))

    def lanes(n):
        first = (lax.broadcasted_iota(jnp.int32, (n, 2 * HD), 1) < HD).astype(F32)
        return first.astype(BF), (1.0 - first).astype(BF)

    def attend(seg):
        at, keys = (s0, own) if seg == 0 else (t1, own + slots)
        q_rows, k_rows = pl.ds(at, own), pl.ds(at, keys)

        @pl.loop(0, pairs)
        def _(j):
            col = lambda g: pl.ds(pl.multiple_of(g * nq + j * 2 * HD, 2 * HD), 2 * HD)
            q, k, v = qkv[q_rows, col(0)], qkv[k_rows, col(1)], qkv[k_rows, col(2)]
            first = lanes(keys)
            allowed = seen(seg, keys)
            got = jnp.zeros((own, 2 * HD), F32)
            for h in range(2):
                pick = first[h]
                sc = dot_nt(q, k * pick) * scale
                sc = jnp.where(allowed, sc, NEGATIVE)
                e = jnp.exp(sc - jnp.max(sc, axis=1, keepdims=True))
                p = (e / jnp.sum(e, axis=1, keepdims=True)).astype(BF)
                probs[seg, 2 * j + h, :, pl.ds(0, keys)] = p
                got += jnp.dot(p, v * pick, preferred_element_type=F32)
            mix[q_rows, pl.ds(pl.multiple_of(j * 2 * HD, 2 * HD), 2 * HD)] = got.astype(BF)

    def attend_back(seg):
        at, keys = (s0, own) if seg == 0 else (t1, own + slots)
        q_rows, k_rows = pl.ds(at, own), pl.ds(at, keys)

        @pl.loop(0, pairs)
        def _(j):
            col = lambda g: pl.ds(pl.multiple_of(g * nq + j * 2 * HD, 2 * HD), 2 * HD)
            q, k, v = qkv[q_rows, col(0)], qkv[k_rows, col(1)], qkv[k_rows, col(2)]
            d = dmix[q_rows, pl.ds(pl.multiple_of(j * 2 * HD, 2 * HD), 2 * HD)]
            first_k, first_q = lanes(keys), lanes(own)
            dq = jnp.zeros((own, 2 * HD), F32)
            dk = jnp.zeros((keys, 2 * HD), F32)
            dv = jnp.zeros((keys, 2 * HD), F32)
            for h in range(2):
                pick_k, pick_q = first_k[h], first_q[h]
                p = probs[seg, 2 * j + h, :, pl.ds(0, keys)]
                pf = p.astype(F32)
                dp = dot_nt(d, v * pick_k)
                ds = (pf * (dp - jnp.sum(pf * dp, axis=1, keepdims=True))).astype(BF)
                dq += jnp.dot(ds, k * pick_k, preferred_element_type=F32)
                dk += dot_tn(ds, q * pick_q)
                dv += dot_tn(p, d * pick_q)
            dqkv[q_rows, col(0)] = (dq * scale).astype(BF)
            dqkv[k_rows, col(1)] = (dk * scale).astype(BF)
            dqkv[k_rows, col(2)] = dv.astype(BF)

    gifts_a, gifts_b, passed = [], [], []
    hu = nu // 2
    chunk = feats >> bits
    chunks = 1 << (bits - 1)

    def share_feats_a(op, src, at, n):
        landing = lxx.at[op, pl.ds(at, n), my_cols]
        partner = at_d if op else at_p
        gifts_a.append((remote(src.at[pl.ds(at, n), my_cols], landing, partner), landing))

    def share_units_a(op, src, at, n):
        side = zd if op else zl
        its = pl.ds(pl.multiple_of((1 - side) * hu, hu), hu)
        landing = rbx.at[pl.ds(at, n), pl.ds(op * hu, hu)]
        partner = at_d if op else at_p
        gifts_a.append((remote(src.at[pl.ds(at, n), its], landing, partner), None))

    y_blocks = [(my_cols, my_cols)]
    if chunk % 128 == 0:
        block = lambda c: pl.ds(pl.multiple_of(c * chunk, chunk), chunk)
        y_blocks = [2 * (t * chunks // 2 + m) for m in range(chunks // 2)]
        y_blocks = [(block(c + 1 - y), block(c + y)) for c in y_blocks]

    def share_feats_b(src, dst, at, n):
        for out, back in y_blocks:
            copy = remote(src.at[pl.ds(at, n), out], dst.at[pl.ds(at, n), out], at_y)
            gifts_b.append((copy, dst.at[pl.ds(at, n), back]))

    def share_units_b(src, dst, at, n):
        gifts_b.append((remote(src.at[pl.ds(at, n), :], dst.at[pl.ds(at, n), :], at_y), None))

    def pass_on(gifts, most=1000):
        while gifts and most:
            most -= 1
            copy, landing = gifts.pop(0)
            copy.wait()
            if landing is not None:
                passed.append(remote(landing, landing, at_core))

    def pass_end():
        while passed:
            passed.pop(0).wait()

    def share_thin(src, dst, at, n, partner):
        block = dst.at[pl.ds(at, n), my_quarter]
        return remote(src.at[pl.ds(at, n), my_quarter], block, partner)

    gifts_q, thin_act1, thin_act2 = [], [], []
    hq = nq // 2

    def share_qkv(at, n):
        for g in range(3):
            its = pl.ds(pl.multiple_of(g * nq + (1 - zl) * hq, hq), hq)
            landing = ra_hbm.at[pl.ds(at, n), pl.ds(g * hq, hq)]
            gifts_q.append(remote(dqkv.at[pl.ds(at, n), its], landing, at_p))

    share_mix = lambda at, n: share_units_b(mix, mx_hbm, at, n)
    share_actv = lambda at, n: share_units_a(0, actv, at, n)
    share_db = lambda at, n: share_units_a(1, db, at, n)

    width = nq // 2
    near = chunk // 2
    per = hu // width
    tiles_a, tiles_b = 2 * per + 3, nq // width
    assert per == 4 and hq == width

    def kind_of(i):
        later = (i // per + 1) // 2
        return 1 - later, later * (i % 2), (1 - later) * i + later * ((i - per) // 2)


    nh = len(halving)
    strips = Strips([wu, wd], width)
    recv_y = strips.take(tiles_a, chunks * chunk, near)
    slots_y = 4
    send_y = strips.take(slots_y, chunks * chunk, near)
    recv_za = [strips.take(tiles_a, chunks * chunk >> (k + 1), near) for k in range(nh)]
    recv_pb = strips.take(tiles_b, chunks * chunk // 2, near)
    recv_zb = [strips.take(tiles_b, chunks * chunk >> (k + 2), near) for k in range(nh)]
    recv_px = strips.take(tiles_a, 2 * chunk, near)
    send_zd = strips.take(per, chunks * chunk // 2, near)
    recv_xb = strips.take(tiles_b, near, near)
    strips = Strips([wqkv, wo], width)
    send_za = [strips.take(tiles_a, chunks * chunk >> (k + 1), near) for k in range(nh)]
    send_pb = strips.take(tiles_b, chunks * chunk // 2, near)
    send_zb = [strips.take(tiles_b, chunks * chunk >> (k + 2), near) for k in range(nh)]
    send_pa = strips.take(tiles_a, chunk, near)

    def linked(src, dst, sem, partner):
        return pltpu.make_async_remote_copy(
            src_ref=src,
            dst_ref=dst,
            send_sem=sem.at[0],
            recv_sem=sem.at[1],
            device_id=partner,
            device_id_type=MESH,
        )

    copy_y = lambda i: linked(send_y(i % slots_y), recv_y(i), sem_y.at[i], at_y)
    def by_kind(i, far, close):
        down, inner, _ = kind_of(i)
        return close + (1 - down - inner) * (far - close)

    def copy_za(k, i, down=False):
        to = by_kind(i, flip(b, halving_down[k]), flip(b, halving[k]))
        src = send_zd if down else send_za[k]
        return linked(src(i), recv_za[k](i), sem_za.at[k, i], (to, s, t))

    def copy_pa(i):
        to = by_kind(i, at_d[0], at_p[0])
        return linked(send_pa(i), recv_px.at(i, 0, chunk), sem_pa.at[i], (to, s, t))

    def place_bit(j, k, value):
        low = 1 << k
        return (j // low) * 2 * low + value * low + j % low

    copy_pb = lambda i: linked(send_pb(i), recv_pb(i), sem_pb.at[i], at_p)
    copy_zb = lambda k, i: linked(send_zb[k](i), recv_zb[k](i), sem_zb.at[k, i], at_h[k])

    def block_product(lefts, rights, c):
        def dots(cols):
            x = dot_tn(lefts[0](cols), rights[0])
            for left, right in zip(lefts[1:], rights[1:]):
                x = x + dot_tn(left(cols), right)
            return x

        if chunk % 128 == 0:
            return dots(pl.ds(pl.multiple_of(c * chunk, chunk), chunk))
        both[...] = dots(pl.ds(pl.multiple_of((c // 2) * 2 * chunk, 2 * chunk), 2 * chunk))
        return both[pl.ds(pl.multiple_of((c % 2) * chunk, chunk), chunk), :]

    main = p0

    def products_a(i, parts, early=False):
        down, inner, k = kind_of(i)
        tile = lambda c: pl.ds(pl.multiple_of(c, width), width)
        cases = (
            (gd, lxx.at[0], actv, zl * hu + k * width, rbx, k * width),
            (act2, lxx.at[1], db, zd * hu + k * width, rbx, hu + k * width),
            (act1, rows, dqkv, k * nq + zl * hq, qkv, k * width),
        )
        for op, (near_l, far_l, near_r, near_at, far_r, far_at) in enumerate(cases):

            @pl.when((1 - down) * (1 + inner) == op)
            def _():
                at = pl.ds(slots, main - slots) if early and op == 0 else slice(None)
                rights = [near_r[at, tile(near_at)], far_r[at, tile(far_at)]]
                lefts = [lambda cols: near_l[at, cols], lambda cols: far_l[at, cols]]
                if op == 0 and not early:
                    rights.append(ar_own[pl.ds(0, 2 * slots), tile(k * width)])
                    lefts.append(lambda cols: dsum[:, cols])
                for n, which, put, after in parts(op):

                    @pl.loop(0, n)
                    def _(j):
                        put(j, block_product(lefts, rights, which(j)))

                    after()

    def products_b(i, parts):
        cols = pl.ds(pl.multiple_of(i * width, width), width)
        r1, r2 = mix[:, cols], dmix[:, cols]
        l1, l2 = (lambda at: gm[:, at]), (lambda at: ar_full[pl.ds(0, p0), at])
        for n, which, put, after in parts:

            @pl.loop(0, n)
            def _(j):
                put(j, block_product((l1, l2), (r1, r2), which(j)))

            after()

    def copy_early(i):
        return linked(early.at[i % 2], ye_hbm.at[i], sem_y.at[i], at_y)

    def a_early(i):
        def put(j, v):
            early[i % 2, pl.ds(pl.multiple_of(j * chunk, chunk), chunk), :] = v.astype(BF)

        if i >= 2:
            copy_early(i - 2).wait_send()
        part = (chunks, lambda j: 2 * j + 1 - y, put, lambda: copy_early(i).start())
        products_a(i, lambda op: [part], True)

    def early_in(i):
        if i >= 2:
            copy_early(i).wait_send()
        copy_early(i).wait_recv()
        return local(ye_hbm.at[i], recv_y(i))

    def a_first(i):
        def put(j, v):
            send_y.at(i % slots_y, j * chunk, chunk)[...] = v.astype(BF)

        part = (chunks, lambda j: 2 * j + 1 - y, put, lambda: copy_y(i).start())
        products_a(i, lambda op: [part])

    def a_second(i, came=None):
        (copy_y(i) if came is None else came).wait()
        n = chunks // 2

        def parts(op):
            bit = bit_of(b, (halving_down if op == 1 else halving)[0])
            k = bits - 3 if op == 1 else bits - 2
            other = lambda j: place_bit(j, k, 1 - bit)
            mine = lambda j: place_bit(j, k, bit)

            def total(v, at):
                return (v + recv_y.at(i, at * chunk, chunk)[...].astype(F32)).astype(BF)

            def give(j, v):
                give_to = send_za[0] if op else send_zd
                give_to.at(i, j * chunk, chunk)[...] = total(v, other(j))

            def keep(j, v):
                x = total(v, mine(j))
                recv_y.at(i, j * chunk, chunk)[...] = x

            return [
                (n, lambda j: 2 * other(j) + y, give, lambda: copy_za(0, i, op == 0).start()),
                (n, lambda j: 2 * mine(j) + y, keep, lambda: None),
            ]

        products_a(i, parts)

    def halve(i, kept, at, recv, n, give, copy, k, bit):
        def total(c):
            x = kept.at(i, (at + c) * chunk, chunk)[...].astype(F32)
            return (x + recv.at(i, c * chunk, chunk)[...].astype(F32)).astype(BF)

        for j in range(n // 2):
            give.at(i, j * chunk, chunk)[...] = total(place_bit(j, k, 1 - bit))
        copy().start()
        for j in range(n // 2):
            x = total(place_bit(j, k, bit))
            kept.at(i, (at + n + j) * chunk, chunk)[...] = x

    ends_a = [0]
    for k in range(nh + 1):
        ends_a.append(ends_a[-1] + (chunks >> (k + 1)))

    def a_third(k, i):
        copy_za(k, i).wait()
        n = chunks >> (k + 1)
        if k + 1 == nh:
            side = by_kind(i, zd, zl)
            halve(i, recv_y, ends_a[k], recv_za[k], n, send_pa, lambda: copy_pa(i), 0, side)
            return
        for op in range(2):

            @pl.when(by_kind(i, 1, 0) == op)
            def _():
                bit = bit_of(b, (halving_down if op else halving)[k + 1])
                at = bits - 4 - k if op else bits - 3 - k
                after = lambda: copy_za(k + 1, i)
                halve(i, recv_y, ends_a[k], recv_za[k], n, send_za[k + 1], after, at, bit)

    my_near = pl.multiple_of(s * near, near)
    its_near = pl.multiple_of((1 - s) * near, near)
    kept_a = lambda i, at: recv_y.at(i, ends_a[nh] * chunk + at, near)

    def copies_xa(i):
        side = by_kind(i, zd, zl)
        return [
            linked(kept_a(i, its_near), recv_px.at(i, chunk + side * near, near), sem_xa.at[i, 0], at_x),
            linked(
                recv_px.at(i, its_near, near),
                recv_px.at(i, chunk + (1 - side) * near, near),
                sem_xa.at[i, 1],
                at_x,
            ),
        ]

    def outs_a(i, picks):
        def to(side, pair):
            down, inner, k = kind_of(i)
            ffn_col = 8 * nq + down * 2 * nu + side * nu + pair * hu + k * width
            col = (1 - inner) * ffn_col + inner * (k * 2 * nq + side * nq + pair * hq)
            return w_hbm.at[:, pl.ds(pl.multiple_of(col, width), width)]

        pieces = [
            (kept_a(i, my_near), to(s, by_kind(i, zd, zl))),
            (recv_px.at(i, my_near, near), to(s, 1 - by_kind(i, zd, zl))),
            (recv_px.at(i, chunk, near), to(1 - s, 0)),
            (recv_px.at(i, chunk + near, near), to(1 - s, 1)),
        ]
        return [pltpu.make_async_copy(*pieces[k], sem_oa.at[i, k]) for k in picks]

    def a_fourth(i):
        copy_pa(i).wait()
        for copy in copies_xa(i) + outs_a(i, (0, 1)):
            copy.start()

    def a_fifth(i):
        for copy in copies_xa(i):
            copy.wait()
        for copy in outs_a(i, (2, 3)):
            copy.start()

    def b_first(i):
        n = chunks // 2

        def put(j, v):
            send_pb.at(i, j * chunk, chunk)[...] = v.astype(BF)

        products_b(i, [(n, lambda j: 2 * (2 * j + 1 - zl) + y, put, lambda: copy_pb(i).start())])

    def b_second(i):
        copy_pb(i).wait()
        bit = bit_of(b, halving[0])
        n = chunks // 4

        def total(v, at):
            return (v + recv_pb.at(i, at * chunk, chunk)[...].astype(F32)).astype(BF)

        def give(j, v):
            send_zb[0].at(i, j * chunk, chunk)[...] = total(v, (1 - bit) * n + j)

        def keep(j, v):
            x = total(v, bit * n + j)
            recv_pb.at(i, j * chunk, chunk)[...] = x

        products_b(
            i,
            [
                (n, lambda j: 2 * (2 * ((1 - bit) * n + j) + zl) + y, give, lambda: copy_zb(0, i).start()),
                (n, lambda j: 2 * (2 * (bit * n + j) + zl) + y, keep, lambda: None),
            ],
        )

    ends_b = [0]
    for k in range(nh):
        ends_b.append(ends_b[-1] + (chunks >> (k + 2)))
    kept_b = lambda i, at: recv_pb.at(i, ends_b[nh] * chunk + at, near)

    def copy_xb(i):
        return linked(kept_b(i, its_near), recv_xb(i), sem_xb.at[i], at_x)

    def outs_b(i, picks):
        def to(side):
            col = 6 * nq + side * nq + i * width
            return w_hbm.at[:, pl.ds(pl.multiple_of(col, width), width)]

        pieces = [(kept_b(i, my_near), to(s)), (recv_xb(i), to(1 - s))]
        return [pltpu.make_async_copy(*pieces[k], sem_ob.at[i, k]) for k in picks]

    def b_third(k, i):
        copy_zb(k, i).wait()
        n = chunks >> (k + 2)
        if k + 1 < nh:
            bit = bit_of(b, halving[k + 1])
            after = lambda: copy_zb(k + 1, i)
            halve(i, recv_pb, ends_b[k], recv_zb[k], n, send_zb[k + 1], after, bits - 4 - k, bit)
        else:
            x = recv_pb.at(i, ends_b[k] * chunk, chunk)[...].astype(F32) + recv_zb[k](i)[...].astype(F32)
            recv_pb.at(i, ends_b[nh] * chunk, chunk)[...] = x.astype(BF)
            copy_xb(i).start()
            outs_b(i, (0,))[0].start()

    def b_fourth(i):
        copy_xb(i).wait()
        outs_b(i, (1,))[0].start()

    small_partners = [at_y] + at_h + [at_p, at_x]

    def small_in(k):
        at = pl.ds((k // 2) * small_out.shape[0], small_out.shape[0])
        return outacc.at[at, pl.ds((k % 2) * quarter, quarter)]

    def small_step(k):
        copy = lambda k: linked(small_out, small_in(k), sem_s.at[k], small_partners[k])
        if k > 0:
            copy(k - 1).wait()
            if k < len(small_partners):
                small_out[...] = small_out[...] + small_in(k - 1)[...]
        if k < len(small_partners):
            copy(k).start()
        else:
            small_final[s] = small_out[...]
            small_final[1 - s] = small_in(k - 1)[...]

    for copy in firsts + from_core:
        copy.wait()
    norm1(s0, slots)
    norm1(t0 + my_toks, toks)
    x_hid[0].wait()
    forward = in_pass(rows, t0)
    x_hid.append(in_x(hid_hbm.at[1], rows, t1))
    x_dhid = [in_x(dhid_hbm.at[0], gd, t0), in_x(dhid_hbm.at[1], gd, t1)]
    forward.wait()
    norm1(t0 + its_toks, toks)
    thin_act1.append(share_thin(act1, la_hbm, 0, own, at_p))
    for copy in weights[:3]:
        copy.wait()
    project(0, own, 0, 3 * nq)
    attend(0)
    share_mix(0, own)
    for copy in weights[3:4]:
        copy.wait()
    T = span
    a1 = Total(slots, 0, 0, whole(slots))
    a2 = Total(T, 2 * slots, 2 * slots, whole(T))
    a1.start(out_product(s0, slots))
    a2.start(out_product(t0, T))
    a1.middle()
    a2.middle()
    x_hid[1].wait()
    forward = in_pass(rows, t1)
    for copy in late_core + laters:
        copy.wait()
    forward.wait()
    norm1(t1, own)
    thin_act1.append(share_thin(act1, la_hbm, t1, own, at_p))
    project(t1, own, 0, 3 * nq)
    a1.finish()
    a1.done()
    enter_ffn(a1, s0, slots)
    weights[4].wait()
    forwards = []
    for copy, at in zip(x_dhid, (t0, t1)):
        copy.wait()
        forwards.append(in_pass(gd, at))
    gd[pl.ds(s1, slots), :] = (dsum[pl.ds(slots, slots), :].astype(F32) * row_live).astype(BF)
    ffn(s0, slots, 0, 0, nu)
    for copy in forwards:
        copy.wait()
    share_feats_a(0, gd, t0, p0 - t0)
    weights[5].wait()
    a3 = Total(slots, slots, slots, whole(slots))
    a3.start(down_product(s0, slots))
    a2.finish()
    a3.middle()
    a2.done()
    enter_ffn(a2, t0, T)
    outacc[pl.ds(0 * toks, toks), :] = mid[pl.ds(t0 + my_toks, toks), my_cols]

    def early_before(c):
        cols, r = pl.ds(c, wide), pl.ds(t1, own)
        db[r, cols] = dot_nt(gd[r, :], wd[cols, :]).astype(BF)

    col_loop(nu, early_before)
    a3.finish()
    thin_act2.append(share_thin(act2, lxx.at[1], s0, own, at_d))
    a3.done()

    def summary(i):
        r = pl.ds(pl.multiple_of(s0 + i * step, step), step)
        f = pl.ds(pl.multiple_of(a3.full + i * step, step), step)
        p = pl.ds(pl.multiple_of(p0 + i * step, step), step)
        x = mid[r, :] + ar_full[f, :].astype(F32) + vec[5:6, :]
        on = (lax.broadcasted_iota(jnp.int32, (step, 1), 0) + i * step < live_count).astype(F32)
        rows[p, :] = (x * on).astype(BF)

    pl.loop(0, slots // step)(summary)
    sum_out[0] = rows[pl.ds(p0, slots), my_cols]
    norm1(p0, slots)
    thin_act1.append(share_thin(act1, la_hbm, p0, slots, at_p))
    project(p0, slots, nq, 3 * nq)
    attend(1)
    share_mix(t1, own)
    a5 = Total(own, 2 * slots + T, 2 * slots + T, whole(own))
    a5.start(out_product(t1, own))
    ffn(t0, T, 1, 0, nu // 4)
    a5.middle()
    ffn(t0, T, 1, nu // 4, nu)
    share_actv(s0, own)
    side = pl.ds(pl.multiple_of(zl * hu, hu), hu)
    rs_own = remote(actv.at[pl.ds(s0, slots), side], rs_hbm.at[pl.ds(0, slots), :], at_y)
    a6 = Total(T, 2 * slots, 2 * slots, whole(T))
    a6.start(up_back(t0, T))
    a6.middle()
    a4 = Total(T, 2 * slots + T + 2 * own, None, [(0, T, True)], 0)
    a4.start(down_product(t0, T))
    a5.flow(lambda base, n: enter_ffn(a5, t1, n, base))
    a4.middle()
    outacc[pl.ds(1 * toks, toks), :] = mid[pl.ds(t1 + my_toks, toks), my_cols]
    outacc[pl.ds(2 * toks, toks), :] = mid[pl.ds(s1, slots), my_cols]
    pass_on(gifts_a, 1)
    ffn(t1, own, 2, 0, nu)
    share_actv(t1, own)
    a8 = Total(own, 2 * slots + T + own, 2 * slots + T + own, whole(own))
    a8.start(up_back(t1, own))
    a6.finish()
    a8.middle()
    a7 = Total(own, 2 * slots + 2 * T + 2 * own, None, [(0, T, True), (T, slots, False)], T)
    a7.start(down_product(t1, own))
    a6.done()
    leave_ffn(a6, t0, T)
    mix_back(t0, T)
    share_feats_b(gm, lm_hbm, t0, T)

    def begin_down():
        pass_on(gifts_a)
        pass_end()
        a_early(0)
        thin_act2.append(share_thin(act2, lxx.at[1], t1, own, at_d))
        share_db(t0, T)
        share_db(t1, own)

    a8.flow(lambda base, n: leave_ffn(a8, t1, n, base), begin_down)
    far = rbx.at[pl.ds(s0, slots), pl.ds(0, hu)]
    rs_far = remote(far, rs_hbm.at[pl.ds(slots, slots), :], at_y)
    a7.middle()
    mix_back(t1, own)
    share_feats_b(gm, lm_hbm, t1, own)
    attend_back(1)
    a9 = Total(slots, 0, 0, whole(slots))
    a9.start(in_back(p0, slots, nq))
    a10 = Total(own, 2 * slots + T, 2 * slots + T, [(0, T, True), (T, slots, False)])
    a9.middle()
    a10.start(in_back(t1, own, 0))
    a9.finish()
    a10.middle()
    for copy in a4.xs + a7.xs:
        copy.wait()
    hid_out[0] = (outacc[pl.ds(0 * toks, toks), :] + a4.sums(0, T, True) + vec[5:6, my_cols]).astype(BF)
    hid_out[1] = (outacc[pl.ds(1 * toks, toks), :] + a7.sums(0, T, True) + vec[5:6, my_cols]).astype(BF)
    sum_out[1] = (
        (outacc[pl.ds(2 * toks, toks), :] + a7.sums(T, slots, False) + vec[5:6, my_cols]) * row_live
    ).astype(BF)
    a9.done()
    first_only = (s == 0).astype(F32)

    def norm1_back(r, f, weight):
        d = ar_full[f, :].astype(F32)
        xhat = (rows[r, :].astype(F32) - stat[r, 0:1]) * stat[r, 1:2]
        gsum[pl.ds(0, 8), :] = gsum[pl.ds(0, 8), :] + fold(d * xhat) * weight
        gsum[pl.ds(8, 8), :] = gsum[pl.ds(8, 8), :] + fold(d) * weight
        return norm_back(d, xhat, stat[r, 1:2], vec[0:1, :])

    def prefix_back(i):
        r = pl.ds(pl.multiple_of(p0 + i * step, step), step)
        f = pl.ds(pl.multiple_of(a9.full + i * step, step), step)
        g = pl.ds(pl.multiple_of(s0 + i * step, step), step)
        on = (lax.broadcasted_iota(jnp.int32, (step, 1), 0) + i * step < live_count).astype(F32)
        d = norm1_back(r, f, first_only)
        gd[g, :] = ((dsum[pl.ds(pl.multiple_of(i * step, step), step), :].astype(F32) + d) * on).astype(BF)

    pl.loop(0, slots // step)(prefix_back)
    before_gifts = len(gifts_a)
    share_feats_a(0, gd, s0, slots)
    late_gifts = gifts_a.pop(before_gifts)
    ls_near = [
        remote(gd.at[pl.ds(s0, slots), out], ls_hbm.at[pl.ds(0, slots), out], at_y)
        for out, _ in y_blocks
    ]

    def last_before(c):
        cols = pl.ds(c, wide)
        r = pl.ds(s0, slots)
        db[r, cols] = (slope0[:, cols] * dot_nt(gd[r, :], wd[cols, :])).astype(BF)

    col_loop(nu, last_before)
    share_db(s0, slots)
    a11 = Total(slots, slots, slots, whole(slots))
    a11.start(up_back(s0, slots))
    askers = [at_x, at_p, at_y] + at_h
    for k, partner in enumerate(askers):
        pl.semaphore_signal(free.at[k], inc=1, device_id=partner, device_id_type=MESH)
    a10.finish()
    a11.middle()
    late_gifts[0].wait()
    share_qkv(t1, own + slots)
    passed.append(remote(late_gifts[1], late_gifts[1], at_core))
    ls_far = [
        remote(lxx.at[0, pl.ds(s0, slots), out], ls_hbm.at[pl.ds(slots, slots), out], at_y)
        for out, _ in y_blocks
    ]
    a10.done()
    gin_copies = []

    def rows_back(total, seg):
        t_at, s_at = (t0, s0) if seg == 0 else (t1, s1)
        t_in, s_in = (slots, 0) if seg == 0 else (0, span)

        def tokens(i):
            r = pl.ds(pl.multiple_of(t_at + my_toks + i * step, step), step)
            f = pl.ds(pl.multiple_of(total.full + t_in + i * step, step), step)
            x = norm1_back(r, f, 1.0)
            mid[r, :] = mid[r, :] + x

        pl.loop(0, toks // step)(tokens)
        gin_copies.append(local(mid.at[pl.ds(t_at + my_toks, toks), my_cols], gin_hbm.at[seg]))

        def summaries(i):
            r = pl.ds(pl.multiple_of(s_at + i * step, step), step)
            f = pl.ds(pl.multiple_of(total.full + s_in + i * step, step), step)
            x = norm1_back(r, f, first_only) + mid[r, :]
            e = pl.ds(pl.multiple_of(i * step, step), step)
            emb_wide[e, :] = x if seg == 1 else emb_wide[e, :] + x

        pl.loop(0, slots // step)(summaries)

    emb_wide = slope0
    for copy in [rs_own, rs_far]:
        copy.wait()
    for copy in ls_near:
        copy.wait()
    for copy in ls_far:
        copy.wait()
    ls_core = remote(ls_hbm.at[:, my_cols], ls_hbm.at[:, my_cols], at_core)
    rs_in = local(rs_hbm, ar_own.at[pl.ds(0, 2 * slots), :])
    came = [early_in(0)]
    a_early(1)
    rows_back(a10, 1)
    pass_end()
    ls_core.wait()
    ls_in = local(ls_hbm, dsum)
    a11.finish()
    for k in range(len(askers)):
        pl.semaphore_wait(free.at[k], 1)
    a11.done()
    rs_in.wait()
    ls_in.wait()
    a_second(0, came[0])
    for copy in thin_act1:
        copy.wait()
    x_act1 = remote(la_hbm.at[:, my_quarter], la_hbm.at[:, my_quarter], at_x)
    leave_ffn(a11, s0, slots)
    mix_back(s0, slots)
    share_feats_b(gm, lm_hbm, s0, slots)
    a_early(2)
    attend_back(0)
    share_qkv(0, own)
    a12 = Total(own, 2 * slots + T + own, 2 * slots + T + own, [(0, slots, False), (slots, T, True)])
    a12.start(in_back(s0, own, 0))
    a12.middle()
    x_act1.wait()
    core_act1 = remote(la_hbm.at[:, my_cols], la_hbm.at[:, my_cols], at_core)
    a_second(1, early_in(1))
    a_early(3)
    for copy in thin_act2:
        copy.wait()
    to_x = remote(lxx.at[1, :, my_quarter], lxx.at[1, :, my_quarter], at_x)
    pass_on(gifts_b)
    stage = [local(mx_hbm, dmix)]
    pass_end()
    stage.append(local(lm_hbm, ar_full.at[pl.ds(0, p0), :]))
    a12.finish()
    for copy in stage:
        copy.wait()
    b_first(0)
    b_first(1)
    ones = jnp.ones((8, p0), BF)
    column = lambda ref, cols: jnp.dot(ones, ref[pl.ds(0, p0), cols], preferred_element_type=F32)[0:1, :]
    base = slots
    small_out[base + 2 : base + 3, :] = column(gm, my_quarter)
    small_out[base + 5 : base + 6, :] = column(gd, my_quarter)
    small_out[base + 3 : base + 4, :] = jnp.sum(fsum[pl.ds(0, 8), my_quarter], axis=0, keepdims=True)
    small_out[base + 4 : base + 5, :] = jnp.sum(fsum[pl.ds(8, 8), my_quarter], axis=0, keepdims=True)
    small_out[base + 6 : base + 7, :] = column(dqkv, pl.ds(0, nq))
    small_out[base + 7 : base + 8, :] = column(dqkv, pl.ds(2 * nq, nq)) + jnp.sum(
        dqkv[pl.ds(p0, slots), pl.ds(2 * nq, nq)].astype(F32), axis=0, keepdims=True
    )
    for k in range(nu // quarter):
        small_out[base + 8 + k : base + 9 + k, :] = column(db, pl.ds(k * quarter, quarter))
    small_out[base + 12 : base + 16, :] = jnp.zeros((4, quarter), F32)
    a12.done()
    rows_back(a12, 0)
    small_out[pl.ds(0, slots), :] = emb_wide[:, my_quarter]
    its_quarter = pl.ds(pl.multiple_of(t * half + (1 - s) * quarter, quarter), quarter)
    gx_send[0:1, :] = jnp.sum(gsum[pl.ds(0, 8), its_quarter], axis=0, keepdims=True)
    gx_send[1:2, :] = jnp.sum(gsum[pl.ds(8, 8), its_quarter], axis=0, keepdims=True)
    gx_send[2:8, :] = jnp.zeros((6, quarter), F32)
    copy = remote(gx_send, gx_recv, at_x)
    copy.wait()
    small_out[base : base + 1, :] = gx_recv[0:1, :] + jnp.sum(gsum[pl.ds(0, 8), my_quarter], axis=0, keepdims=True)
    small_out[base + 1 : base + 2, :] = gx_recv[1:2, :] + jnp.sum(gsum[pl.ds(8, 8), my_quarter], axis=0, keepdims=True)
    small_step(0)
    to_x.wait()
    to_core = remote(lxx.at[1, :, my_cols], lxx.at[1, :, my_cols], at_core)
    pass_on(gifts_a)
    to_core.wait()
    a_first(4)
    a_second(2, early_in(2))
    for copy in gifts_q:
        copy.wait()
    core_act1.wait()
    stage = [local(la_hbm, rows), local(ra_hbm, qkv.at[:, pl.ds(0, 3 * hq)])]
    a_third(0, 0)
    for copy in stage:
        copy.wait()
    a_second(3, early_in(3))
    a_first(5)
    a_third(0, 1)

    def turn(it, lag, first, count, stage):
        @pl.when((it >= first + lag) & (it < lag + count))
        def _():
            stage(it - lag)

    turns = tiles_a + 2 * nh

    @pl.loop(0, turns)
    def _(it):
        turn(it, -4, 4, tiles_a, a_second)
        turn(it, -6, 6, tiles_a, a_first)
        turn(it, 1, 0, tiles_b, b_second)
        for k in range(nh):
            turn(it, 2 * k - 2, 0 if k else 2, tiles_a, functools.partial(a_third, k))
        turn(it, 2 * nh - 2, 0, tiles_a, a_fourth)
        turn(it, 2 * nh, 0, tiles_a, a_fifth)
        for k in range(nh):
            turn(it, 3 + 2 * k, 0, tiles_b, functools.partial(b_third, k))
        turn(it, 3 + 2 * nh, 0, tiles_b, b_fourth)
        for k in range(1, len(small_partners) + 1):

            @pl.when(it == 2 * k - 1)
            def _():
                small_step(k)

    assert counter["l"] <= lsem.shape[0] and counter["r"] <= rsem.shape[0]

    for copy in gin_copies:
        copy.wait()

    @pl.loop(0, tiles_a)
    def _(i):
        for copy in outs_a(i, range(4)):
            copy.wait()

    @pl.loop(0, tiles_b)
    def _(i):
        for copy in outs_b(i, range(2)):
            copy.wait()

def chain(count, emb, dsum, feat_vecs, bq, bv, bu, hid, dhid, wq, wk, wv, wo, wu, wd):
    bits = lax.axis_size("batch").bit_length() - 1
    toks, slots = hid.shape[1], emb.shape[0] + -emb.shape[0] % 64
    half = hid.shape[2]
    feats, quarter = 2 * half, half // 2
    nq, nu = wo.shape[0] // 2, wd.shape[0] // 2
    own = 2 * toks + slots
    main, end = 2 * own, 2 * own + slots
    sums = 2 * slots + 2 * toks + 2 * own
    chunk = feats >> bits
    nh = bits - 2
    ta, tb = 2 * nu // nq + 3, 2
    vm = pltpu.VMEM
    sds = jax.ShapeDtypeStruct
    dma = pltpu.SemaphoreType.DMA
    scratch = [
        vm((feats, 3 * nq), BF),
        vm((nq, feats), BF),
        vm((feats, nu), BF),
        vm((nu, feats), BF),
        vm((end, feats), BF),
        vm((end, feats), BF),
        vm((end, 3 * nq), BF),
        vm((2, nq // HD, own, own + slots), BF),
        vm((main, nq), BF),
        vm((main, feats), F32),
        vm((main, feats), BF),
        vm((main, nu), BF),
        vm((main, nu), BF),
        vm((slots, nu), F32),
        vm((main, feats), BF),
        vm((main, feats), BF),
        vm((main, nq), BF),
        vm((end, 3 * nq), BF),
        vm((2 * slots, feats), BF),
        vm((8, feats), F32),
        vm((1, 3 * nq + nu), F32),
        vm((end, 128), F32),
        vm((max(3 * toks, (slots + 16) * ((bits + 2) // 2)), half), F32),
        vm((16, feats), F32),
        vm((16, feats), F32),
        vm((8, quarter), F32),
        vm((8, quarter), F32),
        vm((sums + 2 * toks + own, half), BF),
        vm((sums + 2 * toks + own, half), BF),
        vm((sums + 2 * toks + own, half), BF),
        vm((sums, feats), BF),
        vm((2 * toks + own, half), BF),
        vm((2, main, feats), BF),
        vm((main, nu), BF),
        vm((2 * chunk if chunk % 128 else 8, nq // 2), F32),
        vm((slots + 16, quarter), F32),
        dma((6,)),
        dma((16,)),
        dma((113, 2)),
        pltpu.SemaphoreType.REGULAR((3 + nh,)),
        dma((ta, 2)),
        dma((nh, ta, 2)),
        dma((ta, 2)),
        dma((ta, 2, 2)),
        dma((tb, 2)),
        dma((nh, tb, 2)),
        dma((tb, 2)),
        dma((ta, 4)),
        dma((tb, 2)),
        dma((bits + 1, 2)),
        vm((2, feats // 2, nq // 2), BF),
        vm(emb.shape, BF),
        vm(dsum.shape, BF),
        [vm(v.shape, BF) for v in feat_vecs + [bq, bv, bu]],
        dma((len(feat_vecs) + 5,)),
    ]
    vmem = pl.BlockSpec(memory_space=pltpu.VMEM)
    hbm = pl.BlockSpec(memory_space=pl.ANY)
    smem = pl.BlockSpec(memory_space=pltpu.SMEM)
    return pl.pallas_call(
        functools.partial(chain_kernel, bits),
        name="layer",
        out_shape=(
            sds((2, toks, half), BF),
            sds((2, slots, half), BF),
            sds((2, toks, half), F32),
            sds((2, slots + 16, quarter), F32),
            sds((chunk // 2, 8 * nq + 4 * nu), BF),
            sds((end, feats), BF),
            sds((main, feats), BF),
            sds((end, 3 * nq // 2), BF),
            sds((main, nq), BF),
            sds((4, feats // 2, nq // 2), BF),
            sds((2 * slots, feats), BF),
            sds((2 * slots, nu // 2), BF),
        ),
        in_specs=[smem, hbm, hbm, [hbm] * 6, hbm, hbm, hbm] + [hbm] * 8,
        out_specs=(vmem, vmem, hbm, vmem) + (hbm,) * 8,
        scratch_shapes=scratch,
        compiler_params=pltpu.CompilerParams(
            collective_id=2, has_side_effects=True, vmem_limit_bytes=63 * 2**20
        ),
    )(count, emb, dsum, feat_vecs, bq, bv, bu, hid, dhid, wq, wk, wv, wo, wu, wd)


def place_kernel(
    hid, sums, gin, small, w, hid_o, sum_o, gin_o, emb_o, vec_o, bup_o, q_o, k_o, v_o, o_o, u_o, d_o,
    hid_v, sum_v, gin_v, small_v, w_v, wide_v, tall_v, sem,
):
    n, wide = q_o.shape[1], u_o.shape[1]
    sections = [(k * n, n) for k in range(4)] + [(4 * n, wide), (4 * n + wide, wide)]
    copy = pltpu.make_async_copy
    ins = []
    for k, (at, m) in enumerate(sections):
        cols = pl.ds(at, m)
        ins.append(copy(w.at[:, cols], w_v.at[:, cols], sem.at[k]))
    plain = ((hid, hid_v), (gin, gin_v), (sums, sum_v), (small, small_v))
    plain = [copy(src, dst, sem.at[6 + k]) for k, (src, dst) in enumerate(plain)]
    order = (5, 4, 3, 0, 1, 2)
    for k in order:
        ins[k].start()
    for c in plain:
        c.start()
    outs = []

    def send(src, dst):
        c = copy(src, dst, sem.at[10 + len(outs)])
        c.start()
        outs.append(c)

    for k in order:
        at, m = sections[k]
        cols = pl.ds(at, m)
        ins[k].wait()
        x = w_v[:, cols].astype(F32)
        if k in (3, 5):
            there = tall_v.at[pl.ds(0, m), :] if k == 5 else tall_v.at[pl.ds(wide, m), :]
            there[...] = x.T
        else:
            there = wide_v.at[:, cols]
            there[...] = x
        send(there, (q_o, k_o, v_o, o_o, u_o, d_o)[k])
    for c in plain[:2]:
        c.wait()
    send(hid_v, hid_o.at[0])
    send(gin_v, gin_o.at[0])
    for c in plain[2:]:
        c.wait()
    used = sum_o.shape[0]
    for seg in range(2):
        sum_o[:, seg, :] = sum_v[seg, :used, :]
    quarter = small_v.shape[2]
    base = small_v.shape[1] - 16
    nu = bup_o.shape[0] // 2
    for side in range(2):
        at = pl.ds(side * quarter, quarter)
        emb_o[:, at] = small_v[side, :used, :]
        for k, ref in enumerate(vec_o):
            ref[at] = small_v[side, base + k]
        for k in range(nu // quarter):
            bup_o[pl.ds(side * nu + k * quarter, quarter)] = small_v[side, base + 8 + k]
    for c in outs:
        c.wait()


def place(hid, sums, gin, small, w, used):
    sds = jax.ShapeDtypeStruct
    _, toks, half = hid.shape
    rows = w.shape[0]
    nu = (w.shape[1] - 4 * half) // 4
    vmem = pl.BlockSpec(memory_space=pltpu.VMEM)
    hbm = pl.BlockSpec(memory_space=pl.ANY)
    vm = pltpu.VMEM
    return pl.pallas_call(
        place_kernel,
        name="place",
        out_shape=(
            sds((1, 2, toks, half), BF),
            sds((used, 2, half), BF),
            sds((1, 2, toks, half), F32),
            sds((used, half), F32),
            [sds((half,), F32)] * 8,
            sds((2 * nu,), F32),
            sds((rows, half), F32),
            sds((rows, half), F32),
            sds((rows, half), F32),
            sds((half, rows), F32),
            sds((rows, 2 * nu), F32),
            sds((2 * nu, rows), F32),
        ),
        in_specs=[hbm] * 5,
        out_specs=(hbm, vmem, hbm, vmem, [vmem] * 8, vmem) + (hbm,) * 6,
        scratch_shapes=[
            vm(hid.shape, BF),
            vm(sums.shape, BF),
            vm(gin.shape, F32),
            vm(small.shape, F32),
            vm(w.shape, BF),
            vm((rows, 4 * half + 2 * nu), F32),
            vm((2 * nu + half, rows), F32),
            pltpu.SemaphoreType.DMA((18,)),
        ],
        compiler_params=pltpu.CompilerParams(vmem_limit_bytes=60 * 2**20),
    )(hid, sums, gin, small, w)


def local(
    hidden_in, summary_counts, summary_embed, ln1_gain, ln1_bias, w_query, b_query, w_key, w_value,
    b_value, w_out, b_out, ln2_gain, ln2_bias, w_up, b_up, w_down, b_down, d_hidden, d_summary,
):
    got = chain(
        summary_counts, summary_embed, d_summary[0].transpose(1, 0, 2),
        [ln1_gain, ln1_bias, ln2_gain, ln2_bias, b_out, b_down], b_query, b_value, b_up,
        hidden_in[0], d_hidden[0], w_query, w_key, w_value, w_out, w_up, w_down,
    )
    hid, sums, gin, emb, vecs, bup, gq, gk, gv, go, gu, gd = place(*got[:5], summary_embed.shape[0])
    return (
        hid, sums.transpose(1, 0, 2)[None], gin, emb, vecs[0], vecs[1], gq, vecs[6], gk, gv,
        vecs[7], go, vecs[2], vecs[3], vecs[4], gu, bup, gd, vecs[5],
    )


def solution(mesh):
    return jax.shard_map(
        local,
        mesh=mesh,
        in_specs=(
            P("batch", None, "seq", "tensor"),
            P("batch"),
            P(None, "tensor"),
            P("tensor"),
            P("tensor"),
            P(None, "tensor"),
            P("tensor"),
            P(None, "tensor"),
            P(None, "tensor"),
            P("tensor"),
            P("tensor", None),
            P("tensor"),
            P("tensor"),
            P("tensor"),
            P(None, "tensor"),
            P("tensor"),
            P("tensor", None),
            P("tensor"),
            P("batch", None, "seq", "tensor"),
            P("batch", None, None, "tensor"),
        ),
        out_specs=(
            P("batch", None, "seq", "tensor"),
            P("batch", None, None, "tensor"),
            P("batch", None, "seq", "tensor"),
            P(None, "tensor"),
            P("tensor"),
            P("tensor"),
            P(("batch", "seq"), "tensor"),
            P("tensor"),
            P(("batch", "seq"), "tensor"),
            P(("batch", "seq"), "tensor"),
            P("tensor"),
            P("tensor", ("batch", "seq")),
            P("tensor"),
            P("tensor"),
            P("tensor"),
            P(("batch", "seq"), "tensor"),
            P("tensor"),
            P("tensor", ("batch", "seq")),
            P("tensor"),
        ),
        check_vma=False,
    )
```

```python
import functools

import jax
import jax.numpy as jnp
from jax import lax
from jax.experimental import pallas as pl
from jax.experimental.pallas import tpu as pltpu
from jax.sharding import PartitionSpec as P

HD = 64
EPSILON = 1e-05
NEGATIVE = -1e30
MESH = pl.DeviceIdType.MESH
BF = jnp.bfloat16
F32 = jnp.float32
PAIR_BIT = 1


def flip(index, bit):
    weight = 1 << bit
    return index + weight - 2 * weight * lax.rem(index // weight, 2)


def bit_of(index, bit):
    return lax.rem(index // (1 << bit), 2)


def dot_nt(a, b):
    return lax.dot_general(a, b, (((1,), (1,)), ((), ())), preferred_element_type=F32)


def dot_tn(a, b):
    return lax.dot_general(a, b, (((0,), (0,)), ((), ())), preferred_element_type=F32)


class Strips:
    def __init__(self, refs, width):
        self.width = width
        self.free = [[ref, ref.shape[0], at, 0] for ref in refs for at in range(ref.shape[1] // width)]

    def take(self, tiles, n, unit):
        for k, (ref, height, at, used) in enumerate(self.free):
            if height < n:
                continue
            if used + tiles * n <= height:
                self.free[k][3] += tiles * n
                return Slab(ref, at, used, tiles, n, unit, self.width)
            per = height // n
            need = -(-tiles // per)
            run = self.free[k : k + need]
            if len(run) == need and all(r[0] is ref and r[3] == 0 for r in run):
                for r in run:
                    r[3] = height
                run[-1][3] = (tiles - per * (need - 1)) * n
                return Slab(ref, at, 0, per, n, unit, self.width)
        raise ValueError("no room")


class Slab:
    def __init__(self, ref, strip, start, per, n, unit, width):
        self.ref, self.strip, self.start, self.per = ref, strip, start, per
        self.n, self.unit, self.width = n, unit, width

    def at(self, i, lo, n):
        first = pl.multiple_of(self.start + (i % self.per) * self.n + lo, self.unit)
        col = pl.multiple_of((self.strip + i // self.per) * self.width, self.width)
        return self.ref.at[pl.ds(first, n), pl.ds(col, self.width)]

    def __call__(self, i):
        return self.at(i, 0, self.n)


def chain_kernel(
    bits,
    count_ref,
    emb_ref,
    dsum_ref,
    feat_refs,
    bq_ref,
    bv_ref,
    bu_ref,
    hid_hbm,
    dhid_hbm,
    wq_hbm,
    wk_hbm,
    wv_hbm,
    wo_hbm,
    wu_hbm,
    wd_hbm,
    hid_out,
    sum_out,
    gin_hbm,
    small_final,
    w_hbm,
    la_hbm,
    lm_hbm,
    ra_hbm,
    mx_hbm,
    ye_hbm,
    ls_hbm,
    rs_hbm,
    wqkv,
    wo,
    wu,
    wd,
    rows,
    act1,
    qkv,
    probs,
    mix,
    mid,
    act2,
    actv,
    db,
    slope0,
    gd,
    gm,
    dmix,
    dqkv,
    dsum,
    vec,
    bias,
    stat,
    outacc,
    fsum,
    gsum,
    gx_send,
    gx_recv,
    ar_send,
    ar_core,
    ar_x,
    ar_full,
    ar_own,
    lxx,
    rbx,
    both,
    small_out,
    wsem,
    lsem,
    rsem,
    free,
    sem_y,
    sem_za,
    sem_pa,
    sem_xa,
    sem_pb,
    sem_zb,
    sem_xb,
    sem_oa,
    sem_ob,
    sem_s,
    early,
    emb_v,
    dsum_v,
    vecs_v,
    isem,
):
    b, s, t = lax.axis_index("batch"), lax.axis_index("seq"), lax.axis_index("tensor")
    at_core = (b, s, 1 - t)
    at_x = (b, 1 - s, t)
    at_p = (flip(b, PAIR_BIT), s, t)
    at_y = (flip(b, 0), s, t)
    halving = list(range(bits - 1, PAIR_BIT, -1))
    at_h = [(flip(b, bit), s, t) for bit in halving]
    zl, y = bit_of(b, PAIR_BIT), bit_of(b, 0)
    halving_down = list(range(bits - 2, 0, -1))
    at_d = (flip(b, bits - 1), s, t)
    zd = bit_of(b, bits - 1)
    count = len(feat_refs)
    small_ins = [(emb_ref, emb_v), (dsum_ref, dsum_v)]
    small_ins += list(zip(list(feat_refs) + [bq_ref, bv_ref, bu_ref], vecs_v))
    small_ins = [
        pltpu.make_async_copy(src, dst, isem.at[k]) for k, (src, dst) in enumerate(small_ins)
    ]
    for copy in small_ins:
        copy.start()
    feat_refs, (bq_ref, bv_ref, bu_ref) = vecs_v[:count], vecs_v[count:]
    emb_ref, dsum_ref = emb_v, dsum_v
    barrier = pltpu.get_barrier_semaphore()
    partners = [at_core, at_x, at_p, at_y] + at_h
    for partner in partners:
        pl.semaphore_signal(barrier, inc=1, device_id=partner, device_id_type=MESH)

    toks = hid_hbm.shape[1]
    slots = slope0.shape[0]
    used = emb_ref.shape[0]
    feats = rows.shape[1]
    half = feats // 2
    quarter = feats // 4
    span = 2 * toks
    s0, t0, t1, s1, p0 = 0, slots, slots + span, slots + 2 * span, 2 * slots + 2 * span
    own = slots + span
    end = p0 + slots
    nq = wo.shape[0]
    nu = wu.shape[1]
    my_cols = pl.ds(pl.multiple_of(t * half, half), half)
    its_cols = pl.ds(pl.multiple_of((1 - t) * half, half), half)
    my_toks = pl.multiple_of(s * toks, toks)
    its_toks = pl.multiple_of((1 - s) * toks, toks)
    my_quarter = pl.ds(pl.multiple_of(t * half + s * quarter, quarter), quarter)

    counter = {"l": 0, "r": 0}

    def local(src, dst):
        counter["l"] += 1
        copy = pltpu.make_async_copy(src, dst, lsem.at[counter["l"] - 1])
        copy.start()
        return copy

    def remote(src, dst, partner):
        counter["r"] += 1
        at = counter["r"] - 1
        copy = pltpu.make_async_remote_copy(
            src_ref=src,
            dst_ref=dst,
            send_sem=rsem.at[at, 0],
            recv_sem=rsem.at[at, 1],
            device_id=partner,
            device_id_type=MESH,
        )
        copy.start()
        return copy

    part = lambda ref, n, axis: (
        ref.at[:, pl.ds(pl.multiple_of(s * n, n), n)]
        if axis
        else ref.at[pl.ds(pl.multiple_of(s * n, n), n), :]
    )
    weights = []
    for at, (src, dst) in enumerate(
        (
            (part(wq_hbm, nq, 1), wqkv.at[:, pl.ds(0, nq)]),
            (part(wk_hbm, nq, 1), wqkv.at[:, pl.ds(nq, nq)]),
            (part(wv_hbm, nq, 1), wqkv.at[:, pl.ds(2 * nq, nq)]),
            (part(wo_hbm, nq, 0), wo),
            (part(wu_hbm, nu, 1), wu),
            (part(wd_hbm, nu, 0), wd),
        )
    ):
        copy = pltpu.make_async_copy(src, dst, wsem.at[at])
        weights.append(copy)

    firsts = []
    for seg, at in enumerate((t0, t1)):
        firsts.append(local(hid_hbm.at[seg], rows.at[pl.ds(at + my_toks, toks), my_cols]))
    laters = []
    for seg, at in enumerate((t0, t1)):
        laters.append(local(dhid_hbm.at[seg], gd.at[pl.ds(at + my_toks, toks), my_cols]))
    for copy in weights[:3]:
        copy.start()
    for copy in small_ins:
        copy.wait()
    for at in (s0, s1):
        rows[pl.ds(at, slots), my_cols] = jnp.zeros((slots, half), BF)
        rows[pl.ds(at, used), my_cols] = emb_ref[...]
    for seg in range(2):
        dsum[pl.ds(seg * slots, slots), my_cols] = jnp.zeros((slots, half), BF)
        dsum[pl.ds(seg * slots, used), my_cols] = dsum_ref[:, seg, :]
    for k, ref in enumerate(feat_refs):
        vec[k : k + 1, my_cols] = ref[...].astype(F32)[None]
    pl.semaphore_wait(barrier, len(partners))

    def in_x(src, dst, at):
        return remote(src, dst.at[pl.ds(at + my_toks, toks), my_cols], at_x)

    def in_core(block):
        return remote(block, block, at_core)

    def in_pass(dst, at):
        return in_core(dst.at[pl.ds(at + its_toks, toks), my_cols])

    x_hid = [in_x(hid_hbm.at[0], rows, t0)]
    from_core = [
        in_core(rows.at[pl.ds(s0, slots), my_cols]),
        in_core(vec.at[:, my_cols]),
        remote(hid_hbm.at[0], rows.at[pl.ds(t0 + my_toks, toks), my_cols], at_core),
    ]
    late_core = [
        in_core(rows.at[pl.ds(s1, slots), my_cols]),
        remote(hid_hbm.at[1], rows.at[pl.ds(t1 + my_toks, toks), my_cols], at_core),
        in_core(dsum.at[:, my_cols]),
    ]
    for src, dst, at in ((dhid_hbm.at[0], gd, t0), (dhid_hbm.at[1], gd, t1)):
        late_core.append(remote(src, dst.at[pl.ds(at + my_toks, toks), my_cols], at_core))
    for copy in weights[3:]:
        copy.start()

    live_count = count_ref[0]
    row_live = (lax.broadcasted_iota(jnp.int32, (slots, 1), 0) < live_count).astype(F32)
    dqkv[pl.ds(p0, slots), pl.ds(0, nq)] = jnp.zeros((slots, nq), BF)
    bias[:, pl.ds(nq, nq)] = jnp.zeros((1, nq), F32)
    for ref, at, n in ((bq_ref, 0, nq), (bv_ref, 2 * nq, nq), (bu_ref, 3 * nq, nu)):
        x = ref[...].astype(F32)[None]
        bias[:, pl.ds(at, n)] = jnp.where(s == 0, x[:, :n], x[:, n:])
    fsum[...] = jnp.zeros_like(fsum)
    gsum[...] = jnp.zeros_like(gsum)

    step = 16
    inverse = 1.0 / feats

    def row_loop(start, n, body):
        @pl.loop(0, n // step)
        def _(i):
            body(pl.ds(pl.multiple_of(start + i * step, step), step))

    def mean(x):
        return jnp.sum(x, axis=1, keepdims=True) * inverse

    def stats(x):
        m = mean(x)
        return m, lax.rsqrt(mean(x * x) - m * m + EPSILON)

    def norm1(start, n):
        def body(at):
            x = rows[at, :].astype(F32)
            m, r = stats(x)
            act1[at, :] = ((x - m) * r * vec[0:1, :] + vec[1:2, :]).astype(BF)
            stat[at, 0:1] = m
            stat[at, 1:2] = r

        row_loop(start, n, body)

    def norm_back(d, xhat, r, gain):
        q = d * gain
        return r * (q - mean(q) - xhat * mean(q * xhat))

    def fold(x):
        return jnp.sum(x.reshape(step // 8, 8, x.shape[1]), axis=0)

    wide = 512

    def col_loop(n, body):
        @pl.loop(0, n // wide)
        def _(j):
            body(pl.multiple_of(j * wide, wide))

    def project(at, n, lo, hi):
        def body(c):
            cols = pl.ds(pl.multiple_of(lo + c, wide), wide)
            x = jnp.dot(act1[pl.ds(at, n), :], wqkv[:, cols], preferred_element_type=F32)
            qkv[pl.ds(at, n), cols] = (x + bias[:, cols]).astype(BF)

        col_loop(hi - lo, body)

    class Total:
        def __init__(self, n, at, full, pieces, own_at=0):
            self.n, self.at, self.full, self.own_at = n, at, full, own_at
            self.pieces = pieces

        def mine(self, r, n):
            if self.full is None:
                return ar_own.at[pl.ds(self.own_at + r, n), :]
            return ar_full.at[pl.ds(self.full + r, n), my_cols]

        def start(self, product):
            at = pl.ds(self.at, self.n)

            def other(c):
                x = product(pl.multiple_of((1 - t) * half + c, wide), wide)
                ar_send[at, pl.ds(c, wide)] = x.astype(BF)

            col_loop(half, other)
            self.core = remote(ar_send.at[at, :], ar_core.at[at, :], at_core)

            def this(c):
                x = product(pl.multiple_of(t * half + c, wide), wide)
                if self.full is None:
                    ar_own[pl.ds(self.own_at, self.n), pl.ds(c, wide)] = x.astype(BF)
                else:
                    cols = pl.ds(pl.multiple_of(t * half + c, wide), wide)
                    ar_full[pl.ds(self.full, self.n), cols] = x.astype(BF)

            col_loop(half, this)

        def middle(self):
            self.core.wait()
            self.xs = []
            for base, n, scatter in self.pieces:
                at = pl.ds(self.at + base, n)
                ar_core[at, :] = (
                    self.mine(base, n)[...].astype(F32) + ar_core[at, :].astype(F32)
                ).astype(BF)
                if scatter:
                    src = ar_core.at[pl.ds(self.at + base + its_toks, toks), :]
                    dst = ar_x.at[pl.ds(self.at + base, toks), :]
                else:
                    src, dst = ar_core.at[at, :], ar_x.at[at, :]
                self.xs.append(remote(src, dst, at_x))

        def sums(self, base, n, scatter):
            if scatter:
                near = ar_core[pl.ds(self.at + base + my_toks, toks), :]
                far = ar_x[pl.ds(self.at + base, toks), :]
            else:
                near = ar_core[pl.ds(self.at + base, n), :]
                far = ar_x[pl.ds(self.at + base, n), :]
            return near.astype(F32) + far.astype(F32)

        def finish(self):
            self.backs = []
            for (base, n, scatter), copy in zip(self.pieces, self.xs):
                copy.wait()
                n = toks if scatter else n
                block = ar_full.at[pl.ds(self.full + base, n), my_cols]
                block[...] = self.sums(base, n, scatter).astype(BF)
                self.backs.append(remote(block, block, at_core))

        def done(self):
            for copy in self.backs:
                copy.wait()

        def flow(self, body, before_last=lambda: None):
            self.backs = []
            for k, ((base, n, _), copy) in enumerate(zip(self.pieces, self.xs)):
                if k == len(self.pieces) - 1:
                    before_last()
                copy.wait()
                block = ar_full.at[pl.ds(self.full + base, n), my_cols]
                block[...] = self.sums(base, n, False).astype(BF)
                self.backs.append(remote(block, block, at_core))
                if k:
                    self.backs[k - 1].wait()
                    body(*self.pieces[k - 1][:2])
            self.backs[-1].wait()
            body(*self.pieces[-1][:2])

    whole = lambda n: [(i, 64, False) for i in range(0, n, 64)]

    def out_product(at, n):
        return lambda c, w: jnp.dot(
            mix[pl.ds(at, n), :], wo[:, pl.ds(c, w)], preferred_element_type=F32
        )

    def down_product(at, n):
        return lambda c, w: jnp.dot(
            actv[pl.ds(at, n), :], wd[:, pl.ds(c, w)], preferred_element_type=F32
        )

    def up_back(at, n):
        return lambda c, w: dot_nt(db[pl.ds(at, n), :], wu[pl.ds(c, w), :])

    def in_back(at, n, lo):
        return lambda c, w: dot_nt(
            dqkv[pl.ds(at, n), pl.ds(lo, 3 * nq - lo)], wqkv[pl.ds(c, w), pl.ds(lo, 3 * nq - lo)]
        )

    def enter_ffn(total, at, n, base=0):
        def body(i):
            r = pl.ds(pl.multiple_of(at + base + i * step, step), step)
            f = pl.ds(pl.multiple_of(total.full + base + i * step, step), step)
            x = rows[r, :].astype(F32) + ar_full[f, :].astype(F32) + vec[4:5, :]
            m, rs = stats(x)
            mid[r, :] = x
            act2[r, :] = ((x - m) * rs * vec[2:3, :] + vec[3:4, :]).astype(BF)
            stat[r, 2:3] = m
            stat[r, 3:4] = rs

        pl.loop(0, n // step)(body)

    def gelu(v):
        c = 0.7978845608028654
        th = jnp.tanh(c * (v + 0.044715 * (v * v * v)))
        act = 0.5 * v * (1.0 + th)
        sl = 0.5 * (1.0 + th) + (0.5 * c) * v * (1.0 - th * th) * (1.0 + (3 * 0.044715) * v * v)
        return act, sl

    def ffn(at, n, back, lo, hi):
        r = pl.ds(at, n)

        def body(c):
            c = pl.multiple_of(lo + c, wide)
            cols = pl.ds(c, wide)
            v = jnp.dot(act2[r, :], wu[:, cols], preferred_element_type=F32)
            act, sl = gelu(v + bias[:, pl.ds(pl.multiple_of(3 * nq + c, wide), wide)])
            actv[r, cols] = act.astype(BF)
            if back == 1:
                db[r, cols] = (sl * dot_nt(gd[r, :], wd[cols, :])).astype(BF)
            elif back == 2:
                db[r, cols] = (sl * db[r, cols].astype(F32)).astype(BF)
            else:
                slope0[:, cols] = sl

        col_loop(hi - lo, body)

    def leave_ffn(total, at, n, base=0):
        def body(i):
            r = pl.ds(pl.multiple_of(at + base + i * step, step), step)
            f = pl.ds(pl.multiple_of(total.full + base + i * step, step), step)
            d = ar_full[f, :].astype(F32)
            xhat = (mid[r, :] - stat[r, 2:3]) * stat[r, 3:4]
            fsum[pl.ds(0, 8), :] = fsum[pl.ds(0, 8), :] + fold(d * xhat)
            fsum[pl.ds(8, 8), :] = fsum[pl.ds(8, 8), :] + fold(d)
            dm = gd[r, :].astype(F32) + norm_back(d, xhat, stat[r, 3:4], vec[2:3, :])
            mid[r, :] = dm
            gm[r, :] = dm.astype(BF)

        pl.loop(0, n // step)(body)

    def mix_back(at, n):
        dmix[pl.ds(at, n), :] = dot_nt(gm[pl.ds(at, n), :], wo[...]).astype(BF)

    pairs = nq // (2 * HD)
    scale = HD**-0.5

    def seen(seg, keys):
        q = lax.broadcasted_iota(jnp.int32, (own, keys), 0)
        k = lax.broadcasted_iota(jnp.int32, (own, keys), 1)
        if seg == 0:
            q = jnp.where(q < slots, q + span, q - slots)
            slot = k
            token = k >= slots
            k = jnp.where(token, k - slots, k + span)
            return (k <= q) & (token | (slot < live_count))
        token = k < span
        ahead = k >= own
        slot = jnp.where(ahead, k - own, k - span)
        return (ahead | (k <= q)) & (token | (slot < live_count))

    def lanes(n):
        first = (lax.broadcasted_iota(jnp.int32, (n, 2 * HD), 1) < HD).astype(F32)
        return first.astype(BF), (1.0 - first).astype(BF)

    def attend(seg):
        at, keys = (s0, own) if seg == 0 else (t1, own + slots)
        q_rows, k_rows = pl.ds(at, own), pl.ds(at, keys)

        @pl.loop(0, pairs)
        def _(j):
            col = lambda g: pl.ds(pl.multiple_of(g * nq + j * 2 * HD, 2 * HD), 2 * HD)
            q, k, v = qkv[q_rows, col(0)], qkv[k_rows, col(1)], qkv[k_rows, col(2)]
            first = lanes(keys)
            allowed = seen(seg, keys)
            got = jnp.zeros((own, 2 * HD), F32)
            for h in range(2):
                pick = first[h]
                sc = dot_nt(q, k * pick) * scale
                sc = jnp.where(allowed, sc, NEGATIVE)
                e = jnp.exp(sc - jnp.max(sc, axis=1, keepdims=True))
                p = (e / jnp.sum(e, axis=1, keepdims=True)).astype(BF)
                probs[seg, 2 * j + h, :, pl.ds(0, keys)] = p
                got += jnp.dot(p, v * pick, preferred_element_type=F32)
            mix[q_rows, pl.ds(pl.multiple_of(j * 2 * HD, 2 * HD), 2 * HD)] = got.astype(BF)

    def attend_back(seg):
        at, keys = (s0, own) if seg == 0 else (t1, own + slots)
        q_rows, k_rows = pl.ds(at, own), pl.ds(at, keys)

        @pl.loop(0, pairs)
        def _(j):
            col = lambda g: pl.ds(pl.multiple_of(g * nq + j * 2 * HD, 2 * HD), 2 * HD)
            q, k, v = qkv[q_rows, col(0)], qkv[k_rows, col(1)], qkv[k_rows, col(2)]
            d = dmix[q_rows, pl.ds(pl.multiple_of(j * 2 * HD, 2 * HD), 2 * HD)]
            first_k, first_q = lanes(keys), lanes(own)
            dq = jnp.zeros((own, 2 * HD), F32)
            dk = jnp.zeros((keys, 2 * HD), F32)
            dv = jnp.zeros((keys, 2 * HD), F32)
            for h in range(2):
                pick_k, pick_q = first_k[h], first_q[h]
                p = probs[seg, 2 * j + h, :, pl.ds(0, keys)]
                pf = p.astype(F32)
                dp = dot_nt(d, v * pick_k)
                ds = (pf * (dp - jnp.sum(pf * dp, axis=1, keepdims=True))).astype(BF)
                dq += jnp.dot(ds, k * pick_k, preferred_element_type=F32)
                dk += dot_tn(ds, q * pick_q)
                dv += dot_tn(p, d * pick_q)
            dqkv[q_rows, col(0)] = (dq * scale).astype(BF)
            dqkv[k_rows, col(1)] = (dk * scale).astype(BF)
            dqkv[k_rows, col(2)] = dv.astype(BF)

    gifts_a, gifts_b, passed = [], [], []
    hu = nu // 2
    chunk = feats >> bits
    chunks = 1 << (bits - 1)

    def share_feats_a(op, src, at, n):
        landing = lxx.at[op, pl.ds(at, n), my_cols]
        partner = at_d if op else at_p
        gifts_a.append((remote(src.at[pl.ds(at, n), my_cols], landing, partner), landing))

    def share_units_a(op, src, at, n):
        side = zd if op else zl
        its = pl.ds(pl.multiple_of((1 - side) * hu, hu), hu)
        landing = rbx.at[pl.ds(at, n), pl.ds(op * hu, hu)]
        partner = at_d if op else at_p
        gifts_a.append((remote(src.at[pl.ds(at, n), its], landing, partner), None))

    y_blocks = [(my_cols, my_cols)]
    if chunk % 128 == 0:
        block = lambda c: pl.ds(pl.multiple_of(c * chunk, chunk), chunk)
        y_blocks = [2 * (t * chunks // 2 + m) for m in range(chunks // 2)]
        y_blocks = [(block(c + 1 - y), block(c + y)) for c in y_blocks]

    def share_feats_b(src, dst, at, n):
        for out, back in y_blocks:
            copy = remote(src.at[pl.ds(at, n), out], dst.at[pl.ds(at, n), out], at_y)
            gifts_b.append((copy, dst.at[pl.ds(at, n), back]))

    def share_units_b(src, dst, at, n):
        gifts_b.append((remote(src.at[pl.ds(at, n), :], dst.at[pl.ds(at, n), :], at_y), None))

    def pass_on(gifts, most=1000):
        while gifts and most:
            most -= 1
            copy, landing = gifts.pop(0)
            copy.wait()
            if landing is not None:
                passed.append(remote(landing, landing, at_core))

    def pass_end():
        while passed:
            passed.pop(0).wait()

    def share_thin(src, dst, at, n, partner):
        block = dst.at[pl.ds(at, n), my_quarter]
        return remote(src.at[pl.ds(at, n), my_quarter], block, partner)

    gifts_q, thin_act1, thin_act2 = [], [], []
    hq = nq // 2

    def share_qkv(at, n):
        for g in range(3):
            its = pl.ds(pl.multiple_of(g * nq + (1 - zl) * hq, hq), hq)
            landing = ra_hbm.at[pl.ds(at, n), pl.ds(g * hq, hq)]
            gifts_q.append(remote(dqkv.at[pl.ds(at, n), its], landing, at_p))

    share_mix = lambda at, n: share_units_b(mix, mx_hbm, at, n)
    share_actv = lambda at, n: share_units_a(0, actv, at, n)
    share_db = lambda at, n: share_units_a(1, db, at, n)

    width = nq // 2
    near = chunk // 2
    per = hu // width
    tiles_a, tiles_b = 2 * per + 3, nq // width
    assert per == 4 and hq == width

    def kind_of(i):
        later = (i // per + 1) // 2
        return 1 - later, later * (i % 2), (1 - later) * i + later * ((i - per) // 2)


    nh = len(halving)
    strips = Strips([wu, wd], width)
    recv_y = strips.take(tiles_a, chunks * chunk, near)
    slots_y = 4
    send_y = strips.take(slots_y, chunks * chunk, near)
    recv_za = [strips.take(tiles_a, chunks * chunk >> (k + 1), near) for k in range(nh)]
    recv_pb = strips.take(tiles_b, chunks * chunk // 2, near)
    recv_zb = [strips.take(tiles_b, chunks * chunk >> (k + 2), near) for k in range(nh)]
    recv_px = strips.take(tiles_a, 2 * chunk, near)
    send_zd = strips.take(per, chunks * chunk // 2, near)
    recv_xb = strips.take(tiles_b, near, near)
    strips = Strips([wqkv, wo], width)
    send_za = [strips.take(tiles_a, chunks * chunk >> (k + 1), near) for k in range(nh)]
    send_pb = strips.take(tiles_b, chunks * chunk // 2, near)
    send_zb = [strips.take(tiles_b, chunks * chunk >> (k + 2), near) for k in range(nh)]
    send_pa = strips.take(tiles_a, chunk, near)

    def linked(src, dst, sem, partner):
        return pltpu.make_async_remote_copy(
            src_ref=src,
            dst_ref=dst,
            send_sem=sem.at[0],
            recv_sem=sem.at[1],
            device_id=partner,
            device_id_type=MESH,
        )

    copy_y = lambda i: linked(send_y(i % slots_y), recv_y(i), sem_y.at[i], at_y)
    def by_kind(i, far, close):
        down, inner, _ = kind_of(i)
        return close + (1 - down - inner) * (far - close)

    def copy_za(k, i, down=False):
        to = by_kind(i, flip(b, halving_down[k]), flip(b, halving[k]))
        src = send_zd if down else send_za[k]
        return linked(src(i), recv_za[k](i), sem_za.at[k, i], (to, s, t))

    def copy_pa(i):
        to = by_kind(i, at_d[0], at_p[0])
        return linked(send_pa(i), recv_px.at(i, 0, chunk), sem_pa.at[i], (to, s, t))

    def place_bit(j, k, value):
        low = 1 << k
        return (j // low) * 2 * low + value * low + j % low

    copy_pb = lambda i: linked(send_pb(i), recv_pb(i), sem_pb.at[i], at_p)
    copy_zb = lambda k, i: linked(send_zb[k](i), recv_zb[k](i), sem_zb.at[k, i], at_h[k])

    def block_product(lefts, rights, c):
        def dots(cols):
            x = dot_tn(lefts[0](cols), rights[0])
            for left, right in zip(lefts[1:], rights[1:]):
                x = x + dot_tn(left(cols), right)
            return x

        if chunk % 128 == 0:
            return dots(pl.ds(pl.multiple_of(c * chunk, chunk), chunk))
        both[...] = dots(pl.ds(pl.multiple_of((c // 2) * 2 * chunk, 2 * chunk), 2 * chunk))
        return both[pl.ds(pl.multiple_of((c % 2) * chunk, chunk), chunk), :]

    main = p0

    def products_a(i, parts, early=False):
        down, inner, k = kind_of(i)
        tile = lambda c: pl.ds(pl.multiple_of(c, width), width)
        cases = (
            (gd, lxx.at[0], actv, zl * hu + k * width, rbx, k * width),
            (act2, lxx.at[1], db, zd * hu + k * width, rbx, hu + k * width),
            (act1, rows, dqkv, k * nq + zl * hq, qkv, k * width),
        )
        for op, (near_l, far_l, near_r, near_at, far_r, far_at) in enumerate(cases):

            @pl.when((1 - down) * (1 + inner) == op)
            def _():
                at = pl.ds(slots, main - slots) if early and op == 0 else slice(None)
                rights = [near_r[at, tile(near_at)], far_r[at, tile(far_at)]]
                lefts = [lambda cols: near_l[at, cols], lambda cols: far_l[at, cols]]
                if op == 0 and not early:
                    rights.append(ar_own[pl.ds(0, 2 * slots), tile(k * width)])
                    lefts.append(lambda cols: dsum[:, cols])
                for n, which, put, after in parts(op):

                    @pl.loop(0, n)
                    def _(j):
                        put(j, block_product(lefts, rights, which(j)))

                    after()

    def products_b(i, parts):
        cols = pl.ds(pl.multiple_of(i * width, width), width)
        r1, r2 = mix[:, cols], dmix[:, cols]
        l1, l2 = (lambda at: gm[:, at]), (lambda at: ar_full[pl.ds(0, p0), at])
        for n, which, put, after in parts:

            @pl.loop(0, n)
            def _(j):
                put(j, block_product((l1, l2), (r1, r2), which(j)))

            after()

    def copy_early(i):
        return linked(early.at[i % 2], ye_hbm.at[i], sem_y.at[i], at_y)

    def a_early(i):
        def put(j, v):
            early[i % 2, pl.ds(pl.multiple_of(j * chunk, chunk), chunk), :] = v.astype(BF)

        if i >= 2:
            copy_early(i - 2).wait_send()
        part = (chunks, lambda j: 2 * j + 1 - y, put, lambda: copy_early(i).start())
        products_a(i, lambda op: [part], True)

    def early_in(i):
        if i >= 2:
            copy_early(i).wait_send()
        copy_early(i).wait_recv()
        return local(ye_hbm.at[i], recv_y(i))

    def a_first(i):
        def put(j, v):
            send_y.at(i % slots_y, j * chunk, chunk)[...] = v.astype(BF)

        part = (chunks, lambda j: 2 * j + 1 - y, put, lambda: copy_y(i).start())
        products_a(i, lambda op: [part])

    def a_second(i, came=None):
        (copy_y(i) if came is None else came).wait()
        n = chunks // 2

        def parts(op):
            bit = bit_of(b, (halving_down if op == 1 else halving)[0])
            k = bits - 3 if op == 1 else bits - 2
            other = lambda j: place_bit(j, k, 1 - bit)
            mine = lambda j: place_bit(j, k, bit)

            def total(v, at):
                return (v + recv_y.at(i, at * chunk, chunk)[...].astype(F32)).astype(BF)

            def give(j, v):
                give_to = send_za[0] if op else send_zd
                give_to.at(i, j * chunk, chunk)[...] = total(v, other(j))

            def keep(j, v):
                x = total(v, mine(j))
                recv_y.at(i, j * chunk, chunk)[...] = x

            return [
                (n, lambda j: 2 * other(j) + y, give, lambda: copy_za(0, i, op == 0).start()),
                (n, lambda j: 2 * mine(j) + y, keep, lambda: None),
            ]

        products_a(i, parts)

    def halve(i, kept, at, recv, n, give, copy, k, bit):
        def total(c):
            x = kept.at(i, (at + c) * chunk, chunk)[...].astype(F32)
            return (x + recv.at(i, c * chunk, chunk)[...].astype(F32)).astype(BF)

        for j in range(n // 2):
            give.at(i, j * chunk, chunk)[...] = total(place_bit(j, k, 1 - bit))
        copy().start()
        for j in range(n // 2):
            x = total(place_bit(j, k, bit))
            kept.at(i, (at + n + j) * chunk, chunk)[...] = x

    ends_a = [0]
    for k in range(nh + 1):
        ends_a.append(ends_a[-1] + (chunks >> (k + 1)))

    def a_third(k, i):
        copy_za(k, i).wait()
        n = chunks >> (k + 1)
        if k + 1 == nh:
            side = by_kind(i, zd, zl)
            halve(i, recv_y, ends_a[k], recv_za[k], n, send_pa, lambda: copy_pa(i), 0, side)
            return
        for op in range(2):

            @pl.when(by_kind(i, 1, 0) == op)
            def _():
                bit = bit_of(b, (halving_down if op else halving)[k + 1])
                at = bits - 4 - k if op else bits - 3 - k
                after = lambda: copy_za(k + 1, i)
                halve(i, recv_y, ends_a[k], recv_za[k], n, send_za[k + 1], after, at, bit)

    my_near = pl.multiple_of(s * near, near)
    its_near = pl.multiple_of((1 - s) * near, near)
    kept_a = lambda i, at: recv_y.at(i, ends_a[nh] * chunk + at, near)

    def copies_xa(i):
        side = by_kind(i, zd, zl)
        return [
            linked(kept_a(i, its_near), recv_px.at(i, chunk + side * near, near), sem_xa.at[i, 0], at_x),
            linked(
                recv_px.at(i, its_near, near),
                recv_px.at(i, chunk + (1 - side) * near, near),
                sem_xa.at[i, 1],
                at_x,
            ),
        ]

    def outs_a(i, picks):
        def to(side, pair):
            down, inner, k = kind_of(i)
            ffn_col = 8 * nq + down * 2 * nu + side * nu + pair * hu + k * width
            col = (1 - inner) * ffn_col + inner * (k * 2 * nq + side * nq + pair * hq)
            return w_hbm.at[:, pl.ds(pl.multiple_of(col, width), width)]

        pieces = [
            (kept_a(i, my_near), to(s, by_kind(i, zd, zl))),
            (recv_px.at(i, my_near, near), to(s, 1 - by_kind(i, zd, zl))),
            (recv_px.at(i, chunk, near), to(1 - s, 0)),
            (recv_px.at(i, chunk + near, near), to(1 - s, 1)),
        ]
        return [pltpu.make_async_copy(*pieces[k], sem_oa.at[i, k]) for k in picks]

    def a_fourth(i):
        copy_pa(i).wait()
        for copy in copies_xa(i) + outs_a(i, (0, 1)):
            copy.start()

    def a_fifth(i):
        for copy in copies_xa(i):
            copy.wait()
        for copy in outs_a(i, (2, 3)):
            copy.start()

    def b_first(i):
        n = chunks // 2

        def put(j, v):
            send_pb.at(i, j * chunk, chunk)[...] = v.astype(BF)

        products_b(i, [(n, lambda j: 2 * (2 * j + 1 - zl) + y, put, lambda: copy_pb(i).start())])

    def b_second(i):
        copy_pb(i).wait()
        bit = bit_of(b, halving[0])
        n = chunks // 4

        def total(v, at):
            return (v + recv_pb.at(i, at * chunk, chunk)[...].astype(F32)).astype(BF)

        def give(j, v):
            send_zb[0].at(i, j * chunk, chunk)[...] = total(v, (1 - bit) * n + j)

        def keep(j, v):
            x = total(v, bit * n + j)
            recv_pb.at(i, j * chunk, chunk)[...] = x

        products_b(
            i,
            [
                (n, lambda j: 2 * (2 * ((1 - bit) * n + j) + zl) + y, give, lambda: copy_zb(0, i).start()),
                (n, lambda j: 2 * (2 * (bit * n + j) + zl) + y, keep, lambda: None),
            ],
        )

    ends_b = [0]
    for k in range(nh):
        ends_b.append(ends_b[-1] + (chunks >> (k + 2)))
    kept_b = lambda i, at: recv_pb.at(i, ends_b[nh] * chunk + at, near)

    def copy_xb(i):
        return linked(kept_b(i, its_near), recv_xb(i), sem_xb.at[i], at_x)

    def outs_b(i, picks):
        def to(side):
            col = 6 * nq + side * nq + i * width
            return w_hbm.at[:, pl.ds(pl.multiple_of(col, width), width)]

        pieces = [(kept_b(i, my_near), to(s)), (recv_xb(i), to(1 - s))]
        return [pltpu.make_async_copy(*pieces[k], sem_ob.at[i, k]) for k in picks]

    def b_third(k, i):
        copy_zb(k, i).wait()
        n = chunks >> (k + 2)
        if k + 1 < nh:
            bit = bit_of(b, halving[k + 1])
            after = lambda: copy_zb(k + 1, i)
            halve(i, recv_pb, ends_b[k], recv_zb[k], n, send_zb[k + 1], after, bits - 4 - k, bit)
        else:
            x = recv_pb.at(i, ends_b[k] * chunk, chunk)[...].astype(F32) + recv_zb[k](i)[...].astype(F32)
            recv_pb.at(i, ends_b[nh] * chunk, chunk)[...] = x.astype(BF)
            copy_xb(i).start()
            outs_b(i, (0,))[0].start()

    def b_fourth(i):
        copy_xb(i).wait()
        outs_b(i, (1,))[0].start()

    small_partners = [at_y] + at_h + [at_p, at_x]

    def small_in(k):
        at = pl.ds((k // 2) * small_out.shape[0], small_out.shape[0])
        return outacc.at[at, pl.ds((k % 2) * quarter, quarter)]

    def small_step(k):
        copy = lambda k: linked(small_out, small_in(k), sem_s.at[k], small_partners[k])
        if k > 0:
            copy(k - 1).wait()
            if k < len(small_partners):
                small_out[...] = small_out[...] + small_in(k - 1)[...]
        if k < len(small_partners):
            copy(k).start()
        else:
            small_final[s] = small_out[...]
            small_final[1 - s] = small_in(k - 1)[...]

    for copy in firsts + from_core:
        copy.wait()
    norm1(s0, slots)
    norm1(t0 + my_toks, toks)
    x_hid[0].wait()
    forward = in_pass(rows, t0)
    x_hid.append(in_x(hid_hbm.at[1], rows, t1))
    x_dhid = [in_x(dhid_hbm.at[0], gd, t0), in_x(dhid_hbm.at[1], gd, t1)]
    forward.wait()
    norm1(t0 + its_toks, toks)
    thin_act1.append(share_thin(act1, la_hbm, 0, own, at_p))
    for copy in weights[:3]:
        copy.wait()
    project(0, own, 0, 3 * nq)
    attend(0)
    share_mix(0, own)
    for copy in weights[3:4]:
        copy.wait()
    T = span
    a1 = Total(slots, 0, 0, whole(slots))
    a2 = Total(T, 2 * slots, 2 * slots, whole(T))
    a1.start(out_product(s0, slots))
    a2.start(out_product(t0, T))
    a1.middle()
    a2.middle()
    x_hid[1].wait()
    forward = in_pass(rows, t1)
    for copy in late_core + laters:
        copy.wait()
    forward.wait()
    norm1(t1, own)
    thin_act1.append(share_thin(act1, la_hbm, t1, own, at_p))
    project(t1, own, 0, 3 * nq)
    a1.finish()
    a1.done()
    enter_ffn(a1, s0, slots)
    weights[4].wait()
    forwards = []
    for copy, at in zip(x_dhid, (t0, t1)):
        copy.wait()
        forwards.append(in_pass(gd, at))
    gd[pl.ds(s1, slots), :] = (dsum[pl.ds(slots, slots), :].astype(F32) * row_live).astype(BF)
    ffn(s0, slots, 0, 0, nu)
    for copy in forwards:
        copy.wait()
    share_feats_a(0, gd, t0, p0 - t0)
    weights[5].wait()
    a3 = Total(slots, slots, slots, whole(slots))
    a3.start(down_product(s0, slots))
    a2.finish()
    a3.middle()
    a2.done()
    enter_ffn(a2, t0, T)
    outacc[pl.ds(0 * toks, toks), :] = mid[pl.ds(t0 + my_toks, toks), my_cols]

    def early_before(c):
        cols, r = pl.ds(c, wide), pl.ds(t1, own)
        db[r, cols] = dot_nt(gd[r, :], wd[cols, :]).astype(BF)

    col_loop(3 * nu // 4, early_before)
    a3.finish()
    early_before(pl.multiple_of(3 * nu // 4, wide))
    thin_act2.append(share_thin(act2, lxx.at[1], s0, own, at_d))
    a3.done()

    def summary(i):
        r = pl.ds(pl.multiple_of(s0 + i * step, step), step)
        f = pl.ds(pl.multiple_of(a3.full + i * step, step), step)
        p = pl.ds(pl.multiple_of(p0 + i * step, step), step)
        x = mid[r, :] + ar_full[f, :].astype(F32) + vec[5:6, :]
        on = (lax.broadcasted_iota(jnp.int32, (step, 1), 0) + i * step < live_count).astype(F32)
        rows[p, :] = (x * on).astype(BF)

    pl.loop(0, slots // step)(summary)
    sum_out[0] = rows[pl.ds(p0, slots), my_cols]
    norm1(p0, slots)
    thin_act1.append(share_thin(act1, la_hbm, p0, slots, at_p))
    project(p0, slots, nq, 3 * nq)
    attend(1)
    share_mix(t1, own)
    a5 = Total(own, 2 * slots + T, 2 * slots + T, whole(own))
    a5.start(out_product(t1, own))
    ffn(t0, T, 1, 0, nu // 4)
    a5.middle()
    ffn(t0, T, 1, nu // 4, nu)
    share_actv(s0, own)
    side = pl.ds(pl.multiple_of(zl * hu, hu), hu)
    rs_own = remote(actv.at[pl.ds(s0, slots), side], rs_hbm.at[pl.ds(0, slots), :], at_y)
    a6 = Total(T, 2 * slots, 2 * slots, whole(T))
    a6.start(up_back(t0, T))
    a6.middle()
    a4 = Total(T, 2 * slots + T + 2 * own, None, [(0, T, True)], 0)
    a4.start(down_product(t0, T))
    a5.flow(lambda base, n: enter_ffn(a5, t1, n, base))
    a4.middle()
    outacc[pl.ds(1 * toks, toks), :] = mid[pl.ds(t1 + my_toks, toks), my_cols]
    outacc[pl.ds(2 * toks, toks), :] = mid[pl.ds(s1, slots), my_cols]
    pass_on(gifts_a, 1)
    ffn(t1, own, 2, 0, nu)
    share_actv(t1, own)
    a8 = Total(own, 2 * slots + T + own, 2 * slots + T + own, whole(own))
    a8.start(up_back(t1, own))
    a6.finish()
    a8.middle()
    a7 = Total(own, 2 * slots + 2 * T + 2 * own, None, [(0, T, True), (T, slots, False)], T)
    a7.start(down_product(t1, own))
    a6.done()
    leave_ffn(a6, t0, T)
    mix_back(t0, T)
    share_feats_b(gm, lm_hbm, t0, T)

    def begin_down():
        pass_on(gifts_a)
        pass_end()
        a_early(0)
        thin_act2.append(share_thin(act2, lxx.at[1], t1, own, at_d))
        share_db(t0, T)
        share_db(t1, own)

    a8.flow(lambda base, n: leave_ffn(a8, t1, n, base), begin_down)
    far = rbx.at[pl.ds(s0, slots), pl.ds(0, hu)]
    rs_far = remote(far, rs_hbm.at[pl.ds(slots, slots), :], at_y)
    a7.middle()
    mix_back(t1, own)
    share_feats_b(gm, lm_hbm, t1, own)
    attend_back(1)
    a9 = Total(slots, 0, 0, whole(slots))
    a9.start(in_back(p0, slots, nq))
    a10 = Total(own, 2 * slots + T, 2 * slots + T, [(0, T, True), (T, slots, False)])
    a9.middle()
    a10.start(in_back(t1, own, 0))
    a9.finish()
    a10.middle()
    for copy in a4.xs + a7.xs:
        copy.wait()
    hid_out[0] = (outacc[pl.ds(0 * toks, toks), :] + a4.sums(0, T, True) + vec[5:6, my_cols]).astype(BF)
    hid_out[1] = (outacc[pl.ds(1 * toks, toks), :] + a7.sums(0, T, True) + vec[5:6, my_cols]).astype(BF)
    sum_out[1] = (
        (outacc[pl.ds(2 * toks, toks), :] + a7.sums(T, slots, False) + vec[5:6, my_cols]) * row_live
    ).astype(BF)
    a9.done()
    first_only = (s == 0).astype(F32)

    def norm1_back(r, f, weight):
        d = ar_full[f, :].astype(F32)
        xhat = (rows[r, :].astype(F32) - stat[r, 0:1]) * stat[r, 1:2]
        gsum[pl.ds(0, 8), :] = gsum[pl.ds(0, 8), :] + fold(d * xhat) * weight
        gsum[pl.ds(8, 8), :] = gsum[pl.ds(8, 8), :] + fold(d) * weight
        return norm_back(d, xhat, stat[r, 1:2], vec[0:1, :])

    def prefix_back(i):
        r = pl.ds(pl.multiple_of(p0 + i * step, step), step)
        f = pl.ds(pl.multiple_of(a9.full + i * step, step), step)
        g = pl.ds(pl.multiple_of(s0 + i * step, step), step)
        on = (lax.broadcasted_iota(jnp.int32, (step, 1), 0) + i * step < live_count).astype(F32)
        d = norm1_back(r, f, first_only)
        gd[g, :] = ((dsum[pl.ds(pl.multiple_of(i * step, step), step), :].astype(F32) + d) * on).astype(BF)

    pl.loop(0, slots // step)(prefix_back)
    before_gifts = len(gifts_a)
    share_feats_a(0, gd, s0, slots)
    late_gifts = gifts_a.pop(before_gifts)
    ls_near = [
        remote(gd.at[pl.ds(s0, slots), out], ls_hbm.at[pl.ds(0, slots), out], at_y)
        for out, _ in y_blocks
    ]

    def last_before(c):
        cols = pl.ds(c, wide)
        r = pl.ds(s0, slots)
        db[r, cols] = (slope0[:, cols] * dot_nt(gd[r, :], wd[cols, :])).astype(BF)

    col_loop(nu, last_before)
    share_db(s0, slots)
    a11 = Total(slots, slots, slots, whole(slots))
    a11.start(up_back(s0, slots))
    askers = [at_x, at_p, at_y] + at_h
    for k, partner in enumerate(askers):
        pl.semaphore_signal(free.at[k], inc=1, device_id=partner, device_id_type=MESH)
    a10.finish()
    a11.middle()
    late_gifts[0].wait()
    share_qkv(t1, own + slots)
    passed.append(remote(late_gifts[1], late_gifts[1], at_core))
    ls_far = [
        remote(lxx.at[0, pl.ds(s0, slots), out], ls_hbm.at[pl.ds(slots, slots), out], at_y)
        for out, _ in y_blocks
    ]
    a10.done()
    gin_copies = []

    def rows_back(total, seg):
        t_at, s_at = (t0, s0) if seg == 0 else (t1, s1)
        t_in, s_in = (slots, 0) if seg == 0 else (0, span)

        def tokens(i):
            r = pl.ds(pl.multiple_of(t_at + my_toks + i * step, step), step)
            f = pl.ds(pl.multiple_of(total.full + t_in + i * step, step), step)
            x = norm1_back(r, f, 1.0)
            mid[r, :] = mid[r, :] + x

        pl.loop(0, toks // step)(tokens)
        gin_copies.append(local(mid.at[pl.ds(t_at + my_toks, toks), my_cols], gin_hbm.at[seg]))

        def summaries(i):
            r = pl.ds(pl.multiple_of(s_at + i * step, step), step)
            f = pl.ds(pl.multiple_of(total.full + s_in + i * step, step), step)
            x = norm1_back(r, f, first_only) + mid[r, :]
            e = pl.ds(pl.multiple_of(i * step, step), step)
            emb_wide[e, :] = x if seg == 1 else emb_wide[e, :] + x

        pl.loop(0, slots // step)(summaries)

    emb_wide = slope0
    for copy in [rs_own, rs_far]:
        copy.wait()
    for copy in ls_near:
        copy.wait()
    for copy in ls_far:
        copy.wait()
    ls_core = remote(ls_hbm.at[:, my_cols], ls_hbm.at[:, my_cols], at_core)
    rs_in = local(rs_hbm, ar_own.at[pl.ds(0, 2 * slots), :])
    came = [early_in(0)]
    a_early(1)
    rows_back(a10, 1)
    pass_end()
    ls_core.wait()
    ls_in = local(ls_hbm, dsum)
    a11.finish()
    for k in range(len(askers)):
        pl.semaphore_wait(free.at[k], 1)
    a11.done()
    rs_in.wait()
    ls_in.wait()
    a_second(0, came[0])
    for copy in thin_act1:
        copy.wait()
    x_act1 = remote(la_hbm.at[:, my_quarter], la_hbm.at[:, my_quarter], at_x)
    leave_ffn(a11, s0, slots)
    mix_back(s0, slots)
    share_feats_b(gm, lm_hbm, s0, slots)
    a_early(2)
    attend_back(0)
    share_qkv(0, own)
    a12 = Total(own, 2 * slots + T + own, 2 * slots + T + own, [(0, slots, False), (slots, T, True)])
    a12.start(in_back(s0, own, 0))
    a12.middle()
    x_act1.wait()
    core_act1 = remote(la_hbm.at[:, my_cols], la_hbm.at[:, my_cols], at_core)
    a_second(1, early_in(1))
    a_early(3)
    for copy in thin_act2:
        copy.wait()
    to_x = remote(lxx.at[1, :, my_quarter], lxx.at[1, :, my_quarter], at_x)
    pass_on(gifts_b)
    stage = [local(mx_hbm, dmix)]
    pass_end()
    stage.append(local(lm_hbm, ar_full.at[pl.ds(0, p0), :]))
    a12.finish()
    for copy in stage:
        copy.wait()
    b_first(0)
    b_first(1)
    ones = jnp.ones((8, p0), BF)
    column = lambda ref, cols: jnp.dot(ones, ref[pl.ds(0, p0), cols], preferred_element_type=F32)[0:1, :]
    base = slots
    small_out[base + 2 : base + 3, :] = column(gm, my_quarter)
    small_out[base + 5 : base + 6, :] = column(gd, my_quarter)
    small_out[base + 3 : base + 4, :] = jnp.sum(fsum[pl.ds(0, 8), my_quarter], axis=0, keepdims=True)
    small_out[base + 4 : base + 5, :] = jnp.sum(fsum[pl.ds(8, 8), my_quarter], axis=0, keepdims=True)
    small_out[base + 6 : base + 7, :] = column(dqkv, pl.ds(0, nq))
    small_out[base + 7 : base + 8, :] = column(dqkv, pl.ds(2 * nq, nq)) + jnp.sum(
        dqkv[pl.ds(p0, slots), pl.ds(2 * nq, nq)].astype(F32), axis=0, keepdims=True
    )
    for k in range(nu // quarter):
        small_out[base + 8 + k : base + 9 + k, :] = column(db, pl.ds(k * quarter, quarter))
    small_out[base + 12 : base + 16, :] = jnp.zeros((4, quarter), F32)
    a12.done()
    rows_back(a12, 0)
    small_out[pl.ds(0, slots), :] = emb_wide[:, my_quarter]
    its_quarter = pl.ds(pl.multiple_of(t * half + (1 - s) * quarter, quarter), quarter)
    gx_send[0:1, :] = jnp.sum(gsum[pl.ds(0, 8), its_quarter], axis=0, keepdims=True)
    gx_send[1:2, :] = jnp.sum(gsum[pl.ds(8, 8), its_quarter], axis=0, keepdims=True)
    gx_send[2:8, :] = jnp.zeros((6, quarter), F32)
    copy = remote(gx_send, gx_recv, at_x)
    copy.wait()
    small_out[base : base + 1, :] = gx_recv[0:1, :] + jnp.sum(gsum[pl.ds(0, 8), my_quarter], axis=0, keepdims=True)
    small_out[base + 1 : base + 2, :] = gx_recv[1:2, :] + jnp.sum(gsum[pl.ds(8, 8), my_quarter], axis=0, keepdims=True)
    small_step(0)
    to_x.wait()
    to_core = remote(lxx.at[1, :, my_cols], lxx.at[1, :, my_cols], at_core)
    pass_on(gifts_a)
    to_core.wait()
    a_first(4)
    a_second(2, early_in(2))
    for copy in gifts_q:
        copy.wait()
    core_act1.wait()
    stage = [local(la_hbm, rows), local(ra_hbm, qkv.at[:, pl.ds(0, 3 * hq)])]
    a_third(0, 0)
    for copy in stage:
        copy.wait()
    a_second(3, early_in(3))
    a_first(5)
    a_third(0, 1)

    def turn(it, lag, first, count, stage):
        @pl.when((it >= first + lag) & (it < lag + count))
        def _():
            stage(it - lag)

    turns = tiles_a + 2 * nh

    @pl.loop(0, turns)
    def _(it):
        turn(it, -4, 4, tiles_a, a_second)
        turn(it, -6, 6, tiles_a, a_first)
        turn(it, 1, 0, tiles_b, b_second)
        for k in range(nh):
            turn(it, 2 * k - 2, 0 if k else 2, tiles_a, functools.partial(a_third, k))
        turn(it, 2 * nh - 2, 0, tiles_a, a_fourth)
        turn(it, 2 * nh, 0, tiles_a, a_fifth)
        for k in range(nh):
            turn(it, 3 + 2 * k, 0, tiles_b, functools.partial(b_third, k))
        turn(it, 3 + 2 * nh, 0, tiles_b, b_fourth)
        for k in range(1, len(small_partners) + 1):

            @pl.when(it == 2 * k - 1)
            def _():
                small_step(k)

    assert counter["l"] <= lsem.shape[0] and counter["r"] <= rsem.shape[0]

    for copy in gin_copies:
        copy.wait()

    @pl.loop(0, tiles_a)
    def _(i):
        for copy in outs_a(i, range(4)):
            copy.wait()

    @pl.loop(0, tiles_b)
    def _(i):
        for copy in outs_b(i, range(2)):
            copy.wait()

def chain(count, emb, dsum, feat_vecs, bq, bv, bu, hid, dhid, wq, wk, wv, wo, wu, wd):
    bits = lax.axis_size("batch").bit_length() - 1
    toks, slots = hid.shape[1], emb.shape[0] + -emb.shape[0] % 64
    half = hid.shape[2]
    feats, quarter = 2 * half, half // 2
    nq, nu = wo.shape[0] // 2, wd.shape[0] // 2
    own = 2 * toks + slots
    main, end = 2 * own, 2 * own + slots
    sums = 2 * slots + 2 * toks + 2 * own
    chunk = feats >> bits
    nh = bits - 2
    ta, tb = 2 * nu // nq + 3, 2
    vm = pltpu.VMEM
    sds = jax.ShapeDtypeStruct
    dma = pltpu.SemaphoreType.DMA
    scratch = [
        vm((feats, 3 * nq), BF),
        vm((nq, feats), BF),
        vm((feats, nu), BF),
        vm((nu, feats), BF),
        vm((end, feats), BF),
        vm((end, feats), BF),
        vm((end, 3 * nq), BF),
        vm((2, nq // HD, own, own + slots), BF),
        vm((main, nq), BF),
        vm((main, feats), F32),
        vm((main, feats), BF),
        vm((main, nu), BF),
        vm((main, nu), BF),
        vm((slots, nu), F32),
        vm((main, feats), BF),
        vm((main, feats), BF),
        vm((main, nq), BF),
        vm((end, 3 * nq), BF),
        vm((2 * slots, feats), BF),
        vm((8, feats), F32),
        vm((1, 3 * nq + nu), F32),
        vm((end, 128), F32),
        vm((max(3 * toks, (slots + 16) * ((bits + 2) // 2)), half), F32),
        vm((16, feats), F32),
        vm((16, feats), F32),
        vm((8, quarter), F32),
        vm((8, quarter), F32),
        vm((sums + 2 * toks + own, half), BF),
        vm((sums + 2 * toks + own, half), BF),
        vm((sums + 2 * toks + own, half), BF),
        vm((sums, feats), BF),
        vm((2 * toks + own, half), BF),
        vm((2, main, feats), BF),
        vm((main, nu), BF),
        vm((2 * chunk if chunk % 128 else 8, nq // 2), F32),
        vm((slots + 16, quarter), F32),
        dma((6,)),
        dma((16,)),
        dma((113, 2)),
        pltpu.SemaphoreType.REGULAR((3 + nh,)),
        dma((ta, 2)),
        dma((nh, ta, 2)),
        dma((ta, 2)),
        dma((ta, 2, 2)),
        dma((tb, 2)),
        dma((nh, tb, 2)),
        dma((tb, 2)),
        dma((ta, 4)),
        dma((tb, 2)),
        dma((bits + 1, 2)),
        vm((2, feats // 2, nq // 2), BF),
        vm(emb.shape, BF),
        vm(dsum.shape, BF),
        [vm(v.shape, BF) for v in feat_vecs + [bq, bv, bu]],
        dma((len(feat_vecs) + 5,)),
    ]
    vmem = pl.BlockSpec(memory_space=pltpu.VMEM)
    hbm = pl.BlockSpec(memory_space=pl.ANY)
    smem = pl.BlockSpec(memory_space=pltpu.SMEM)
    return pl.pallas_call(
        functools.partial(chain_kernel, bits),
        name="layer",
        out_shape=(
            sds((2, toks, half), BF),
            sds((2, slots, half), BF),
            sds((2, toks, half), F32),
            sds((2, slots + 16, quarter), F32),
            sds((chunk // 2, 8 * nq + 4 * nu), BF),
            sds((end, feats), BF),
            sds((main, feats), BF),
            sds((end, 3 * nq // 2), BF),
            sds((main, nq), BF),
            sds((4, feats // 2, nq // 2), BF),
            sds((2 * slots, feats), BF),
            sds((2 * slots, nu // 2), BF),
        ),
        in_specs=[smem, hbm, hbm, [hbm] * 6, hbm, hbm, hbm] + [hbm] * 8,
        out_specs=(vmem, vmem, hbm, vmem) + (hbm,) * 8,
        scratch_shapes=scratch,
        compiler_params=pltpu.CompilerParams(
            collective_id=2, has_side_effects=True, vmem_limit_bytes=63 * 2**20
        ),
    )(count, emb, dsum, feat_vecs, bq, bv, bu, hid, dhid, wq, wk, wv, wo, wu, wd)


def place_kernel(
    hid, sums, gin, small, w, hid_o, sum_o, gin_o, emb_o, vec_o, bup_o, q_o, k_o, v_o, o_o, u_o, d_o,
    hid_v, sum_v, gin_v, small_v, w_v, wide_v, tall_v, sem,
):
    n, wide = q_o.shape[1], u_o.shape[1]
    sections = [(k * n, n) for k in range(4)] + [(4 * n, wide), (4 * n + wide, wide)]
    copy = pltpu.make_async_copy
    ins = []
    for k, (at, m) in enumerate(sections):
        cols = pl.ds(at, m)
        ins.append(copy(w.at[:, cols], w_v.at[:, cols], sem.at[k]))
    plain = ((hid, hid_v), (gin, gin_v), (sums, sum_v), (small, small_v))
    plain = [copy(src, dst, sem.at[6 + k]) for k, (src, dst) in enumerate(plain)]
    order = (5, 4, 3, 0, 1, 2)
    for k in order:
        ins[k].start()
    for c in plain:
        c.start()
    outs = []

    def send(src, dst):
        c = copy(src, dst, sem.at[10 + len(outs)])
        c.start()
        outs.append(c)

    for k in order:
        at, m = sections[k]
        cols = pl.ds(at, m)
        ins[k].wait()
        x = w_v[:, cols].astype(F32)
        if k in (3, 5):
            there = tall_v.at[pl.ds(0, m), :] if k == 5 else tall_v.at[pl.ds(wide, m), :]
            there[...] = x.T
        else:
            there = wide_v.at[:, cols]
            there[...] = x
        send(there, (q_o, k_o, v_o, o_o, u_o, d_o)[k])
    for c in plain[:2]:
        c.wait()
    send(hid_v, hid_o.at[0])
    send(gin_v, gin_o.at[0])
    for c in plain[2:]:
        c.wait()
    used = sum_o.shape[0]
    for seg in range(2):
        sum_o[:, seg, :] = sum_v[seg, :used, :]
    quarter = small_v.shape[2]
    base = small_v.shape[1] - 16
    nu = bup_o.shape[0] // 2
    for side in range(2):
        at = pl.ds(side * quarter, quarter)
        emb_o[:, at] = small_v[side, :used, :]
        for k, ref in enumerate(vec_o):
            ref[at] = small_v[side, base + k]
        for k in range(nu // quarter):
            bup_o[pl.ds(side * nu + k * quarter, quarter)] = small_v[side, base + 8 + k]
    for c in outs:
        c.wait()


def place(hid, sums, gin, small, w, used):
    sds = jax.ShapeDtypeStruct
    _, toks, half = hid.shape
    rows = w.shape[0]
    nu = (w.shape[1] - 4 * half) // 4
    vmem = pl.BlockSpec(memory_space=pltpu.VMEM)
    hbm = pl.BlockSpec(memory_space=pl.ANY)
    vm = pltpu.VMEM
    return pl.pallas_call(
        place_kernel,
        name="place",
        out_shape=(
            sds((1, 2, toks, half), BF),
            sds((used, 2, half), BF),
            sds((1, 2, toks, half), F32),
            sds((used, half), F32),
            [sds((half,), F32)] * 8,
            sds((2 * nu,), F32),
            sds((rows, half), F32),
            sds((rows, half), F32),
            sds((rows, half), F32),
            sds((half, rows), F32),
            sds((rows, 2 * nu), F32),
            sds((2 * nu, rows), F32),
        ),
        in_specs=[hbm] * 5,
        out_specs=(hbm, vmem, hbm, vmem, [vmem] * 8, vmem) + (hbm,) * 6,
        scratch_shapes=[
            vm(hid.shape, BF),
            vm(sums.shape, BF),
            vm(gin.shape, F32),
            vm(small.shape, F32),
            vm(w.shape, BF),
            vm((rows, 4 * half + 2 * nu), F32),
            vm((2 * nu + half, rows), F32),
            pltpu.SemaphoreType.DMA((18,)),
        ],
        compiler_params=pltpu.CompilerParams(vmem_limit_bytes=60 * 2**20),
    )(hid, sums, gin, small, w)


def local(
    hidden_in, summary_counts, summary_embed, ln1_gain, ln1_bias, w_query, b_query, w_key, w_value,
    b_value, w_out, b_out, ln2_gain, ln2_bias, w_up, b_up, w_down, b_down, d_hidden, d_summary,
):
    got = chain(
        summary_counts, summary_embed, d_summary[0].transpose(1, 0, 2),
        [ln1_gain, ln1_bias, ln2_gain, ln2_bias, b_out, b_down], b_query, b_value, b_up,
        hidden_in[0], d_hidden[0], w_query, w_key, w_value, w_out, w_up, w_down,
    )
    hid, sums, gin, emb, vecs, bup, gq, gk, gv, go, gu, gd = place(*got[:5], summary_embed.shape[0])
    return (
        hid, sums.transpose(1, 0, 2)[None], gin, emb, vecs[0], vecs[1], gq, vecs[6], gk, gv,
        vecs[7], go, vecs[2], vecs[3], vecs[4], gu, bup, gd, vecs[5],
    )


def solution(mesh):
    return jax.shard_map(
        local,
        mesh=mesh,
        in_specs=(
            P("batch", None, "seq", "tensor"),
            P("batch"),
            P(None, "tensor"),
            P("tensor"),
            P("tensor"),
            P(None, "tensor"),
            P("tensor"),
            P(None, "tensor"),
            P(None, "tensor"),
            P("tensor"),
            P("tensor", None),
            P("tensor"),
            P("tensor"),
            P("tensor"),
            P(None, "tensor"),
            P("tensor"),
            P("tensor", None),
            P("tensor"),
            P("batch", None, "seq", "tensor"),
            P("batch", None, None, "tensor"),
        ),
        out_specs=(
            P("batch", None, "seq", "tensor"),
            P("batch", None, None, "tensor"),
            P("batch", None, "seq", "tensor"),
            P(None, "tensor"),
            P("tensor"),
            P("tensor"),
            P(("batch", "seq"), "tensor"),
            P("tensor"),
            P(("batch", "seq"), "tensor"),
            P(("batch", "seq"), "tensor"),
            P("tensor"),
            P("tensor", ("batch", "seq")),
            P("tensor"),
            P("tensor"),
            P("tensor"),
            P(("batch", "seq"), "tensor"),
            P("tensor"),
            P("tensor", ("batch", "seq")),
            P("tensor"),
        ),
        check_vma=False,
    )
```
